512 devices in a mesh: seq: 16 (over y, z_lo), batch: 32 (over z_hi, x, core).
Axes of the slice: x: 4, y: 4, z: 16 (z_hi: 4, z_lo: 4; z = z_hi * 4 + z_lo), core: 2. Of those that a mesh axis runs over, the one named last changes fastest.
Arguments:
- history: bfloat16 [32, 16384, 256], P('batch', 'seq'), may hold values from -36 to 36
- cotangent: bfloat16 [32, 16384, 256], P('batch', 'seq'), may hold values from -6 to 6
- filter_weight: bfloat16 [2, 128, 128, 256], P(None, 'seq', 'batch'), may hold values from -4 to 4
- gain_first: float32 [256], replicated, may hold values from 0.1 to 1.9
- bias_first: float32 [256], replicated, may hold values from -3 to 3
- w_in: bfloat16 [256, 512], replicated, may hold values from -0.375 to 0.375
- w_out: bfloat16 [512, 256], replicated, may hold values from -0.25 to 0.25
- gain_second: float32 [256], replicated, may hold values from 0.1 to 1.9
Outputs:
- history_grad: bfloat16 [32, 16384, 256], P('batch', 'seq')
- filter_grad: float32 [2, 128, 128, 256], P(None, 'seq', 'batch')
The draws below stay inside these ranges and needn't reach their ends.
All inputs are finite; a program needn't handle non-finite values.
Results may differ from the reference program's by a relative error of at most 0.025.
Values may be sent and summed in bfloat16 or wider, within the bound.
A program may use at most 64 MiB of HBM per device.

```python
import math
import jax
import jax.numpy as jnp
from jax import lax

D = 256
FF = 512
F1 = 128
F2 = 128
USER_DEV = 1
USERS = 32
SEQ_LEN = 16384
N_BATCH = 32


def draw_history(key, part):
    key = jax.random.fold_in(key, 11)
    base_key, row_key, col_key = jax.random.split(key, 3)
    shape = (USERS, SEQ_LEN, D)
    row_scale = jnp.exp(jax.random.uniform(row_key, (USERS, SEQ_LEN, 1), jnp.float32, math.log(0.3), math.log(3.0)))
    col_scale = jnp.exp(jax.random.uniform(col_key, (1, 1, D), jnp.float32, math.log(0.3), math.log(3.0)))
    base = jax.random.truncated_normal(base_key, -4.0, 4.0, shape, jnp.float32)
    return (base * row_scale * col_scale).astype(jnp.bfloat16)


def block_levels(rng, extent, pieces, smallest, largest):
    gain, own = 1.0, jax.random.fold_in(rng, 6)
    for dim, shards_of in pieces:
        draws = jnp.exp(jax.random.uniform(jax.random.fold_in(own, dim), (shards_of,), jnp.float32, smallest / len(pieces), largest / len(pieces)))
        gain = gain * jnp.repeat(draws, extent[dim] // shards_of).reshape([-1 if axis == dim else 1 for axis in range(len(extent))])
    return gain


def noise(key, extent, width, reach, shards=(), kind=jnp.bfloat16):
    drawn = jax.random.normal(key, extent, jnp.float32) * width
    if len(shards) > 0:
        drawn = block_levels(key, extent, shards, -0.22, 0.18) * drawn
    return jnp.clip(drawn, min=-reach, max=reach).astype(kind)


def setup_inputs(seed: int = 0) -> dict:
    key_of = jax.random.split(jax.random.key(seed), 9)
    history = draw_history(jax.random.fold_in(key_of[8], 71), 0)
    cotangent = noise(key_of[1], (USERS, SEQ_LEN, D), 1.0, 6.0, ((0, 32), (1, 16)))
    filter_weight = noise(key_of[2], (2, F1, F2, D), 1.0, 4.0, ((1, 16), (2, 32)))
    gain_first = jnp.clip(1.0 + 0.18 * jax.random.normal(key_of[3], (D,), jnp.float32), 0.1, 1.9)
    bias_first = noise(key_of[4], (D,), 0.5, 3.0, (), jnp.float32)
    w_in = noise(key_of[5], (D, FF), D ** -0.5, 0.375)
    w_out = noise(key_of[6], (FF, D), FF ** -0.5, 0.25)
    gain_second = jnp.clip(1.0 + 0.18 * jax.random.normal(key_of[7], (D,), jnp.float32), 0.1, 1.9)
    return dict(history=history, cotangent=cotangent, filter_weight=filter_weight, gain_first=gain_first, bias_first=bias_first, w_in=w_in, w_out=w_out, gain_second=gain_second)


epsilon = 1e-05
inv_root_two = 1.0 / math.sqrt(2.0)
inv_root_tau = 1.0 / math.sqrt(2.0 * math.pi)

def dft_table(length):
    positions = jnp.arange(length, dtype=jnp.int32)
    phases = (positions[:, None] * positions[None, :] % length).astype(jnp.float32) * (2.0 * math.pi / length)
    return (jnp.cos(phases).astype(jnp.bfloat16), jnp.sin(phases).astype(jnp.bfloat16))

def twiddle(row_index, col_index, modulus):
    phases = (row_index[:, None] * col_index[None, :] % modulus).astype(jnp.float32) * (2.0 * math.pi / modulus)
    return (jnp.cos(phases)[:, :, None], jnp.sin(phases)[:, :, None])

def apply_table(form, dft_matrix, values):
    return jnp.einsum(form, dft_matrix.astype(jnp.float32), values.astype(jnp.float32), precision=lax.Precision.HIGHEST)

def first_forward(values, cos_table, sine_table, tw_cos, tw_sin):
    real_part = apply_table('ka,uabd->ukbd', cos_table, values)
    imag_part = -apply_table('ka,uabd->ukbd', sine_table, values)
    return jnp.stack([real_part * tw_cos + imag_part * tw_sin, imag_part * tw_cos - real_part * tw_sin]).astype(jnp.bfloat16)

def second_forward(complex_pair, cos_table, sine_table):
    real_in, imag_in = (complex_pair[0], complex_pair[1])
    real_part = apply_table('qb,upbd->upqd', cos_table, real_in) + apply_table('qb,upbd->upqd', sine_table, imag_in)
    imag_part = apply_table('qb,upbd->upqd', cos_table, imag_in) - apply_table('qb,upbd->upqd', sine_table, real_in)
    return jnp.stack([real_part, imag_part]).astype(jnp.bfloat16)

def first_inverse(complex_pair, cos_table, sine_table, tw_cos, tw_sin):
    real_in, imag_in = (complex_pair[0], complex_pair[1])
    real_part = apply_table('qb,upqd->upbd', cos_table, real_in) - apply_table('qb,upqd->upbd', sine_table, imag_in)
    imag_part = apply_table('qb,upqd->upbd', cos_table, imag_in) + apply_table('qb,upqd->upbd', sine_table, real_in)
    return jnp.stack([real_part * tw_cos - imag_part * tw_sin, imag_part * tw_cos + real_part * tw_sin]).astype(jnp.bfloat16)

def second_inverse(complex_pair, cos_table, sine_table, factor):
    real_part = apply_table('pa,upbd->uabd', cos_table, complex_pair[0])
    imag_part = apply_table('pa,upbd->uabd', sine_table, complex_pair[1])
    return (real_part - imag_part) * factor

def filter_apply(spectrum, filter_full):
    spec_re, spec_im = (spectrum[0].astype(jnp.float32), spectrum[1].astype(jnp.float32))
    filt_re, filt_im = (filter_full[0].astype(jnp.float32), filter_full[1].astype(jnp.float32))
    return jnp.stack([spec_re * filt_re - spec_im * filt_im, spec_re * filt_im + spec_im * filt_re]).astype(jnp.bfloat16)

def filter_back(slope_spec, filter_full):
    slope_re, slope_im = (slope_spec[0].astype(jnp.float32), slope_spec[1].astype(jnp.float32))
    filt_re, filt_im = (filter_full[0].astype(jnp.float32), filter_full[1].astype(jnp.float32))
    return jnp.stack([filt_re * slope_re + filt_im * slope_im, filt_re * slope_im - filt_im * slope_re]).astype(jnp.bfloat16)

def filter_term(spectrum, slope_spec, factor):
    spec_re, spec_im = (spectrum[0].astype(jnp.float32), spectrum[1].astype(jnp.float32))
    slope_re, slope_im = (slope_spec[0].astype(jnp.float32), slope_spec[1].astype(jnp.float32))
    term_re = lax.optimization_barrier(jnp.sum((spec_re * slope_re + spec_im * slope_im) * factor, axis=0))
    term_im = lax.optimization_barrier(jnp.sum((spec_re * slope_im - spec_im * slope_re) * factor, axis=0))
    return jnp.stack([term_re, term_im])

def local_pass(mixed_rows, history_rows, cot_rows, gain_first, bias_first, w_in, w_out, gain_second):
    summed = mixed_rows.astype(jnp.float32) + history_rows.astype(jnp.float32)
    center_one = summed - lax.optimization_barrier(jnp.mean(summed, axis=-1, keepdims=True))
    inv_one = lax.rsqrt(lax.optimization_barrier(jnp.mean(center_one * center_one, axis=-1, keepdims=True)) + epsilon)
    norm_one = center_one * inv_one
    hidden = (norm_one * gain_first + bias_first).astype(jnp.bfloat16)
    preact = jnp.dot(hidden, w_in, preferred_element_type=jnp.float32)
    cumul = 0.5 * (1.0 + lax.erf(preact * inv_root_two))
    activation = (preact * cumul).astype(jnp.bfloat16)
    output_sum = jnp.dot(activation, w_out, preferred_element_type=jnp.float32) + hidden.astype(jnp.float32)
    center_two = output_sum - lax.optimization_barrier(jnp.mean(output_sum, axis=-1, keepdims=True))
    inv_two = lax.rsqrt(lax.optimization_barrier(jnp.mean(center_two * center_two, axis=-1, keepdims=True)) + epsilon)
    norm_two = center_two * inv_two
    grad_norm = cot_rows.astype(jnp.float32) * gain_second
    grad_sum = inv_two * (grad_norm - lax.optimization_barrier(jnp.mean(grad_norm, axis=-1, keepdims=True)) - norm_two * lax.optimization_barrier(jnp.mean(grad_norm * norm_two, axis=-1, keepdims=True)))
    grad_act = jnp.dot(grad_sum.astype(jnp.bfloat16), w_out.T, preferred_element_type=jnp.float32)
    density = jnp.exp(-0.5 * preact * preact) * inv_root_tau
    grad_pre = (grad_act * (cumul + preact * density)).astype(jnp.bfloat16)
    grad_hidden = jnp.dot(grad_pre, w_in.T, preferred_element_type=jnp.float32) + grad_sum
    grad_scaled = grad_hidden * gain_first
    grad_input = inv_one * (grad_scaled - lax.optimization_barrier(jnp.mean(grad_scaled, axis=-1, keepdims=True)) - norm_one * lax.optimization_barrier(jnp.mean(grad_scaled * norm_one, axis=-1, keepdims=True)))
    return (grad_input, grad_input.astype(jnp.bfloat16))

def reference(history, cotangent, filter_weight, gain_first, bias_first, w_in, w_out, gain_second):
    cos_one, sin_one = dft_table(F1)
    cos_two, sin_two = dft_table(F2)
    tw_cos, tw_sin = twiddle(jnp.arange(F1, dtype=jnp.int32), jnp.arange(F2, dtype=jnp.int32), F1 * F2)
    inv_length = 1.0 / (F1 * F2)

    def spectrum_of(values):
        return second_forward(first_forward(values, cos_one, sin_one, tw_cos, tw_sin), cos_two, sin_two)

    def field_of(complex_pair):
        return second_inverse(first_inverse(complex_pair, cos_two, sin_two, tw_cos, tw_sin), cos_one, sin_one, inv_length)

    def one_user(user_rows, cot_rows):
        values = user_rows.reshape(1, F1, F2, D)
        spectrum = spectrum_of(values)
        seq_mix = field_of(filter_apply(spectrum, filter_weight)).astype(jnp.bfloat16)
        grad_input, slope = local_pass(seq_mix.reshape(-1, D), user_rows, cot_rows, gain_first, bias_first, w_in, w_out, gain_second)
        slope_spec = spectrum_of(slope.reshape(1, F1, F2, D))
        back_field = field_of(filter_back(slope_spec, filter_weight)).astype(jnp.bfloat16)
        user_grad = (grad_input + back_field.reshape(-1, D).astype(jnp.float32)).astype(jnp.bfloat16)
        return (user_grad, filter_term(spectrum, slope_spec, inv_length))

    def group_step(running, group):
        group_rows, group_cot = group
        partial_value = jnp.zeros((2, F1, F2, D), jnp.float32)
        grads = []
        for member in range(USER_DEV):
            user_grad, term = one_user(group_rows[member], group_cot[member])
            partial_value = partial_value + term
            grads.append(user_grad)
        rounded = lax.optimization_barrier(partial_value.astype(jnp.bfloat16)).astype(jnp.float32)
        return (running + rounded, jnp.stack(grads))
    start = jnp.zeros((2, F1, F2, D), jnp.float32)
    groups = (history.reshape(N_BATCH, USER_DEV, SEQ_LEN, D), cotangent.reshape(N_BATCH, USER_DEV, SEQ_LEN, D))
    filter_grad, grads = lax.scan(group_step, start, groups)
    return (grads.reshape(USERS, SEQ_LEN, D), filter_grad)
```

```python
import functools
import math

import jax
import jax.numpy as jnp
import ml_dtypes
import numpy as np
from jax import lax
from jax.experimental import pallas as pl
from jax.experimental.pallas import tpu as pltpu
from jax.sharding import PartitionSpec as P

F1 = 128
F2 = 128
LINES = 64
CHUNK = 2

epsilon = 1e-05
inv_root_two = 1.0 / math.sqrt(2.0)
inv_root_tau = 1.0 / math.sqrt(2.0 * math.pi)
inv_length = 1.0 / (F1 * F2)


def host_tables():
    index = np.arange(F1)
    angle = 2.0 * np.pi * (index[:, None] * index[None, :] % F1) / F1
    cos, sin = np.cos(angle), np.sin(angle)
    outer_fwd = np.concatenate([cos[:LINES], -sin[:LINES]], axis=0)
    outer_inv = np.concatenate([cos[:LINES], -sin[:LINES]], axis=0).T
    inner_fwd = np.block([[cos, -sin], [sin, cos]])
    inner_inv = np.block([[cos, sin], [-sin, cos]])
    lines = np.arange(LINES + 1)
    phase = 2.0 * np.pi * (lines[:, None] * index[None, :]) / (F1 * F2)
    narrow = [t.astype(ml_dtypes.bfloat16) for t in (outer_fwd, outer_inv, inner_fwd, inner_inv)]
    twiddles = np.stack([np.cos(phase), np.sin(phase)]).astype(np.float32)
    return (*narrow, twiddles[:, :LINES], twiddles[:, LINES:])


def dot(a, b):
    return jnp.dot(a, b, preferred_element_type=jnp.float32)


def dot_nt(a, b):
    return lax.dot_general(a, b, (((1,), (1,)), ((), ())), preferred_element_type=jnp.float32)


def mean(x):
    return jnp.mean(x, axis=-1, keepdims=True)


def local_rows(mixed, history, cot, gain_first, bias_first, w_in, w_out, gain_second):
    summed = mixed + history.astype(jnp.float32)
    center_one = summed - mean(summed)
    inv_one = lax.rsqrt(mean(center_one * center_one) + epsilon)
    norm_one = center_one * inv_one
    hidden = (norm_one * gain_first + bias_first).astype(jnp.bfloat16)
    preact = dot(hidden, w_in)
    cumul = 0.5 * (1.0 + lax.erf(preact * inv_root_two))
    activation = (preact * cumul).astype(jnp.bfloat16)
    output_sum = dot(activation, w_out) + hidden.astype(jnp.float32)
    center_two = output_sum - mean(output_sum)
    inv_two = lax.rsqrt(mean(center_two * center_two) + epsilon)
    norm_two = center_two * inv_two
    grad_norm = cot.astype(jnp.float32) * gain_second
    grad_sum = inv_two * (grad_norm - mean(grad_norm) - norm_two * mean(grad_norm * norm_two))
    grad_act = dot_nt(grad_sum.astype(jnp.bfloat16), w_out)
    density = jnp.exp(-0.5 * preact * preact) * inv_root_tau
    grad_pre = (grad_act * (cumul + preact * density)).astype(jnp.bfloat16)
    grad_hidden = dot_nt(grad_pre, w_in) + grad_sum
    grad_scaled = grad_hidden * gain_first
    return inv_one * (grad_scaled - mean(grad_scaled) - norm_one * mean(grad_scaled * norm_one))


def kernel(
    seq,
    history,
    cotangent,
    filt,
    filt_mid,
    gain_first,
    bias_first,
    w_in,
    w_out,
    gain_second,
    outer_fwd,
    outer_inv,
    inner_fwd,
    inner_inv,
    twiddle,
    twiddle_mid,
    out,
    grad,
    grad_mid,
    send_in,
    send_out,
    recv_in,
    recv_out,
    spec,
    spec_mid,
    field,
    grad_rows,
    send_sem,
    recv_sem,
):
    me = lax.axis_index("seq")
    rows = F1 // seq
    feats = history.shape[1] // seq
    chunks = rows // CHUNK

    barrier = pltpu.get_barrier_semaphore()

    def greet(k, _):
        pl.semaphore_signal(
            barrier,
            inc=1,
            device_id={"seq": lax.rem(me + k, seq)},
            device_id_type=pl.DeviceIdType.MESH,
        )
        return 0

    lax.fori_loop(1, seq, greet, 0)
    pl.semaphore_wait(barrier, seq - 1)

    def exchange(src, dst, way, chunk):
        def one(k, _):
            peer = lax.rem(me + k, seq)
            pltpu.make_async_remote_copy(
                src_ref=src(peer),
                dst_ref=dst,
                send_sem=send_sem.at[way],
                recv_sem=recv_sem.at[way, chunk],
                device_id={"seq": peer},
                device_id_type=pl.DeviceIdType.MESH,
            ).start()
            return 0

        lax.fori_loop(1, seq, one, 0)

    def send_positions(x, way, chunk):
        for j in range(chunk * CHUNK, (chunk + 1) * CHUNK):
            block = x(j).T.reshape(seq, feats, F2)
            send_in[way, j] = block
        part = pl.ds(chunk * CHUNK, CHUNK)
        recv_in[way, me, part] = send_in[way, part, me]
        exchange(
            lambda peer: send_in.at[way, part, peer], recv_in.at[way, me, part], 2 * way, chunk
        )

    def send_features(way, chunk):
        part = pl.ds(chunk * CHUNK, CHUNK)
        recv_out[way, part, me] = send_out[way, me, part]
        exchange(
            lambda peer: send_out.at[way, peer, part], recv_out.at[way, part, me], 2 * way + 1, chunk
        )

    def wait_chunk(way, chunk):
        whole = send_in.at[0, pl.ds(0, CHUNK), pl.ds(0, seq - 1)]
        pltpu.make_async_copy(whole, whole, recv_sem.at[way, chunk]).wait()

    def transform(way, multiply, multiply_mid):
        tiles = recv_in[way].reshape(F1 // 2, 2, feats, F2)
        mid = jnp.sum(
            tiles[:, 0].astype(jnp.float32) - tiles[:, 1].astype(jnp.float32), axis=0
        )
        field[...] = recv_in[way].reshape(F1 * feats, F2).astype(jnp.float32)
        cos, sin = twiddle[0], twiddle[1]

        def pair(first):
            return [field[pl.ds(first + i, F1, stride=feats), :] for i in range(2)]

        def step(group, _):
            base = group * 4
            halves = []
            for sub in range(2):
                two = jnp.concatenate(pair(base + 2 * sub), axis=1).astype(jnp.bfloat16)
                both = dot(outer_fwd[...], two)
                for i in range(2):
                    real = both[:LINES, i * F2 : (i + 1) * F2]
                    imag = both[LINES:, i * F2 : (i + 1) * F2]
                    halves.append(
                        jnp.concatenate(
                            [real * cos + imag * sin, imag * cos - real * sin], axis=1
                        ).astype(jnp.bfloat16)
                    )
            spectrum = dot(jnp.concatenate(halves, axis=0), inner_fwd[...])
            where = pl.ds(pl.multiple_of(base * LINES, 4 * LINES), 4 * LINES)
            product = multiply(spectrum, where)
            half = dot(product, inner_inv[...])
            for sub in range(2):
                columns = []
                for i in range(2):
                    piece = half[(2 * sub + i) * LINES : (2 * sub + i + 1) * LINES]
                    real, imag = piece[:, :F2], piece[:, F2:]
                    columns.append(
                        jnp.concatenate(
                            [real * cos - imag * sin, imag * cos + real * sin], axis=0
                        ).astype(jnp.bfloat16)
                    )
                result = dot(outer_inv[...], jnp.concatenate(columns, axis=1)) * inv_length
                for i in range(2):
                    field[pl.ds(base + 2 * sub + i, F1, stride=feats), :] = result[
                        :, i * F2 : (i + 1) * F2
                    ]
            return 0

        lax.fori_loop(0, feats // 4, step, 0)

        cos_mid, sin_mid = twiddle_mid[0], twiddle_mid[1]
        half = jnp.concatenate([mid * cos_mid, -mid * sin_mid], axis=1).astype(jnp.bfloat16)
        product = multiply_mid(dot(half, inner_fwd[...]))
        half = dot(product, inner_inv[...])
        last = (half[:, :F2] * cos_mid - half[:, F2:] * sin_mid).astype(jnp.bfloat16)
        last = last.astype(jnp.float32) * inv_length
        both = field[...].reshape(F1 // 2, 2, feats, F2)
        sign = jnp.where(lax.broadcasted_iota(jnp.int32, both.shape, 1) == 0, 1.0, -1.0)
        both = both + sign * last[None, None]
        send_out[way] = both.astype(jnp.bfloat16).reshape(seq, rows, feats, F2)

    def split(z):
        return z[:, :F2].astype(jnp.float32), z[:, F2:].astype(jnp.float32)

    def times(z, f):
        zr, zi = split(z)
        fr, fi = split(f)
        return jnp.concatenate([zr * fr - zi * fi, zr * fi + zi * fr], axis=1).astype(jnp.bfloat16)

    def times_conj(z, f):
        zr, zi = split(z)
        fr, fi = split(f)
        return jnp.concatenate([fr * zr + fi * zi, fr * zi - fi * zr], axis=1)

    def filter_main(z, where):
        z = z.astype(jnp.bfloat16)
        spec[where, :] = z
        return times(z, filt[where, :])

    def filter_mid(z):
        z = z.astype(jnp.bfloat16)
        spec_mid[...] = z
        return times(z, filt_mid[...])

    def back_main(z, where):
        z = z.astype(jnp.bfloat16)
        grad[where, :] = (times_conj(z, spec[where, :]) * inv_length).astype(jnp.bfloat16)
        return times_conj(z, filt[where, :]).astype(jnp.bfloat16)

    def back_mid(z):
        z = z.astype(jnp.bfloat16)
        grad_mid[...] = (times_conj(z, spec_mid[...]) * inv_length).astype(jnp.bfloat16)
        return times_conj(z, filt_mid[...]).astype(jnp.bfloat16)

    for chunk in range(chunks):
        send_positions(lambda j: history[pl.ds(j * F2, F2), :], 0, chunk)
    for chunk in range(chunks):
        wait_chunk(0, chunk)
    transform(0, filter_main, filter_mid)
    for chunk in range(chunks):
        send_features(0, chunk)

    for chunk in range(chunks):
        wait_chunk(1, chunk)
        for j in range(chunk * CHUNK, (chunk + 1) * CHUNK):
            mixed = recv_out[0, j].reshape(seq * feats, F2).T.astype(jnp.float32)
            part = pl.ds(j * F2, F2)
            grad_rows[part, :] = local_rows(
                mixed,
                history[part, :],
                cotangent[part, :],
                gain_first[...],
                bias_first[...],
                w_in[...],
                w_out[...],
                gain_second[...],
            )
        send_positions(
            lambda j: grad_rows[pl.ds(j * F2, F2), :].astype(jnp.bfloat16), 1, chunk
        )

    for chunk in range(chunks):
        wait_chunk(2, chunk)
    transform(1, back_main, back_mid)
    for chunk in range(chunks):
        send_features(1, chunk)
    for chunk in range(chunks):
        wait_chunk(3, chunk)
        for j in range(chunk * CHUNK, (chunk + 1) * CHUNK):
            back = recv_out[1, j].reshape(seq * feats, F2).T.astype(jnp.float32)
            part = pl.ds(j * F2, F2)
            out[part, :] = (grad_rows[part, :] + back).astype(jnp.bfloat16)

    sent = send_in.at[0, :, pl.ds(0, seq - 1)]
    for way in range(4):
        pltpu.make_async_copy(sent, sent, send_sem.at[way]).wait()


def local(history, cotangent, filter_weight, gain_first, bias_first, w_in, w_out, gain_second):
    user_count, row_count, features = history.shape
    seq = lax.axis_size("seq")
    feats = features // seq
    rows = F1 // seq
    bf16, f32 = jnp.bfloat16, jnp.float32
    tables = [jnp.asarray(t) for t in host_tables()]

    full = lax.all_to_all(filter_weight, "seq", split_axis=3, concat_axis=1, tiled=True)
    full = lax.all_gather(full, "batch", axis=2, tiled=True)
    mirrored = jnp.flip(full[:, LINES:], axis=(1, 2)).astype(f32) * jnp.array(
        [1.0, -1.0], f32
    ).reshape(2, 1, 1, 1)
    main = full[:, :LINES].astype(f32) + jnp.pad(
        mirrored[:, : LINES - 1], ((0, 0), (1, 0), (0, 0), (0, 0))
    )
    filt = main.astype(bf16).transpose(3, 1, 0, 2).reshape(feats * LINES, 2 * F2)
    filt_mid = mirrored[:, LINES - 1].astype(bf16).transpose(2, 0, 1).reshape(feats, 2 * F2)

    vmem = pl.BlockSpec(memory_space=pltpu.VMEM)
    out, grad, grad_mid = pl.pallas_call(
        functools.partial(kernel, seq),
        out_shape=(
            jax.ShapeDtypeStruct((row_count, features), bf16),
            jax.ShapeDtypeStruct((feats * LINES, 2 * F2), bf16),
            jax.ShapeDtypeStruct((feats, 2 * F2), bf16),
        ),
        in_specs=[vmem] * 15,
        out_specs=(vmem,) * 3,
        scratch_shapes=[
            pltpu.VMEM((2, rows, seq, feats, F2), bf16),
            pltpu.VMEM((2, seq, rows, feats, F2), bf16),
            pltpu.VMEM((2, seq, rows, feats, F2), bf16),
            pltpu.VMEM((2, rows, seq, feats, F2), bf16),
            pltpu.VMEM((feats * LINES, 2 * F2), bf16),
            pltpu.VMEM((feats, 2 * F2), bf16),
            pltpu.VMEM((F1 * feats, F2), f32),
            pltpu.VMEM((row_count, features), f32),
            pltpu.SemaphoreType.DMA((4,)),
            pltpu.SemaphoreType.DMA((4, rows // CHUNK)),
        ],
        compiler_params=pltpu.CompilerParams(
            collective_id=0, has_side_effects=True, vmem_limit_bytes=48 * 2**20
        ),
    )(
        history.reshape(row_count, features),
        cotangent.reshape(row_count, features),
        filt,
        filt_mid,
        gain_first.reshape(1, features),
        bias_first.reshape(1, features),
        w_in,
        w_out,
        gain_second.reshape(1, features),
        *tables
    )
    half = jnp.concatenate(
        [
            grad.reshape(feats, LINES, 2, F2).transpose(2, 1, 3, 0),
            grad_mid.reshape(feats, 1, 2, F2).transpose(2, 1, 3, 0),
        ],
        axis=1,
    )
    sign = jnp.array([1.0, -1.0], bf16).reshape(2, 1, 1, 1)
    whole = jnp.concatenate([half, jnp.flip(half[:, 1:LINES], axis=(1, 2)) * sign], axis=1)
    part = lax.psum_scatter(whole, "batch", scatter_dimension=2, tiled=True)
    filter_grad = lax.all_to_all(part, "seq", split_axis=1, concat_axis=3, tiled=True)
    return (out.reshape(user_count, row_count, features), filter_grad.astype(f32))


def solution(mesh):
    placed = (
        P("batch", "seq", None),
        P("batch", "seq", None),
        P(None, "seq", "batch", None),
        P(),
        P(),
        P(),
        P(),
        P(),
    )
    return jax.shard_map(
        local,
        mesh=mesh,
        in_specs=placed,
        out_specs=(P("batch", "seq", None), P(None, "seq", "batch", None)),
        check_vma=False,
    )
```

```python
import functools
import math

import jax
import jax.numpy as jnp
import ml_dtypes
import numpy as np
from jax import lax
from jax.experimental import pallas as pl
from jax.experimental.pallas import tpu as pltpu
from jax.sharding import PartitionSpec as P

F1 = 128
F2 = 128
LINES = 64
CHUNK = 2
ZS, XS, CORES = 4, 4, 2

epsilon = 1e-05
inv_root_two = 1.0 / math.sqrt(2.0)
inv_root_tau = 1.0 / math.sqrt(2.0 * math.pi)
inv_length = 1.0 / (F1 * F2)


def host_tables():
    index = np.arange(F1)
    angle = 2.0 * np.pi * (index[:, None] * index[None, :] % F1) / F1
    cos, sin = np.cos(angle), np.sin(angle)
    outer_fwd = np.concatenate([cos[:LINES], -sin[:LINES]], axis=0)
    outer_inv = np.concatenate([cos[:LINES], -sin[:LINES]], axis=0).T
    inner_fwd = np.block([[cos, -sin], [sin, cos]])
    inner_inv = np.block([[cos, sin], [-sin, cos]])
    lines = np.arange(LINES + 1)
    phase = 2.0 * np.pi * (lines[:, None] * index[None, :]) / (F1 * F2)
    narrow = [t.astype(ml_dtypes.bfloat16) for t in (outer_fwd, outer_inv, inner_fwd, inner_inv)]
    twiddles = np.stack([np.cos(phase), np.sin(phase)]).astype(np.float32)
    return (*narrow, twiddles[:, :LINES], twiddles[:, LINES:], *permutations())


def permutations():
    spread = np.zeros((2, 2 * F2, 4 * F2), np.float32)
    collect = np.zeros((2 * F2, 2 * F2), np.float32)
    for part in range(2):
        for q in range(F2):
            for h in range(2):
                spread[h, part * F2 + q, (q // 4) * 16 + h * 8 + part * 4 + q % 4] = 1.0
            collect[(q // 4) * 8 + part * 4 + q % 4, part * F2 + q] = 1.0
    return spread.astype(ml_dtypes.bfloat16), collect.astype(ml_dtypes.bfloat16)


def dot(a, b):
    return jnp.dot(a, b, preferred_element_type=jnp.float32)


def dot_nt(a, b):
    return lax.dot_general(a, b, (((1,), (1,)), ((), ())), preferred_element_type=jnp.float32)


def mirror_rows(x):
    axis = x.ndim - 2
    size = x.shape[axis]
    row = lax.broadcasted_iota(jnp.int32, x.shape, axis)
    for step in (1, 2):
        up, down = pltpu.roll(x, step, axis), pltpu.roll(x, size - step, axis)
        x = jnp.where((row & step) != 0, up, down)
    return jnp.where((row & 4) != 0, -x, x)


def block_transpose(tiles):
    lane = lax.broadcasted_iota(jnp.int32, tiles[0].shape, 1) // 16
    result = []
    for to in range(8):
        total = tiles[to]
        for block in range(8):
            if block != to:
                moved = pltpu.roll(tiles[block], 16 * ((block - to) % 8), 1)
                total = jnp.where(lane == block, moved, total)
        result.append(total)
    return result


def mean(x):
    return jnp.mean(x, axis=-1, keepdims=True)


def local_rows(mixed, history, cot, gain_first, bias_first, w_in, w_out, gain_second):
    summed = mixed + history.astype(jnp.float32)
    center_one = summed - mean(summed)
    inv_one = lax.rsqrt(mean(center_one * center_one) + epsilon)
    norm_one = center_one * inv_one
    hidden = (norm_one * gain_first + bias_first).astype(jnp.bfloat16)
    preact = dot(hidden, w_in)
    cumul = 0.5 * (1.0 + lax.erf(preact * inv_root_two))
    activation = (preact * cumul).astype(jnp.bfloat16)
    output_sum = dot(activation, w_out) + hidden.astype(jnp.float32)
    center_two = output_sum - mean(output_sum)
    inv_two = lax.rsqrt(mean(center_two * center_two) + epsilon)
    norm_two = center_two * inv_two
    grad_norm = cot.astype(jnp.float32) * gain_second
    grad_sum = inv_two * (grad_norm - mean(grad_norm) - norm_two * mean(grad_norm * norm_two))
    grad_act = dot_nt(grad_sum.astype(jnp.bfloat16), w_out)
    density = jnp.exp(-0.5 * preact * preact) * inv_root_tau
    grad_pre = (grad_act * (cumul + preact * density)).astype(jnp.bfloat16)
    grad_hidden = dot_nt(grad_pre, w_in) + grad_sum
    grad_scaled = grad_hidden * gain_first
    return inv_one * (grad_scaled - mean(grad_scaled) - norm_one * mean(grad_scaled * norm_one))


def kernel(
    seq,
    batch,
    history,
    cotangent,
    filter_weight,
    gain_first,
    bias_first,
    w_in,
    w_out,
    gain_second,
    outer_fwd,
    outer_inv,
    inner_fwd,
    inner_inv,
    twiddle,
    twiddle_mid,
    spread,
    collect,
    out,
    filter_grad,
    send_in,
    send_out,
    recv_in,
    recv_out,
    spec,
    spec_mid,
    filt,
    filt_mid,
    field,
    grad_field,
    grad_mid,
    grad_rows,
    stage,
    scatter_send,
    scatter_recv,
    gathered,
    core_send,
    core_recv,
    x_send,
    x_recv,
    z_send,
    z_recv,
    return_send,
    return_recv,
    send_sem,
    recv_sem,
    side_send_sem,
    side_recv_sem,
):
    me = lax.axis_index("seq")
    mine = lax.axis_index("batch")
    rows = F1 // seq
    feats = history.shape[1] // seq
    chunks = rows // CHUNK
    core = lax.rem(mine, CORES)
    along_x = lax.rem(mine // CORES, XS)
    along_z = mine // (CORES * XS)
    opposite = batch - 1 - mine
    low = me < seq // 2

    def batch_index(z, x, c):
        return (z * XS + x) * CORES + c

    barrier = pltpu.get_barrier_semaphore()

    def greet(peer):
        pl.semaphore_signal(
            barrier, inc=1, device_id=peer, device_id_type=pl.DeviceIdType.MESH
        )

    def greet_seq(k, _):
        greet({"seq": lax.rem(me + k, seq)})
        return 0

    def greet_opposite(k, _):
        greet({"seq": k, "batch": opposite})
        return 0

    x_peers = [lax.rem(along_x + k, XS) for k in range(1, XS)]
    z_peers = [lax.rem(along_z + k, ZS) for k in range(1, ZS)]
    lax.fori_loop(1, seq, greet_seq, 0)
    lax.fori_loop(0, seq, greet_opposite, 0)
    for x in x_peers:
        greet({"batch": batch_index(along_z, x, core)})
    for z in z_peers:
        greet({"batch": batch_index(z, along_x, core)})
    greet({"batch": batch_index(along_z, along_x, 1 - core)})
    pl.semaphore_wait(barrier, 2 * seq - 1 + XS - 1 + ZS - 1 + 1)

    def side_copy(src, dst, way, peer):
        pltpu.make_async_remote_copy(
            src_ref=src,
            dst_ref=dst,
            send_sem=side_send_sem.at[way],
            recv_sem=side_recv_sem.at[way],
            device_id=peer,
            device_id_type=pl.DeviceIdType.MESH,
        ).start()

    def wait_bytes(ref, sem):
        pltpu.make_async_copy(ref, ref, sem).wait()

    def wait_all_seq(ref, sem):
        @pl.when(low)
        def _():
            wait_bytes(ref.at[pl.ds(0, seq - 1)], sem)

        @pl.when(jnp.logical_not(low))
        def _():
            wait_bytes(ref, sem)

    def scatter_filter():
        for part in range(2):
            for tile in range(2):
                for line in range(8):
                    stage[line, 8 * tile + 4 * part : 8 * tile + 4 * part + 4, :] = filter_weight[
                        part, line, :, 128 * tile : 128 * (tile + 1)
                    ].astype(jnp.float32)
        tiles = []
        for line in range(8):
            tile = stage[jnp.where(low, line, 7 - line)]
            tiles.append(jnp.where(low, tile, mirror_rows(tile)))
        for to, tile in enumerate(block_transpose(tiles)):
            scatter_send[to] = tile[:8]
            scatter_send[8 + to] = tile[8:]
        target = jnp.where(low, mine, opposite)

        def one(k, _):
            peer = lax.rem(me + k, seq)
            side_copy(
                scatter_send.at[peer], scatter_recv.at[me], 0, {"seq": peer, "batch": target}
            )
            return 0

        @pl.when(low)
        def _():
            scatter_recv[me] = scatter_send[me]

        lax.fori_loop(jnp.where(low, 1, 0), seq, one, 0)

    def gather_z():
        wait_all_seq(scatter_recv, side_recv_sem.at[0])
        lane = lax.broadcasted_iota(jnp.int32, (8, 128), 1)
        zeros = jnp.zeros((8, 128), jnp.float32)
        moved = [pltpu.roll(scatter_recv[seq - 1 - t], 16, 1) for t in range(8)]
        tiles = []
        for t in range(9):
            before = moved[t - 1] if t > 0 else zeros
            after = moved[t] if t < 8 else zeros
            tile = jnp.where(lane < 16, before, after)
            tiles.append(tile + scatter_recv[t] if t < 8 else tile)
        upper = jnp.concatenate(tiles[0:4] + [tiles[8]], axis=1)
        lower = jnp.concatenate(tiles[4:8] + [zeros], axis=1)
        gathered[along_z, along_x, core] = jnp.concatenate([upper, lower], axis=0).astype(
            jnp.bfloat16
        )
        for z in z_peers:
            here = gathered.at[along_z, along_x, core]
            side_copy(here, here, 1, {"batch": batch_index(z, along_x, core)})

    def gather_x():
        wait_bytes(gathered.at[pl.ds(0, ZS - 1), 0, 0], side_recv_sem.at[1])
        for x in x_peers:
            here = gathered.at[:, along_x, core]
            side_copy(here, here, 2, {"batch": batch_index(along_z, x, core)})

    def gather_core():
        wait_bytes(gathered.at[:, pl.ds(0, XS - 1), 0], side_recv_sem.at[2])
        here = gathered.at[:, :, core]
        side_copy(here, here, 3, {"batch": batch_index(along_z, along_x, 1 - core)})

    def gather_finish():
        wait_bytes(gathered.at[:, :, 0], side_recv_sem.at[3])
        whole = gathered[...].reshape(batch * 16, 640)
        for h in range(2):
            piece = dot(spread[h], whole[:, :512]).astype(jnp.bfloat16).T.astype(jnp.float32)
            field[512 * h : 512 * (h + 1), :] = piece[:, :F2]
            field[1024 + 512 * h : 1024 + 512 * (h + 1), :] = piece[:, F2:]
        piece = dot(spread[0], whole[:, 512:]).astype(jnp.bfloat16).T
        filt_mid[...] = piece[:feats]
        for d in range(feats):
            real = field[pl.ds(d, LINES, stride=feats), :]
            imag = field[pl.ds(1024 + d, LINES, stride=feats), :]
            filt[d * LINES : (d + 1) * LINES, :] = jnp.concatenate([real, imag], axis=1).astype(
                jnp.bfloat16
            )

    def reduce_core():
        parts = []
        for h in range(2):
            real = grad_field[512 * h : 512 * (h + 1), :]
            imag = grad_field[1024 + 512 * h : 1024 + 512 * (h + 1), :]
            both = jnp.concatenate([real, imag], axis=1).astype(jnp.bfloat16)
            parts.append(dot_nt(collect[...], both).reshape(batch, 8, 512))
        mid = jnp.concatenate(
            [grad_mid[...], jnp.zeros((128 - feats, 2 * F2), jnp.float32)], axis=0
        ).astype(jnp.bfloat16)
        last = dot_nt(collect[...], mid).reshape(batch, 8, 128)
        both = jnp.concatenate(
            [
                jnp.concatenate(parts, axis=1),
                jnp.concatenate([last, jnp.zeros_like(last)], axis=1),
            ],
            axis=2,
        )
        core_send[...] = both.astype(jnp.bfloat16).reshape(ZS, XS, CORES, 16, 640)
        side_copy(
            core_send.at[:, :, 1 - core],
            core_recv,
            4,
            {"batch": batch_index(along_z, along_x, 1 - core)},
        )

    def reduce_x():
        wait_bytes(core_recv, side_recv_sem.at[4])
        own = core_send[:, :, core].astype(jnp.float32) + core_recv[...].astype(jnp.float32)
        x_send[...] = own.astype(jnp.bfloat16)
        x_recv[along_x] = x_send[:, along_x]
        for x in x_peers:
            side_copy(
                x_send.at[:, x], x_recv.at[along_x], 5, {"batch": batch_index(along_z, x, core)}
            )

    def reduce_z():
        wait_bytes(x_recv.at[pl.ds(0, XS - 1)], side_recv_sem.at[5])
        z_send[...] = jnp.sum(x_recv[...].astype(jnp.float32), axis=0).astype(jnp.bfloat16)
        z_recv[along_z] = z_send[along_z]
        for z in z_peers:
            side_copy(
                z_send.at[z], z_recv.at[along_z], 6, {"batch": batch_index(z, along_x, core)}
            )

    def return_grad():
        wait_bytes(z_recv.at[pl.ds(0, ZS - 1)], side_recv_sem.at[6])
        total = jnp.sum(z_recv[...].astype(jnp.float32), axis=0)
        tiles = [total[:8, 128 * t : 128 * (t + 1)] for t in range(4)]
        tiles += [total[8:, 128 * t : 128 * (t + 1)] for t in range(4)]
        tiles.append(total[:8, 512:])
        lane = lax.broadcasted_iota(jnp.int32, (8, 128), 1)
        moved = [pltpu.roll(t, 112, 1) for t in tiles]
        for t in range(8):
            return_send[t] = tiles[t]
            return_send[seq - 1 - t] = jnp.where(lane < 112, moved[t], moved[t + 1])

        def one(k, _):
            peer = lax.rem(me + k, seq)
            target = jnp.where(peer < seq // 2, mine, opposite)
            side_copy(
                return_send.at[peer], return_recv.at[me], 7, {"seq": peer, "batch": target}
            )
            return 0

        @pl.when(low)
        def _():
            return_recv[me] = return_send[me]

        lax.fori_loop(jnp.where(low, 1, 0), seq, one, 0)

    def return_finish():
        wait_all_seq(return_recv, side_recv_sem.at[7])
        tiles = [
            jnp.concatenate([return_recv[t], return_recv[8 + t]], axis=0) for t in range(8)
        ]
        for line, tile in enumerate(block_transpose(tiles)):
            stage[jnp.where(low, line, 7 - line)] = jnp.where(low, tile, mirror_rows(tile))
        for part in range(2):
            for tile in range(2):
                for line in range(8):
                    filter_grad[part, line, :, 128 * tile : 128 * (tile + 1)] = stage[
                        line, 8 * tile + 4 * part : 8 * tile + 4 * part + 4, :
                    ]

    def side_drain():
        wait_all_seq(scatter_send, side_send_sem.at[0])
        wait_bytes(gathered.at[pl.ds(0, ZS - 1), 0, 0], side_send_sem.at[1])
        wait_bytes(gathered.at[:, pl.ds(0, XS - 1), 0], side_send_sem.at[2])
        wait_bytes(gathered.at[:, :, 0], side_send_sem.at[3])
        wait_bytes(core_recv, side_send_sem.at[4])
        wait_bytes(x_recv.at[pl.ds(0, XS - 1)], side_send_sem.at[5])
        wait_bytes(z_recv.at[pl.ds(0, ZS - 1)], side_send_sem.at[6])
        wait_all_seq(return_send, side_send_sem.at[7])

    def exchange(src, dst, way, chunk):
        def one(k, _):
            peer = lax.rem(me + k, seq)
            pltpu.make_async_remote_copy(
                src_ref=src(peer),
                dst_ref=dst,
                send_sem=send_sem.at[way],
                recv_sem=recv_sem.at[way, chunk],
                device_id={"seq": peer},
                device_id_type=pl.DeviceIdType.MESH,
            ).start()
            return 0

        lax.fori_loop(1, seq, one, 0)

    def send_positions(x, way, chunk):
        for j in range(chunk * CHUNK, (chunk + 1) * CHUNK):
            block = x(j).T.reshape(seq, feats, F2)
            send_in[way, j] = block
        part = pl.ds(chunk * CHUNK, CHUNK)
        recv_in[way, me, part] = send_in[way, part, me]
        exchange(
            lambda peer: send_in.at[way, part, peer], recv_in.at[way, me, part], 2 * way, chunk
        )

    def send_features(way, chunk):
        part = pl.ds(chunk * CHUNK, CHUNK)
        recv_out[way, part, me] = send_out[way, me, part]
        exchange(
            lambda peer: send_out.at[way, peer, part], recv_out.at[way, part, me], 2 * way + 1, chunk
        )

    def wait_chunk(way, chunk):
        whole = send_in.at[0, pl.ds(0, CHUNK), pl.ds(0, seq - 1)]
        pltpu.make_async_copy(whole, whole, recv_sem.at[way, chunk]).wait()

    def transform(way, multiply, multiply_mid):
        tiles = recv_in[way].reshape(F1 // 2, 2, feats, F2)
        mid = jnp.sum(
            tiles[:, 0].astype(jnp.float32) - tiles[:, 1].astype(jnp.float32), axis=0
        )
        field[...] = recv_in[way].reshape(F1 * feats, F2).astype(jnp.float32)
        cos, sin = twiddle[0], twiddle[1]

        def pair(first):
            return [field[pl.ds(first + i, F1, stride=feats), :] for i in range(2)]

        def step(group, _):
            base = group * 4
            halves = []
            for sub in range(2):
                two = jnp.concatenate(pair(base + 2 * sub), axis=1).astype(jnp.bfloat16)
                both = dot(outer_fwd[...], two)
                for i in range(2):
                    real = both[:LINES, i * F2 : (i + 1) * F2]
                    imag = both[LINES:, i * F2 : (i + 1) * F2]
                    halves.append(
                        jnp.concatenate(
                            [real * cos + imag * sin, imag * cos - real * sin], axis=1
                        ).astype(jnp.bfloat16)
                    )
            spectrum = dot(jnp.concatenate(halves, axis=0), inner_fwd[...])
            where = pl.ds(pl.multiple_of(base * LINES, 4 * LINES), 4 * LINES)
            product = multiply(spectrum, where, base)
            half = dot(product, inner_inv[...])
            for sub in range(2):
                columns = []
                for i in range(2):
                    piece = half[(2 * sub + i) * LINES : (2 * sub + i + 1) * LINES]
                    real, imag = piece[:, :F2], piece[:, F2:]
                    columns.append(
                        jnp.concatenate(
                            [real * cos - imag * sin, imag * cos + real * sin], axis=0
                        ).astype(jnp.bfloat16)
                    )
                result = dot(outer_inv[...], jnp.concatenate(columns, axis=1)) * inv_length
                for i in range(2):
                    field[pl.ds(base + 2 * sub + i, F1, stride=feats), :] = result[
                        :, i * F2 : (i + 1) * F2
                    ]
            return 0

        lax.fori_loop(0, feats // 4, step, 0)

        cos_mid, sin_mid = twiddle_mid[0], twiddle_mid[1]
        half = jnp.concatenate([mid * cos_mid, -mid * sin_mid], axis=1).astype(jnp.bfloat16)
        product = multiply_mid(dot(half, inner_fwd[...]))
        half = dot(product, inner_inv[...])
        last = (half[:, :F2] * cos_mid - half[:, F2:] * sin_mid).astype(jnp.bfloat16)
        last = last.astype(jnp.float32) * inv_length
        both = field[...].reshape(F1 // 2, 2, feats, F2)
        sign = jnp.where(lax.broadcasted_iota(jnp.int32, both.shape, 1) == 0, 1.0, -1.0)
        both = both + sign * last[None, None]
        send_out[way] = both.astype(jnp.bfloat16).reshape(seq, rows, feats, F2)

    def split(z):
        return z[:, :F2].astype(jnp.float32), z[:, F2:].astype(jnp.float32)

    def times(z, f):
        zr, zi = split(z)
        fr, fi = split(f)
        return jnp.concatenate([zr * fr - zi * fi, zr * fi + zi * fr], axis=1).astype(jnp.bfloat16)

    def times_conj(z, f):
        zr, zi = split(z)
        fr, fi = split(f)
        return jnp.concatenate([fr * zr + fi * zi, fr * zi - fi * zr], axis=1)

    def filter_main(z, where, feature):
        z = z.astype(jnp.bfloat16)
        spec[where, :] = z
        return times(z, filt[where, :])

    def filter_mid(z):
        z = z.astype(jnp.bfloat16)
        spec_mid[...] = z
        return times(z, filt_mid[...])

    def back_main(z, where, feature):
        z = z.astype(jnp.bfloat16)
        term = times_conj(z, spec[where, :]) * inv_length
        for i in range(4):
            piece = term[i * LINES : (i + 1) * LINES]
            grad_field[pl.ds(feature + i, LINES, stride=feats), :] = piece[:, :F2]
            grad_field[pl.ds(1024 + feature + i, LINES, stride=feats), :] = piece[:, F2:]
        return times_conj(z, filt[where, :]).astype(jnp.bfloat16)

    def back_mid(z):
        z = z.astype(jnp.bfloat16)
        grad_mid[...] = times_conj(z, spec_mid[...]) * inv_length
        return times_conj(z, filt_mid[...]).astype(jnp.bfloat16)

    scatter_filter()
    for chunk in range(chunks):
        send_positions(lambda j: history[pl.ds(j * F2, F2), :], 0, chunk)
    gather_z()
    gather_x()
    gather_core()
    gather_finish()
    for chunk in range(chunks):
        wait_chunk(0, chunk)
    transform(0, filter_main, filter_mid)
    for chunk in range(chunks):
        send_features(0, chunk)

    for chunk in range(chunks):
        wait_chunk(1, chunk)
        for j in range(chunk * CHUNK, (chunk + 1) * CHUNK):
            mixed = recv_out[0, j].reshape(seq * feats, F2).T.astype(jnp.float32)
            part = pl.ds(j * F2, F2)
            grad_rows[part, :] = local_rows(
                mixed,
                history[part, :],
                cotangent[part, :],
                gain_first[...],
                bias_first[...],
                w_in[...],
                w_out[...],
                gain_second[...],
            )
        send_positions(
            lambda j: grad_rows[pl.ds(j * F2, F2), :].astype(jnp.bfloat16), 1, chunk
        )

    for chunk in range(chunks):
        wait_chunk(2, chunk)
    transform(1, back_main, back_mid)
    for chunk in range(chunks):
        send_features(1, chunk)
    reduce_core()
    reduce_x()
    reduce_z()
    return_grad()
    for chunk in range(chunks):
        wait_chunk(3, chunk)
        for j in range(chunk * CHUNK, (chunk + 1) * CHUNK):
            back = recv_out[1, j].reshape(seq * feats, F2).T.astype(jnp.float32)
            part = pl.ds(j * F2, F2)
            out[part, :] = (grad_rows[part, :] + back).astype(jnp.bfloat16)

    return_finish()
    side_drain()
    sent = send_in.at[0, :, pl.ds(0, seq - 1)]
    for way in range(4):
        pltpu.make_async_copy(sent, sent, send_sem.at[way]).wait()


def local(history, cotangent, filter_weight, gain_first, bias_first, w_in, w_out, gain_second):
    user_count, row_count, features = history.shape
    seq = lax.axis_size("seq")
    feats = features // seq
    rows = F1 // seq
    bf16, f32 = jnp.bfloat16, jnp.float32
    tables = [jnp.asarray(t) for t in host_tables()]

    vmem = pl.BlockSpec(memory_space=pltpu.VMEM)
    batch = lax.axis_size("batch")
    dma = pltpu.SemaphoreType.DMA
    out, filter_grad = pl.pallas_call(
        functools.partial(kernel, seq, batch),
        out_shape=(
            jax.ShapeDtypeStruct((row_count, features), bf16),
            jax.ShapeDtypeStruct(filter_weight.shape, f32),
        ),
        in_specs=[vmem] * 16,
        out_specs=(vmem,) * 2,
        scratch_shapes=[
            pltpu.VMEM((2, rows, seq, feats, F2), bf16),
            pltpu.VMEM((2, seq, rows, feats, F2), bf16),
            pltpu.VMEM((2, seq, rows, feats, F2), bf16),
            pltpu.VMEM((2, rows, seq, feats, F2), bf16),
            pltpu.VMEM((feats * LINES, 2 * F2), bf16),
            pltpu.VMEM((feats, 2 * F2), bf16),
            pltpu.VMEM((feats * LINES, 2 * F2), bf16),
            pltpu.VMEM((feats, 2 * F2), bf16),
            pltpu.VMEM((F1 * feats, F2), f32),
            pltpu.VMEM((2 * LINES * feats, F2), f32),
            pltpu.VMEM((feats, 2 * F2), f32),
            pltpu.VMEM((row_count, features), f32),
            pltpu.VMEM((8, 16, 128), f32),
            pltpu.VMEM((seq, 8, 128), f32),
            pltpu.VMEM((seq, 8, 128), f32),
            pltpu.VMEM((ZS, XS, CORES, 16, 640), bf16),
            pltpu.VMEM((ZS, XS, CORES, 16, 640), bf16),
            pltpu.VMEM((ZS, XS, 16, 640), bf16),
            pltpu.VMEM((ZS, XS, 16, 640), bf16),
            pltpu.VMEM((XS, ZS, 16, 640), bf16),
            pltpu.VMEM((ZS, 16, 640), bf16),
            pltpu.VMEM((ZS, 16, 640), bf16),
            pltpu.VMEM((seq, 8, 128), f32),
            pltpu.VMEM((seq, 8, 128), f32),
            dma((4,)),
            dma((4, rows // CHUNK)),
            dma((8,)),
            dma((8,)),
        ],
        compiler_params=pltpu.CompilerParams(
            collective_id=0, has_side_effects=True, vmem_limit_bytes=48 * 2**20
        ),
    )(
        history.reshape(row_count, features),
        cotangent.reshape(row_count, features),
        filter_weight,
        gain_first.reshape(1, features),
        bias_first.reshape(1, features),
        w_in,
        w_out,
        gain_second.reshape(1, features),
        *tables
    )
    return (out.reshape(user_count, row_count, features), filter_grad)


def solution(mesh):
    placed = (
        P("batch", "seq", None),
        P("batch", "seq", None),
        P(None, "seq", "batch", None),
        P(),
        P(),
        P(),
        P(),
        P(),
    )
    return jax.shard_map(
        local,
        mesh=mesh,
        in_specs=placed,
        out_specs=(P("batch", "seq", None), P(None, "seq", "batch", None)),
        check_vma=False,
    )
```

```python
import functools
import math

import jax
import jax.numpy as jnp
import ml_dtypes
import numpy as np
from jax import lax
from jax.experimental import pallas as pl
from jax.experimental.pallas import tpu as pltpu
from jax.sharding import PartitionSpec as P

F1 = 128
F2 = 128
LINES = 64
CHUNK = 2
ZS, XS, CORES = 4, 4, 2

epsilon = 1e-05
inv_root_two = 1.0 / math.sqrt(2.0)
inv_root_tau = 1.0 / math.sqrt(2.0 * math.pi)
inv_length = 1.0 / (F1 * F2)


def columns(table):
    blocks = np.split(table, table.shape[1] // 128, axis=1)
    return np.stack(blocks).astype(ml_dtypes.bfloat16)


def whole(table):
    return jnp.concatenate([table[k] for k in range(table.shape[0])], axis=1)


def host_tables():
    index = np.arange(F1)
    angle = 2.0 * np.pi * (index[:, None] * index[None, :] % F1) / F1
    cos, sin = np.cos(angle), np.sin(angle)
    outer_fwd = np.concatenate([cos[:LINES], -sin[:LINES]], axis=0)
    outer_inv = np.concatenate([cos[:LINES], -sin[:LINES]], axis=0).T
    inner_fwd = np.block([[cos, -sin], [sin, cos]])
    inner_inv = np.block([[cos, sin], [-sin, cos]])
    lines = np.arange(LINES + 1)
    phase = 2.0 * np.pi * (lines[:, None] * index[None, :]) / (F1 * F2)
    narrow = [columns(t) for t in (outer_fwd, outer_inv, inner_fwd, inner_inv)]
    twiddles = np.stack([np.cos(phase), np.sin(phase)]).astype(np.float32)
    return (*narrow, twiddles[:, :LINES], twiddles[:, LINES:], *permutations())


def permutations():
    spread = np.zeros((2, 2 * F2, 4 * F2), np.float32)
    collect = np.zeros((2 * F2, 2 * F2), np.float32)
    for part in range(2):
        for q in range(F2):
            for h in range(2):
                spread[h, part * F2 + q, (q // 4) * 16 + h * 8 + part * 4 + q % 4] = 1.0
            collect[(q // 4) * 8 + part * 4 + q % 4, part * F2 + q] = 1.0
    return columns(spread.reshape(4 * F2, 4 * F2)), columns(collect)


def dot(a, b):
    return jnp.dot(a, b, preferred_element_type=jnp.float32)


def dot_nt(a, b):
    return lax.dot_general(a, b, (((1,), (1,)), ((), ())), preferred_element_type=jnp.float32)


def mirror_rows(x):
    axis = x.ndim - 2
    size = x.shape[axis]
    row = lax.broadcasted_iota(jnp.int32, x.shape, axis)
    for step in (1, 2):
        up, down = pltpu.roll(x, step, axis), pltpu.roll(x, size - step, axis)
        x = jnp.where((row & step) != 0, up, down)
    return jnp.where((row & 4) != 0, -x, x)


def block_transpose(tiles):
    lane = lax.broadcasted_iota(jnp.int32, tiles[0].shape, 1) // 16
    result = []
    for to in range(8):
        total = tiles[to]
        for block in range(8):
            if block != to:
                moved = pltpu.roll(tiles[block], 16 * ((block - to) % 8), 1)
                total = jnp.where(lane == block, moved, total)
        result.append(total)
    return result


def mean(x):
    return jnp.mean(x, axis=-1, keepdims=True)


def local_rows(mixed, history, cot, gain_first, bias_first, w_in, w_out, gain_second):
    summed = mixed + history.astype(jnp.float32)
    center_one = summed - mean(summed)
    inv_one = lax.rsqrt(mean(center_one * center_one) + epsilon)
    norm_one = center_one * inv_one
    hidden = (norm_one * gain_first + bias_first).astype(jnp.bfloat16)
    preact = dot(hidden, w_in)
    cumul = 0.5 * (1.0 + lax.erf(preact * inv_root_two))
    activation = (preact * cumul).astype(jnp.bfloat16)
    output_sum = dot(activation, w_out) + hidden.astype(jnp.float32)
    center_two = output_sum - mean(output_sum)
    inv_two = lax.rsqrt(mean(center_two * center_two) + epsilon)
    norm_two = center_two * inv_two
    grad_norm = cot.astype(jnp.float32) * gain_second
    grad_sum = inv_two * (grad_norm - mean(grad_norm) - norm_two * mean(grad_norm * norm_two))
    grad_act = dot_nt(grad_sum.astype(jnp.bfloat16), w_out)
    density = jnp.exp(-0.5 * preact * preact) * inv_root_tau
    grad_pre = (grad_act * (cumul + preact * density)).astype(jnp.bfloat16)
    grad_hidden = dot_nt(grad_pre, w_in) + grad_sum
    grad_scaled = grad_hidden * gain_first
    return inv_one * (grad_scaled - mean(grad_scaled) - norm_one * mean(grad_scaled * norm_one))


def kernel(
    seq,
    batch,
    history_hbm,
    cotangent_hbm,
    filter_weight_hbm,
    gain_first_hbm,
    bias_first_hbm,
    w_in_hbm,
    w_out_hbm,
    gain_second_hbm,
    outer_fwd_hbm,
    outer_inv_hbm,
    inner_fwd_hbm,
    inner_inv_hbm,
    twiddle_hbm,
    twiddle_mid_hbm,
    spread_hbm,
    collect_hbm,
    out_hbm,
    filter_grad_hbm,
    history,
    cotangent,
    filter_weight,
    gain_first,
    bias_first,
    w_in,
    w_out,
    gain_second,
    outer_fwd,
    outer_inv,
    inner_fwd,
    inner_inv,
    twiddle,
    twiddle_mid,
    spread,
    collect,
    out,
    filter_grad,
    send_in,
    send_out,
    recv_in,
    recv_out,
    spec,
    spec_mid,
    back_spec,
    back_mid,
    filt,
    filt_mid,
    field,
    grad_field,
    grad_rows,
    stage,
    scatter_send,
    scatter_recv,
    gathered,
    core_send,
    core_recv,
    x_send,
    x_half,
    x_recv,
    z_send,
    z_half_left,
    z_half_right,
    z_recv,
    return_send,
    return_recv,
    load_sem,
    store_sem,
    send_sem,
    recv_sem,
    side_send_sem,
    side_recv_sem,
):
    me = lax.axis_index("seq")
    mine = lax.axis_index("batch")
    rows = F1 // seq
    feats = history.shape[1] // seq
    chunks = rows // CHUNK
    core = lax.rem(mine, CORES)
    along_x = lax.rem(mine // CORES, XS)
    along_z = mine // (CORES * XS)
    opposite = batch - 1 - mine
    low = me < seq // 2

    def batch_index(z, x, c):
        return (z * XS + x) * CORES + c

    x_right, x_left, x_far = (lax.rem(along_x + k, XS) for k in (1, XS - 1, 2))
    z_right, z_left, z_far = (lax.rem(along_z + k, ZS) for k in (1, ZS - 1, 2))
    to_x_right = {"batch": batch_index(along_z, x_right, core)}
    to_x_left = {"batch": batch_index(along_z, x_left, core)}
    to_z_right = {"batch": batch_index(z_right, along_x, core)}
    to_z_left = {"batch": batch_index(z_left, along_x, core)}
    to_core = {"batch": batch_index(along_z, along_x, 1 - core)}

    loads = {}
    for name, source, target in (
        ("filter", filter_weight_hbm, filter_weight),
        ("history", history_hbm, history),
        ("outer_fwd", outer_fwd_hbm, outer_fwd),
        ("twiddle", twiddle_hbm, twiddle),
        ("twiddle_mid", twiddle_mid_hbm, twiddle_mid),
        ("inner_fwd", inner_fwd_hbm, inner_fwd),
        ("spread", spread_hbm, spread),
        ("inner_inv", inner_inv_hbm, inner_inv),
        ("outer_inv", outer_inv_hbm, outer_inv),
        ("gain_first", gain_first_hbm, gain_first),
        ("bias_first", bias_first_hbm, bias_first),
        ("w_in", w_in_hbm, w_in),
        ("w_out", w_out_hbm, w_out),
        ("gain_second", gain_second_hbm, gain_second),
        ("cotangent", cotangent_hbm, cotangent),
        ("collect", collect_hbm, collect),
    ):
        loads[name] = pltpu.make_async_copy(source, target, load_sem.at[len(loads)])
        loads[name].start()

    barrier = pltpu.get_barrier_semaphore()

    def greet(peer):
        pl.semaphore_signal(
            barrier, inc=1, device_id=peer, device_id_type=pl.DeviceIdType.MESH
        )

    def greet_seq(k, _):
        greet({"seq": lax.rem(me + k, seq)})
        return 0

    def greet_opposite(k, _):
        greet({"seq": k, "batch": opposite})
        return 0

    lax.fori_loop(0, seq, greet_opposite, 0)
    for peer in (to_x_right, to_x_left, to_z_right, to_z_left, to_core):
        greet(peer)
    lax.fori_loop(1, seq, greet_seq, 0)

    def side_copy(src, dst, way, peer):
        pltpu.make_async_remote_copy(
            src_ref=src,
            dst_ref=dst,
            send_sem=side_send_sem.at[way],
            recv_sem=side_recv_sem.at[way],
            device_id=peer,
            device_id_type=pl.DeviceIdType.MESH,
        ).start()

    def wait_bytes(ref, sem):
        pltpu.make_async_copy(ref, ref, sem).wait()

    def wait_all_seq(ref, sem):
        @pl.when(low)
        def _():
            wait_bytes(ref.at[pl.ds(0, seq - 1)], sem)

        @pl.when(jnp.logical_not(low))
        def _():
            wait_bytes(ref, sem)

    piece = gathered.at[0, 0, 0]
    sizes = {
        1: piece,
        2: piece,
        3: piece.at[pl.ds(0, 3)],
        4: piece.at[pl.ds(0, 2)],
        5: gathered.at[:, 0, 0],
        6: gathered.at[:, 0, 0],
        7: gathered.at[pl.ds(0, 2), 0, 0],
        8: gathered.at[pl.ds(0, 2), 0, 0],
        9: gathered.at[:, :, 0],
        10: core_recv,
        11: x_half.at[0],
        12: x_half.at[0],
        13: x_recv.at[0],
        14: x_recv.at[0],
        15: z_half_left,
        16: z_half_right,
        17: z_recv.at[0],
        18: z_recv.at[0],
    }

    def arrived(*ways):
        for way in ways:
            wait_bytes(sizes[way], side_recv_sem.at[way])

    def scatter_prepare():
        for part in range(2):
            for tile in range(2):
                for line in range(8):
                    stage[line, 8 * tile + 4 * part : 8 * tile + 4 * part + 4, :] = filter_weight[
                        part, line, :, 128 * tile : 128 * (tile + 1)
                    ].astype(jnp.float32)
        tiles = []
        for line in range(8):
            tile = stage[jnp.where(low, line, 7 - line)]
            tiles.append(jnp.where(low, tile, mirror_rows(tile)))
        for to, tile in enumerate(block_transpose(tiles)):
            scatter_send[to] = tile[:8]
            scatter_send[8 + to] = tile[8:]

    def scatter_start():
        target = jnp.where(low, mine, opposite)

        def one(k, _):
            peer = lax.rem(me + k, seq)
            side_copy(
                scatter_send.at[peer], scatter_recv.at[me], 0, {"seq": peer, "batch": target}
            )
            return 0

        @pl.when(low)
        def _():
            scatter_recv[me] = scatter_send[me]

        lax.fori_loop(jnp.where(low, 1, 0), seq, one, 0)

    def gather():
        wait_all_seq(scatter_recv, side_recv_sem.at[0])
        lane = lax.broadcasted_iota(jnp.int32, (8, 128), 1)
        zeros = jnp.zeros((8, 128), jnp.float32)
        moved = [pltpu.roll(scatter_recv[seq - 1 - t], 16, 1) for t in range(8)]
        tiles = []
        for t in range(9):
            before = moved[t - 1] if t > 0 else zeros
            after = moved[t] if t < 8 else zeros
            tile = jnp.where(lane < 16, before, after)
            tiles.append(tile + scatter_recv[t] if t < 8 else tile)
        for t in range(5):
            upper = tiles[t] if t < 4 else tiles[8]
            lower = tiles[4 + t] if t < 4 else zeros
            gathered[along_z, along_x, core, t] = jnp.concatenate([upper, lower], axis=0).astype(
                jnp.bfloat16
            )
        own = gathered.at[along_z, along_x, core]
        side_copy(own, own, 1, to_z_right)
        side_copy(own, own, 2, to_z_left)
        arrived(1)
        block = gathered.at[z_left, along_x, core, pl.ds(0, 3)]
        side_copy(block, block, 3, to_z_right)
        arrived(2)
        block = gathered.at[z_right, along_x, core, pl.ds(3, 2)]
        side_copy(block, block, 4, to_z_left)
        arrived(3, 4)
        block = gathered.at[:, along_x, core]
        side_copy(block, block, 5, to_x_right)
        side_copy(block, block, 6, to_x_left)
        arrived(5)
        block = gathered.at[pl.ds(0, 2), x_left, core]
        side_copy(block, block, 7, to_x_right)
        arrived(6)
        block = gathered.at[pl.ds(2, 2), x_right, core]
        side_copy(block, block, 8, to_x_left)
        arrived(7, 8)
        block = gathered.at[:, :, core]
        side_copy(block, block, 9, to_core)
        arrived(9)
        loads["spread"].wait()
        parts = [gathered[:, :, :, t].reshape(batch * 16, 128) for t in range(5)]
        block = jnp.concatenate(parts[:4], axis=1)
        for h in range(2):
            table = jnp.concatenate(
                [spread[k, 2 * F2 * h : 2 * F2 * (h + 1)] for k in range(4)], axis=1
            )
            result = dot(table, block).astype(jnp.bfloat16).T.astype(jnp.float32)
            field[512 * h : 512 * (h + 1), :] = result[:, :F2]
            field[1024 + 512 * h : 1024 + 512 * (h + 1), :] = result[:, F2:]
        table = jnp.concatenate([spread[k, : 2 * F2] for k in range(4)], axis=1)
        filt_mid[...] = dot(table, parts[4]).astype(jnp.bfloat16).T[:feats]
        for d in range(feats):
            real = field[pl.ds(d, LINES, stride=feats), :]
            imag = field[pl.ds(1024 + d, LINES, stride=feats), :]
            filt[d * LINES : (d + 1) * LINES, :] = jnp.concatenate([real, imag], axis=1).astype(
                jnp.bfloat16
            )

    def reduce_start():
        for d in range(feats):
            where = pl.ds(d * LINES, LINES)
            term = times_conj(back_spec[where, :], spec[where, :]) * inv_length
            grad_field[pl.ds(d, LINES, stride=feats), :] = term[:, :F2]
            grad_field[pl.ds(1024 + d, LINES, stride=feats), :] = term[:, F2:]
        loads["collect"].wait()
        parts = []
        for h in range(2):
            real = grad_field[512 * h : 512 * (h + 1), :]
            imag = grad_field[1024 + 512 * h : 1024 + 512 * (h + 1), :]
            both = jnp.concatenate([real, imag], axis=1).astype(jnp.bfloat16)
            parts.append(dot_nt(whole(collect), both).reshape(batch, 8, 512))
        mid = jnp.concatenate(
            [
                times_conj(back_mid[...], spec_mid[...]) * inv_length,
                jnp.zeros((128 - feats, 2 * F2), jnp.float32),
            ],
            axis=0,
        ).astype(jnp.bfloat16)
        last = dot_nt(whole(collect), mid).reshape(batch, 8, 128)
        both = jnp.concatenate(parts, axis=1).astype(jnp.bfloat16)
        both = both.reshape(ZS, XS, CORES, 16, 512)
        for t in range(4):
            core_send[:, :, :, t] = both[..., 128 * t : 128 * (t + 1)]
        last = jnp.concatenate([last, jnp.zeros_like(last)], axis=1).astype(jnp.bfloat16)
        core_send[:, :, :, 4] = last.reshape(ZS, XS, CORES, 16, 128)
        side_copy(core_send.at[:, :, 1 - core], core_recv, 10, to_core)

    def add(a, b):
        return (a.astype(jnp.float32) + b.astype(jnp.float32)).astype(jnp.bfloat16)

    def reduce_x():
        arrived(10)
        for x in range(XS):
            x_send[x] = add(core_send[:, x, core], core_recv[:, x])
        side_copy(x_send.at[x_far, pl.ds(0, 2)], x_half.at[0], 11, to_x_right)
        side_copy(x_send.at[x_far, pl.ds(2, 2)], x_half.at[1], 12, to_x_left)

    def reduce_x_second():
        arrived(11)
        x_send[x_right, 0:2] = add(x_send[x_right, 0:2], x_half[0])
        side_copy(x_send.at[x_right], x_recv.at[0], 13, to_x_right)
        arrived(12)
        x_send[x_left, 2:4] = add(x_send[x_left, 2:4], x_half[1])
        side_copy(x_send.at[x_left], x_recv.at[1], 14, to_x_left)

    def reduce_z():
        arrived(13, 14)
        total = x_send[along_x].astype(jnp.float32) + x_recv[0].astype(jnp.float32)
        z_send[...] = (total + x_recv[1].astype(jnp.float32)).astype(jnp.bfloat16)
        side_copy(z_send.at[z_far, pl.ds(0, 3)], z_half_left, 15, to_z_right)
        side_copy(z_send.at[z_far, pl.ds(3, 2)], z_half_right, 16, to_z_left)

    def reduce_z_second():
        arrived(15)
        z_send[z_right, 0:3] = add(z_send[z_right, 0:3], z_half_left[...])
        side_copy(z_send.at[z_right], z_recv.at[0], 17, to_z_right)
        arrived(16)
        z_send[z_left, 3:5] = add(z_send[z_left, 3:5], z_half_right[...])
        side_copy(z_send.at[z_left], z_recv.at[1], 18, to_z_left)

    def return_grad():
        arrived(17, 18)
        total = z_send[along_z].astype(jnp.float32) + z_recv[0].astype(jnp.float32)
        total = total + z_recv[1].astype(jnp.float32)
        tiles = [total[t, :8] for t in range(4)] + [total[t, 8:] for t in range(4)]
        tiles.append(total[4, :8])
        lane = lax.broadcasted_iota(jnp.int32, (8, 128), 1)
        moved = [pltpu.roll(t, 112, 1) for t in tiles]
        for t in range(8):
            return_send[t] = tiles[t]
            return_send[seq - 1 - t] = jnp.where(lane < 112, moved[t], moved[t + 1])

        def one(k, _):
            peer = lax.rem(me + k, seq)
            target = jnp.where(peer < seq // 2, mine, opposite)
            side_copy(
                return_send.at[peer], return_recv.at[me], 19, {"seq": peer, "batch": target}
            )
            return 0

        @pl.when(low)
        def _():
            return_recv[me] = return_send[me]

        lax.fori_loop(jnp.where(low, 1, 0), seq, one, 0)

    def return_finish():
        wait_all_seq(return_recv, side_recv_sem.at[19])
        tiles = [
            jnp.concatenate([return_recv[t], return_recv[8 + t]], axis=0) for t in range(8)
        ]
        for line, tile in enumerate(block_transpose(tiles)):
            stage[jnp.where(low, line, 7 - line)] = jnp.where(low, tile, mirror_rows(tile))
        for part in range(2):
            for tile in range(2):
                for line in range(8):
                    filter_grad[part, line, :, 128 * tile : 128 * (tile + 1)] = stage[
                        line, 8 * tile + 4 * part : 8 * tile + 4 * part + 4, :
                    ]

    def exchange(src, dst, way, chunk):
        def one(k, _):
            peer = lax.rem(me + k, seq)
            pltpu.make_async_remote_copy(
                src_ref=src(peer),
                dst_ref=dst,
                send_sem=send_sem.at[way],
                recv_sem=recv_sem.at[way, chunk],
                device_id={"seq": peer},
                device_id_type=pl.DeviceIdType.MESH,
            ).start()
            return 0

        lax.fori_loop(1, seq, one, 0)

    def turn(x, way, chunk):
        for j in range(chunk * CHUNK, (chunk + 1) * CHUNK):
            send_in[way, j] = x(j).T.reshape(seq, feats, F2)

    def send_positions(way, chunk):
        part = pl.ds(chunk * CHUNK, CHUNK)
        recv_in[way, me, part] = send_in[way, part, me]
        exchange(
            lambda peer: send_in.at[way, part, peer], recv_in.at[way, me, part], 2 * way, chunk
        )

    def send_features(way, chunk):
        part = pl.ds(chunk * CHUNK, CHUNK)
        recv_out[way, part, me] = send_out[way, me, part]
        exchange(
            lambda peer: send_out.at[way, peer, part], recv_out.at[way, part, me], 2 * way + 1, chunk
        )

    def wait_chunk(way, chunk):
        wait_bytes(
            send_in.at[0, pl.ds(0, CHUNK), pl.ds(0, seq - 1)], recv_sem.at[way, chunk]
        )

    def forward(way, spectrum, spectrum_mid):
        tiles = recv_in[way].reshape(F1 // 2, 2, feats, F2)
        mid = jnp.sum(
            tiles[:, 0].astype(jnp.float32) - tiles[:, 1].astype(jnp.float32), axis=0
        )
        field[...] = recv_in[way].reshape(F1 * feats, F2).astype(jnp.float32)
        cos, sin = twiddle[0], twiddle[1]

        def step(group, _):
            base = group * 4
            halves = []
            for sub in range(2):
                pair = [
                    field[pl.ds(base + 2 * sub + i, F1, stride=feats), :] for i in range(2)
                ]
                two = jnp.concatenate(pair, axis=1).astype(jnp.bfloat16)
                both = dot(whole(outer_fwd), two)
                for i in range(2):
                    real = both[:LINES, i * F2 : (i + 1) * F2]
                    imag = both[LINES:, i * F2 : (i + 1) * F2]
                    halves.append(
                        jnp.concatenate(
                            [real * cos + imag * sin, imag * cos - real * sin], axis=1
                        ).astype(jnp.bfloat16)
                    )
            where = pl.ds(pl.multiple_of(base * LINES, 4 * LINES), 4 * LINES)
            spectrum[where, :] = dot(jnp.concatenate(halves, axis=0), whole(inner_fwd)).astype(
                jnp.bfloat16
            )
            return 0

        lax.fori_loop(0, feats // 4, step, 0)
        cos_mid, sin_mid = twiddle_mid[0], twiddle_mid[1]
        half = jnp.concatenate([mid * cos_mid, -mid * sin_mid], axis=1).astype(jnp.bfloat16)
        spectrum_mid[...] = dot(half, whole(inner_fwd)).astype(jnp.bfloat16)

    def backward(way, product, product_mid):
        cos, sin = twiddle[0], twiddle[1]

        def step(group, _):
            base = group * 4
            where = pl.ds(pl.multiple_of(base * LINES, 4 * LINES), 4 * LINES)
            half = dot(product(where), whole(inner_inv))
            for sub in range(2):
                columns = []
                for i in range(2):
                    part = half[(2 * sub + i) * LINES : (2 * sub + i + 1) * LINES]
                    real, imag = part[:, :F2], part[:, F2:]
                    columns.append(
                        jnp.concatenate(
                            [real * cos - imag * sin, imag * cos + real * sin], axis=0
                        ).astype(jnp.bfloat16)
                    )
                result = dot(whole(outer_inv), jnp.concatenate(columns, axis=1)) * inv_length
                for i in range(2):
                    field[pl.ds(base + 2 * sub + i, F1, stride=feats), :] = result[
                        :, i * F2 : (i + 1) * F2
                    ]
            return 0

        lax.fori_loop(0, feats // 4, step, 0)
        half = dot(product_mid(), whole(inner_inv))
        last = (half[:, :F2] * twiddle_mid[0] - half[:, F2:] * twiddle_mid[1]).astype(jnp.bfloat16)
        last = last.astype(jnp.float32) * inv_length
        both = field[...].reshape(F1 // 2, 2, feats, F2)
        sign = jnp.where(lax.broadcasted_iota(jnp.int32, both.shape, 1) == 0, 1.0, -1.0)
        both = both + sign * last[None, None]
        send_out[way] = both.astype(jnp.bfloat16).reshape(seq, rows, feats, F2)

    def split(z):
        return z[:, :F2].astype(jnp.float32), z[:, F2:].astype(jnp.float32)

    def times(z, f):
        zr, zi = split(z)
        fr, fi = split(f)
        return jnp.concatenate([zr * fr - zi * fi, zr * fi + zi * fr], axis=1).astype(jnp.bfloat16)

    def times_conj(z, f):
        zr, zi = split(z)
        fr, fi = split(f)
        return jnp.concatenate([fr * zr + fi * zi, fr * zi - fi * zr], axis=1)

    loads["filter"].wait()
    scatter_prepare()
    loads["history"].wait()
    for chunk in range(chunks):
        turn(lambda j: history[pl.ds(j * F2, F2), :], 0, chunk)
    pl.semaphore_wait(barrier, 2 * seq - 1 + 5)
    scatter_start()
    for chunk in range(chunks):
        send_positions(0, chunk)
    gather()
    for name in ("outer_fwd", "twiddle", "twiddle_mid", "inner_fwd", "inner_inv", "outer_inv"):
        loads[name].wait()
    for chunk in range(chunks):
        wait_chunk(0, chunk)
    forward(0, spec, spec_mid)
    backward(
        0,
        lambda where: times(spec[where, :], filt[where, :]),
        lambda: times(spec_mid[...], filt_mid[...]),
    )
    for chunk in range(chunks):
        send_features(0, chunk)

    for name in ("gain_first", "bias_first", "w_in", "w_out", "gain_second", "cotangent"):
        loads[name].wait()
    for chunk in range(chunks):
        wait_chunk(1, chunk)
        for j in range(chunk * CHUNK, (chunk + 1) * CHUNK):
            mixed = recv_out[0, j].reshape(seq * feats, F2).T.astype(jnp.float32)
            part = pl.ds(j * F2, F2)
            grad_rows[part, :] = local_rows(
                mixed,
                history[part, :],
                cotangent[part, :],
                gain_first[...],
                bias_first[...],
                w_in[...],
                w_out[...],
                gain_second[...],
            )
        turn(lambda j: grad_rows[pl.ds(j * F2, F2), :].astype(jnp.bfloat16), 1, chunk)
        send_positions(1, chunk)

    for chunk in range(chunks):
        wait_chunk(2, chunk)
    forward(1, back_spec, back_mid)
    reduce_start()
    backward(
        1,
        lambda where: times_conj(back_spec[where, :], filt[where, :]).astype(jnp.bfloat16),
        lambda: times_conj(back_mid[...], filt_mid[...]).astype(jnp.bfloat16),
    )
    reduce_x()
    for chunk in range(chunks):
        send_features(1, chunk)
    reduce_x_second()
    reduce_z()
    reduce_z_second()
    return_grad()
    for chunk in range(chunks):
        wait_chunk(3, chunk)
        for j in range(chunk * CHUNK, (chunk + 1) * CHUNK):
            back = recv_out[1, j].reshape(seq * feats, F2).T.astype(jnp.float32)
            part = pl.ds(j * F2, F2)
            out[part, :] = (grad_rows[part, :] + back).astype(jnp.bfloat16)
        part = pl.ds(chunk * CHUNK * F2, CHUNK * F2)
        pltpu.make_async_copy(out.at[part], out_hbm.at[part], store_sem.at[0]).start()
    return_finish()
    store = pltpu.make_async_copy(filter_grad, filter_grad_hbm, store_sem.at[1])
    store.start()

    wait_all_seq(scatter_send, side_send_sem.at[0])
    for way, ref in sizes.items():
        wait_bytes(ref, side_send_sem.at[way])
    wait_all_seq(return_send, side_send_sem.at[19])
    sent = send_in.at[0, :, pl.ds(0, seq - 1)]
    for way in range(4):
        wait_bytes(sent, send_sem.at[way])
    pltpu.make_async_copy(out, out_hbm, store_sem.at[0]).wait()
    store.wait()


def local(history, cotangent, filter_weight, gain_first, bias_first, w_in, w_out, gain_second):
    user_count, row_count, features = history.shape
    seq = lax.axis_size("seq")
    feats = features // seq
    rows = F1 // seq
    bf16, f32 = jnp.bfloat16, jnp.float32
    tables = [jnp.asarray(t) for t in host_tables()]

    batch = lax.axis_size("batch")
    dma = pltpu.SemaphoreType.DMA
    operands = (
        history.reshape(row_count, features),
        cotangent.reshape(row_count, features),
        filter_weight,
        gain_first.reshape(1, features),
        bias_first.reshape(1, features),
        w_in,
        w_out,
        gain_second.reshape(1, features),
        *tables,
    )
    out, filter_grad = pl.pallas_call(
        functools.partial(kernel, seq, batch),
        out_shape=(
            jax.ShapeDtypeStruct((row_count, features), bf16),
            jax.ShapeDtypeStruct(filter_weight.shape, f32),
        ),
        in_specs=[pl.BlockSpec(memory_space=pltpu.HBM)] * len(operands),
        out_specs=(pl.BlockSpec(memory_space=pltpu.HBM),) * 2,
        scratch_shapes=[
            *[pltpu.VMEM(x.shape, x.dtype) for x in operands],
            pltpu.VMEM((row_count, features), bf16),
            pltpu.VMEM(filter_weight.shape, f32),
            pltpu.VMEM((2, rows, seq, feats, F2), bf16),
            pltpu.VMEM((2, seq, rows, feats, F2), bf16),
            pltpu.VMEM((2, seq, rows, feats, F2), bf16),
            pltpu.VMEM((2, rows, seq, feats, F2), bf16),
            pltpu.VMEM((feats * LINES, 2 * F2), bf16),
            pltpu.VMEM((feats, 2 * F2), bf16),
            pltpu.VMEM((feats * LINES, 2 * F2), bf16),
            pltpu.VMEM((feats, 2 * F2), bf16),
            pltpu.VMEM((feats * LINES, 2 * F2), bf16),
            pltpu.VMEM((feats, 2 * F2), bf16),
            pltpu.VMEM((F1 * feats, F2), f32),
            pltpu.VMEM((2 * LINES * feats, F2), f32),
            pltpu.VMEM((row_count, features), f32),
            pltpu.VMEM((8, 16, 128), f32),
            pltpu.VMEM((seq, 8, 128), f32),
            pltpu.VMEM((seq, 8, 128), f32),
            pltpu.VMEM((ZS, XS, CORES, 5, 16, 128), bf16),
            pltpu.VMEM((ZS, XS, CORES, 5, 16, 128), bf16),
            pltpu.VMEM((ZS, XS, 5, 16, 128), bf16),
            pltpu.VMEM((XS, ZS, 5, 16, 128), bf16),
            pltpu.VMEM((2, 2, 5, 16, 128), bf16),
            pltpu.VMEM((2, ZS, 5, 16, 128), bf16),
            pltpu.VMEM((ZS, 5, 16, 128), bf16),
            pltpu.VMEM((3, 16, 128), bf16),
            pltpu.VMEM((2, 16, 128), bf16),
            pltpu.VMEM((2, 5, 16, 128), bf16),
            pltpu.VMEM((seq, 8, 128), f32),
            pltpu.VMEM((seq, 8, 128), f32),
            dma((len(operands),)),
            dma((2,)),
            dma((4,)),
            dma((4, rows // CHUNK)),
            dma((20,)),
            dma((20,)),
        ],
        compiler_params=pltpu.CompilerParams(
            collective_id=0, has_side_effects=True, vmem_limit_bytes=60 * 2**20
        ),
    )(*operands)
    return (out.reshape(user_count, row_count, features), filter_grad)


def solution(mesh):
    placed = (
        P("batch", "seq", None),
        P("batch", "seq", None),
        P(None, "seq", "batch", None),
        P(),
        P(),
        P(),
        P(),
        P(),
    )
    return jax.shard_map(
        local,
        mesh=mesh,
        in_specs=placed,
        out_specs=(P("batch", "seq", None), P(None, "seq", "batch", None)),
        check_vma=False,
    )
```

```python
import functools
import math

import jax
import jax.numpy as jnp
import ml_dtypes
import numpy as np
from jax import lax
from jax.experimental import pallas as pl
from jax.experimental.pallas import tpu as pltpu
from jax.sharding import PartitionSpec as P

F1 = 128
F2 = 128
LINES = 64
CHUNK = 2
ZS, XS, CORES = 4, 4, 2

epsilon = 1e-05
inv_root_two = 1.0 / math.sqrt(2.0)
inv_root_tau = 1.0 / math.sqrt(2.0 * math.pi)
inv_length = 1.0 / (F1 * F2)


def columns(table):
    blocks = np.split(table, table.shape[1] // 128, axis=1)
    return np.stack(blocks).astype(ml_dtypes.bfloat16)


def whole(table):
    return jnp.concatenate([table[k] for k in range(table.shape[0])], axis=1)


def host_tables():
    index = np.arange(F1)
    angle = 2.0 * np.pi * (index[:, None] * index[None, :] % F1) / F1
    cos, sin = np.cos(angle), np.sin(angle)
    outer_fwd = np.concatenate([cos[:LINES], -sin[:LINES]], axis=0)
    outer_inv = np.concatenate([cos[:LINES], -sin[:LINES]], axis=0).T
    inner_fwd = np.block([[cos, -sin], [sin, cos]])
    inner_inv = np.block([[cos, sin], [-sin, cos]])
    lines = np.arange(LINES + 1)
    phase = 2.0 * np.pi * (lines[:, None] * index[None, :]) / (F1 * F2)
    narrow = [columns(t) for t in (outer_fwd, outer_inv, inner_fwd, inner_inv)]
    twiddles = np.stack([np.cos(phase), np.sin(phase)]).astype(np.float32)
    return (*narrow, twiddles[:, :LINES], twiddles[:, LINES:], *permutations())


def permutations():
    spread = np.zeros((2, 2 * F2, 4 * F2), np.float32)
    collect = np.zeros((2 * F2, 2 * F2), np.float32)
    for part in range(2):
        for q in range(F2):
            for h in range(2):
                spread[h, part * F2 + q, (q // 4) * 16 + h * 8 + part * 4 + q % 4] = 1.0
            collect[(q // 4) * 8 + part * 4 + q % 4, part * F2 + q] = 1.0
    return columns(spread.reshape(4 * F2, 4 * F2)), columns(collect)


def dot(a, b):
    return jnp.dot(a, b, preferred_element_type=jnp.float32)


def dot_nt(a, b):
    return lax.dot_general(a, b, (((1,), (1,)), ((), ())), preferred_element_type=jnp.float32)


def mirror_rows(x):
    axis = x.ndim - 2
    size = x.shape[axis]
    row = lax.broadcasted_iota(jnp.int32, x.shape, axis)
    for step in (1, 2):
        up, down = pltpu.roll(x, step, axis), pltpu.roll(x, size - step, axis)
        x = jnp.where((row & step) != 0, up, down)
    return jnp.where((row & 4) != 0, -x, x)


def block_transpose(tiles):
    lane = lax.broadcasted_iota(jnp.int32, tiles[0].shape, 1) // 16
    result = []
    for to in range(8):
        total = tiles[to]
        for block in range(8):
            if block != to:
                moved = pltpu.roll(tiles[block], 16 * ((block - to) % 8), 1)
                total = jnp.where(lane == block, moved, total)
        result.append(total)
    return result


def mean(x):
    return jnp.mean(x, axis=-1, keepdims=True)


def local_rows(mixed, history, cot, gain_first, bias_first, w_in, w_out, gain_second):
    summed = mixed + history.astype(jnp.float32)
    center_one = summed - mean(summed)
    inv_one = lax.rsqrt(mean(center_one * center_one) + epsilon)
    norm_one = center_one * inv_one
    hidden = (norm_one * gain_first + bias_first).astype(jnp.bfloat16)
    preact = dot(hidden, w_in)
    cumul = 0.5 * (1.0 + lax.erf(preact * inv_root_two))
    activation = (preact * cumul).astype(jnp.bfloat16)
    output_sum = dot(activation, w_out) + hidden.astype(jnp.float32)
    center_two = output_sum - mean(output_sum)
    inv_two = lax.rsqrt(mean(center_two * center_two) + epsilon)
    norm_two = center_two * inv_two
    grad_norm = cot.astype(jnp.float32) * gain_second
    grad_sum = inv_two * (grad_norm - mean(grad_norm) - norm_two * mean(grad_norm * norm_two))
    grad_act = dot_nt(grad_sum.astype(jnp.bfloat16), w_out)
    density = jnp.exp(-0.5 * preact * preact) * inv_root_tau
    grad_pre = (grad_act * (cumul + preact * density)).astype(jnp.bfloat16)
    grad_hidden = dot_nt(grad_pre, w_in) + grad_sum
    grad_scaled = grad_hidden * gain_first
    return inv_one * (grad_scaled - mean(grad_scaled) - norm_one * mean(grad_scaled * norm_one))


def kernel(
    seq,
    batch,
    history_hbm,
    cotangent_hbm,
    filter_weight_hbm,
    gain_first_hbm,
    bias_first_hbm,
    w_in_hbm,
    w_out_hbm,
    gain_second_hbm,
    outer_fwd_hbm,
    outer_inv_hbm,
    inner_fwd_hbm,
    inner_inv_hbm,
    twiddle_hbm,
    twiddle_mid_hbm,
    spread_hbm,
    collect_hbm,
    out_hbm,
    filter_grad_hbm,
    history,
    cotangent,
    filter_weight,
    gain_first,
    bias_first,
    w_in,
    w_out,
    gain_second,
    outer_fwd,
    outer_inv,
    inner_fwd,
    inner_inv,
    twiddle,
    twiddle_mid,
    spread,
    collect,
    out,
    filter_grad,
    send_in,
    send_out,
    recv_in,
    recv_out,
    spec,
    spec_mid,
    back_spec,
    back_mid,
    filt,
    filt_mid,
    field,
    grad_field,
    grad_rows,
    stage,
    scatter_send,
    scatter_recv,
    gathered,
    core_send,
    core_recv,
    x_send,
    x_half,
    x_recv,
    z_send,
    z_recv,
    return_send,
    return_recv,
    load_sem,
    store_sem,
    send_sem,
    recv_sem,
    side_send_sem,
    side_recv_sem,
):
    me = lax.axis_index("seq")
    mine = lax.axis_index("batch")
    rows = F1 // seq
    feats = history.shape[1] // seq
    chunks = rows // CHUNK
    core = lax.rem(mine, CORES)
    along_x = lax.rem(mine // CORES, XS)
    along_z = mine // (CORES * XS)
    opposite = batch - 1 - mine
    low = me < seq // 2

    def batch_index(z, x, c):
        return (z * XS + x) * CORES + c

    x_right, x_left, x_far = (lax.rem(along_x + k, XS) for k in (1, XS - 1, 2))
    to_x_right = {"batch": batch_index(along_z, x_right, core)}
    to_x_left = {"batch": batch_index(along_z, x_left, core)}
    x_peers = [lax.rem(along_x + k, XS) for k in range(1, XS)]
    z_peers = [lax.rem(along_z + k, ZS) for k in range(1, ZS)]
    to_x = [{"batch": batch_index(along_z, x, core)} for x in x_peers]
    to_z = [{"batch": batch_index(z, along_x, core)} for z in z_peers]
    to_core = {"batch": batch_index(along_z, along_x, 1 - core)}

    loads = {}
    for name, source, target in (
        ("filter", filter_weight_hbm, filter_weight),
        ("history", history_hbm, history),
        ("outer_fwd", outer_fwd_hbm, outer_fwd),
        ("twiddle", twiddle_hbm, twiddle),
        ("twiddle_mid", twiddle_mid_hbm, twiddle_mid),
        ("inner_fwd", inner_fwd_hbm, inner_fwd),
        ("spread", spread_hbm, spread),
        ("inner_inv", inner_inv_hbm, inner_inv),
        ("outer_inv", outer_inv_hbm, outer_inv),
        ("gain_first", gain_first_hbm, gain_first),
        ("bias_first", bias_first_hbm, bias_first),
        ("w_in", w_in_hbm, w_in),
        ("w_out", w_out_hbm, w_out),
        ("gain_second", gain_second_hbm, gain_second),
        ("cotangent", cotangent_hbm, cotangent),
        ("collect", collect_hbm, collect),
    ):
        loads[name] = pltpu.make_async_copy(source, target, load_sem.at[len(loads)])
        loads[name].start()

    barrier = pltpu.get_barrier_semaphore()

    def greet(peer):
        pl.semaphore_signal(
            barrier, inc=1, device_id=peer, device_id_type=pl.DeviceIdType.MESH
        )

    def greet_seq(k, _):
        greet({"seq": lax.rem(me + k, seq)})
        return 0

    def greet_opposite(k, _):
        greet({"seq": k, "batch": opposite})
        return 0

    lax.fori_loop(0, seq, greet_opposite, 0)
    for peer in (*to_z, *to_x, to_core):
        greet(peer)
    lax.fori_loop(1, seq, greet_seq, 0)

    def side_copy(src, dst, way, peer):
        pltpu.make_async_remote_copy(
            src_ref=src,
            dst_ref=dst,
            send_sem=side_send_sem.at[way],
            recv_sem=side_recv_sem.at[way],
            device_id=peer,
            device_id_type=pl.DeviceIdType.MESH,
        ).start()

    def wait_bytes(ref, sem):
        pltpu.make_async_copy(ref, ref, sem).wait()

    def wait_all_seq(ref, sem):
        @pl.when(low)
        def _():
            wait_bytes(ref.at[pl.ds(0, seq - 1)], sem)

        @pl.when(jnp.logical_not(low))
        def _():
            wait_bytes(ref, sem)

    sizes = {
        1: gathered.at[0, 0, 0],
        2: gathered.at[0, 0, 0],
        3: gathered.at[0, 0, 0],
        4: gathered.at[:, pl.ds(0, XS - 1), 0],
        9: gathered.at[:, :, 0],
        10: core_recv,
        11: x_half.at[0],
        12: x_half.at[0],
        13: x_recv.at[0],
        14: x_recv.at[0],
        15: z_recv,
    }

    def arrived(*ways):
        for way in ways:
            wait_bytes(sizes[way], side_recv_sem.at[way])

    def scatter_prepare():
        for part in range(2):
            for tile in range(2):
                for line in range(8):
                    stage[line, 8 * tile + 4 * part : 8 * tile + 4 * part + 4, :] = filter_weight[
                        part, line, :, 128 * tile : 128 * (tile + 1)
                    ].astype(jnp.float32)
        tiles = []
        for line in range(8):
            tile = stage[jnp.where(low, line, 7 - line)]
            tiles.append(jnp.where(low, tile, mirror_rows(tile)))
        for to, tile in enumerate(block_transpose(tiles)):
            scatter_send[to] = tile[:8]
            scatter_send[8 + to] = tile[8:]

    def scatter_start():
        target = jnp.where(low, mine, opposite)

        def one(k, _):
            peer = lax.rem(me + k, seq)
            side_copy(
                scatter_send.at[peer], scatter_recv.at[me], 0, {"seq": peer, "batch": target}
            )
            return 0

        @pl.when(low)
        def _():
            scatter_recv[me] = scatter_send[me]

        lax.fori_loop(jnp.where(low, 1, 0), seq, one, 0)

    def gather_start():
        wait_all_seq(scatter_recv, side_recv_sem.at[0])
        lane = lax.broadcasted_iota(jnp.int32, (8, 128), 1)
        zeros = jnp.zeros((8, 128), jnp.float32)
        moved = [pltpu.roll(scatter_recv[seq - 1 - t], 16, 1) for t in range(8)]
        tiles = []
        for t in range(9):
            before = moved[t - 1] if t > 0 else zeros
            after = moved[t] if t < 8 else zeros
            tile = jnp.where(lane < 16, before, after)
            tiles.append(tile + scatter_recv[t] if t < 8 else tile)
        for t in range(5):
            upper = tiles[t] if t < 4 else tiles[8]
            lower = tiles[4 + t] if t < 4 else zeros
            gathered[along_z, along_x, core, t] = jnp.concatenate([upper, lower], axis=0).astype(
                jnp.bfloat16
            )
        own = gathered.at[along_z, along_x, core]
        for k, peer in enumerate(to_z):
            side_copy(own, own, 1 + k, peer)
        gather_forward(along_z)

    def gather_forward(z):
        for peer in to_x:
            block = gathered.at[z, along_x, core]
            side_copy(block, block, 4, peer)

    def gather_z(k):
        arrived(1 + k)
        gather_forward(lax.rem(along_z + ZS - 1 - k, ZS))

    def gather_core():
        arrived(4)
        block = gathered.at[:, :, core]
        side_copy(block, block, 9, to_core)

    def gather_finish():
        arrived(9)
        loads["spread"].wait()
        parts = [gathered[:, :, :, t].reshape(batch * 16, 128) for t in range(5)]
        block = jnp.concatenate(parts[:4], axis=1)
        for h in range(2):
            table = jnp.concatenate(
                [spread[k, 2 * F2 * h : 2 * F2 * (h + 1)] for k in range(4)], axis=1
            )
            result = dot(table, block).astype(jnp.bfloat16).T.astype(jnp.float32)
            field[512 * h : 512 * (h + 1), :] = result[:, :F2]
            field[1024 + 512 * h : 1024 + 512 * (h + 1), :] = result[:, F2:]
        table = jnp.concatenate([spread[k, : 2 * F2] for k in range(4)], axis=1)
        filt_mid[...] = dot(table, parts[4]).astype(jnp.bfloat16).T[:feats]
        for d in range(feats):
            real = field[pl.ds(d, LINES, stride=feats), :]
            imag = field[pl.ds(1024 + d, LINES, stride=feats), :]
            filt[d * LINES : (d + 1) * LINES, :] = jnp.concatenate([real, imag], axis=1).astype(
                jnp.bfloat16
            )

    def reduce_start():
        for d in range(feats):
            where = pl.ds(d * LINES, LINES)
            term = times_conj(back_spec[where, :], spec[where, :]) * inv_length
            grad_field[pl.ds(d, LINES, stride=feats), :] = term[:, :F2]
            grad_field[pl.ds(1024 + d, LINES, stride=feats), :] = term[:, F2:]
        loads["collect"].wait()
        parts = []
        for h in range(2):
            real = grad_field[512 * h : 512 * (h + 1), :]
            imag = grad_field[1024 + 512 * h : 1024 + 512 * (h + 1), :]
            both = jnp.concatenate([real, imag], axis=1).astype(jnp.bfloat16)
            parts.append(dot_nt(whole(collect), both).reshape(batch, 8, 512))
        mid = jnp.concatenate(
            [
                times_conj(back_mid[...], spec_mid[...]) * inv_length,
                jnp.zeros((128 - feats, 2 * F2), jnp.float32),
            ],
            axis=0,
        ).astype(jnp.bfloat16)
        last = dot_nt(whole(collect), mid).reshape(batch, 8, 128)
        both = jnp.concatenate(parts, axis=1).astype(jnp.bfloat16)
        both = both.reshape(ZS, XS, CORES, 16, 512)
        for t in range(4):
            core_send[:, :, :, t] = both[..., 128 * t : 128 * (t + 1)]
        last = jnp.concatenate([last, jnp.zeros_like(last)], axis=1).astype(jnp.bfloat16)
        core_send[:, :, :, 4] = last.reshape(ZS, XS, CORES, 16, 128)
        side_copy(core_send.at[:, :, 1 - core], core_recv, 10, to_core)

    def add(a, b):
        return (a.astype(jnp.float32) + b.astype(jnp.float32)).astype(jnp.bfloat16)

    def reduce_x():
        arrived(10)
        for x in range(XS):
            x_send[x] = add(core_send[:, x, core], core_recv[:, x])
        side_copy(x_send.at[x_far, pl.ds(0, 2)], x_half.at[0], 11, to_x_right)
        side_copy(x_send.at[x_far, pl.ds(2, 2)], x_half.at[1], 12, to_x_left)

    def reduce_x_second():
        arrived(11)
        x_send[x_right, 0:2] = add(x_send[x_right, 0:2], x_half[0])
        side_copy(x_send.at[x_right], x_recv.at[0], 13, to_x_right)
        arrived(12)
        x_send[x_left, 2:4] = add(x_send[x_left, 2:4], x_half[1])
        side_copy(x_send.at[x_left], x_recv.at[1], 14, to_x_left)

    def reduce_z():
        arrived(13, 14)
        total = x_send[along_x].astype(jnp.float32) + x_recv[0].astype(jnp.float32)
        z_send[...] = (total + x_recv[1].astype(jnp.float32)).astype(jnp.bfloat16)
        for k, peer in enumerate(to_z):
            side_copy(z_send.at[z_peers[k]], z_recv.at[k], 15, peer)

    def return_grad():
        arrived(15)
        total = z_send[along_z].astype(jnp.float32)
        for k in range(ZS - 1):
            total = total + z_recv[k].astype(jnp.float32)
        tiles = [total[t, :8] for t in range(4)] + [total[t, 8:] for t in range(4)]
        tiles.append(total[4, :8])
        lane = lax.broadcasted_iota(jnp.int32, (8, 128), 1)
        moved = [pltpu.roll(t, 112, 1) for t in tiles]
        for t in range(8):
            return_send[t] = tiles[t]
            return_send[seq - 1 - t] = jnp.where(lane < 112, moved[t], moved[t + 1])

        def one(k, _):
            peer = lax.rem(me + k, seq)
            target = jnp.where(peer < seq // 2, mine, opposite)
            side_copy(
                return_send.at[peer], return_recv.at[me], 19, {"seq": peer, "batch": target}
            )
            return 0

        @pl.when(low)
        def _():
            return_recv[me] = return_send[me]

        lax.fori_loop(jnp.where(low, 1, 0), seq, one, 0)

    def return_finish():
        wait_all_seq(return_recv, side_recv_sem.at[19])
        tiles = [
            jnp.concatenate([return_recv[t], return_recv[8 + t]], axis=0) for t in range(8)
        ]
        for line, tile in enumerate(block_transpose(tiles)):
            stage[jnp.where(low, line, 7 - line)] = jnp.where(low, tile, mirror_rows(tile))
        for part in range(2):
            for tile in range(2):
                for line in range(8):
                    filter_grad[part, line, :, 128 * tile : 128 * (tile + 1)] = stage[
                        line, 8 * tile + 4 * part : 8 * tile + 4 * part + 4, :
                    ]

    def exchange(src, dst, way, chunk):
        def one(k, _):
            peer = lax.rem(me + k, seq)
            pltpu.make_async_remote_copy(
                src_ref=src(peer),
                dst_ref=dst,
                send_sem=send_sem.at[way],
                recv_sem=recv_sem.at[way, chunk],
                device_id={"seq": peer},
                device_id_type=pl.DeviceIdType.MESH,
            ).start()
            return 0

        lax.fori_loop(1, seq, one, 0)

    def turn(x, way, chunk):
        for j in range(chunk * CHUNK, (chunk + 1) * CHUNK):
            send_in[way, j] = x(j).T.reshape(seq, feats, F2)

    def send_positions(way, chunk):
        part = pl.ds(chunk * CHUNK, CHUNK)
        recv_in[way, me, part] = send_in[way, part, me]
        exchange(
            lambda peer: send_in.at[way, part, peer], recv_in.at[way, me, part], 2 * way, chunk
        )

    def send_features(way, chunk):
        part = pl.ds(chunk * CHUNK, CHUNK)
        recv_out[way, part, me] = send_out[way, me, part]
        exchange(
            lambda peer: send_out.at[way, peer, part], recv_out.at[way, part, me], 2 * way + 1, chunk
        )

    def wait_chunk(way, chunk):
        wait_bytes(
            send_in.at[0, pl.ds(0, CHUNK), pl.ds(0, seq - 1)], recv_sem.at[way, chunk]
        )

    def forward(way, spectrum, spectrum_mid):
        tiles = recv_in[way].reshape(F1 // 2, 2, feats, F2)
        mid = jnp.sum(
            tiles[:, 0].astype(jnp.float32) - tiles[:, 1].astype(jnp.float32), axis=0
        )
        field[...] = recv_in[way].reshape(F1 * feats, F2).astype(jnp.float32)
        cos, sin = twiddle[0], twiddle[1]

        def step(group, _):
            base = group * 4
            halves = []
            for sub in range(2):
                pair = [
                    field[pl.ds(base + 2 * sub + i, F1, stride=feats), :] for i in range(2)
                ]
                two = jnp.concatenate(pair, axis=1).astype(jnp.bfloat16)
                both = dot(whole(outer_fwd), two)
                for i in range(2):
                    real = both[:LINES, i * F2 : (i + 1) * F2]
                    imag = both[LINES:, i * F2 : (i + 1) * F2]
                    halves.append(
                        jnp.concatenate(
                            [real * cos + imag * sin, imag * cos - real * sin], axis=1
                        ).astype(jnp.bfloat16)
                    )
            where = pl.ds(pl.multiple_of(base * LINES, 4 * LINES), 4 * LINES)
            spectrum[where, :] = dot(jnp.concatenate(halves, axis=0), whole(inner_fwd)).astype(
                jnp.bfloat16
            )
            return 0

        lax.fori_loop(0, feats // 4, step, 0, unroll=True)
        cos_mid, sin_mid = twiddle_mid[0], twiddle_mid[1]
        half = jnp.concatenate([mid * cos_mid, -mid * sin_mid], axis=1).astype(jnp.bfloat16)
        spectrum_mid[...] = dot(half, whole(inner_fwd)).astype(jnp.bfloat16)

    def backward(way, product, product_mid):
        cos, sin = twiddle[0], twiddle[1]

        def step(group, _):
            base = group * 4
            where = pl.ds(pl.multiple_of(base * LINES, 4 * LINES), 4 * LINES)
            half = dot(product(where), whole(inner_inv))
            for sub in range(2):
                columns = []
                for i in range(2):
                    part = half[(2 * sub + i) * LINES : (2 * sub + i + 1) * LINES]
                    real, imag = part[:, :F2], part[:, F2:]
                    columns.append(
                        jnp.concatenate(
                            [real * cos - imag * sin, imag * cos + real * sin], axis=0
                        ).astype(jnp.bfloat16)
                    )
                result = dot(whole(outer_inv), jnp.concatenate(columns, axis=1)) * inv_length
                for i in range(2):
                    field[pl.ds(base + 2 * sub + i, F1, stride=feats), :] = result[
                        :, i * F2 : (i + 1) * F2
                    ]
            return 0

        lax.fori_loop(0, feats // 4, step, 0, unroll=True)
        half = dot(product_mid(), whole(inner_inv))
        last = (half[:, :F2] * twiddle_mid[0] - half[:, F2:] * twiddle_mid[1]).astype(jnp.bfloat16)
        last = last.astype(jnp.float32) * inv_length
        both = field[...].reshape(F1 // 2, 2, feats, F2)
        sign = jnp.where(lax.broadcasted_iota(jnp.int32, both.shape, 1) == 0, 1.0, -1.0)
        both = both + sign * last[None, None]
        send_out[way] = both.astype(jnp.bfloat16).reshape(seq, rows, feats, F2)

    def split(z):
        return z[:, :F2].astype(jnp.float32), z[:, F2:].astype(jnp.float32)

    def times(z, f):
        zr, zi = split(z)
        fr, fi = split(f)
        return jnp.concatenate([zr * fr - zi * fi, zr * fi + zi * fr], axis=1).astype(jnp.bfloat16)

    def times_conj(z, f):
        zr, zi = split(z)
        fr, fi = split(f)
        return jnp.concatenate([fr * zr + fi * zi, fr * zi - fi * zr], axis=1)

    loads["filter"].wait()
    scatter_prepare()
    loads["history"].wait()
    for chunk in range(chunks):
        turn(lambda j: history[pl.ds(j * F2, F2), :], 0, chunk)
    pl.semaphore_wait(barrier, 2 * seq - 1 + ZS - 1 + XS - 1 + 1)
    scatter_start()
    for chunk in range(chunks // 2):
        send_positions(0, chunk)
    gather_start()
    gather_z(0)
    gather_z(2)
    for chunk in range(chunks // 2, chunks):
        send_positions(0, chunk)
    gather_z(1)
    for name in ("outer_fwd", "twiddle", "twiddle_mid", "inner_fwd", "inner_inv", "outer_inv"):
        loads[name].wait()
    for chunk in range(chunks):
        wait_chunk(0, chunk)
    forward(0, spec, spec_mid)
    gather_core()
    gather_finish()
    backward(
        0,
        lambda where: times(spec[where, :], filt[where, :]),
        lambda: times(spec_mid[...], filt_mid[...]),
    )
    for chunk in range(chunks):
        send_features(0, chunk)

    for name in ("gain_first", "bias_first", "w_in", "w_out", "gain_second", "cotangent"):
        loads[name].wait()
    for chunk in range(chunks):
        wait_chunk(1, chunk)
        for j in range(chunk * CHUNK, (chunk + 1) * CHUNK):
            mixed = recv_out[0, j].reshape(seq * feats, F2).T.astype(jnp.float32)
            part = pl.ds(j * F2, F2)
            grad_rows[part, :] = local_rows(
                mixed,
                history[part, :],
                cotangent[part, :],
                gain_first[...],
                bias_first[...],
                w_in[...],
                w_out[...],
                gain_second[...],
            )
        turn(lambda j: grad_rows[pl.ds(j * F2, F2), :].astype(jnp.bfloat16), 1, chunk)
        send_positions(1, chunk)

    for chunk in range(chunks):
        wait_chunk(2, chunk)
    forward(1, back_spec, back_mid)
    reduce_start()
    reduce_x()
    backward(
        1,
        lambda where: times_conj(back_spec[where, :], filt[where, :]).astype(jnp.bfloat16),
        lambda: times_conj(back_mid[...], filt_mid[...]).astype(jnp.bfloat16),
    )
    reduce_x_second()
    for chunk in range(chunks // 2):
        send_features(1, chunk)
    reduce_z()
    for chunk in range(chunks // 2, chunks):
        send_features(1, chunk)
    return_grad()
    for chunk in range(chunks):
        wait_chunk(3, chunk)
        for j in range(chunk * CHUNK, (chunk + 1) * CHUNK):
            back = recv_out[1, j].reshape(seq * feats, F2).T.astype(jnp.float32)
            part = pl.ds(j * F2, F2)
            out[part, :] = (grad_rows[part, :] + back).astype(jnp.bfloat16)
        part = pl.ds(chunk * CHUNK * F2, CHUNK * F2)
        pltpu.make_async_copy(out.at[part], out_hbm.at[part], store_sem.at[0]).start()
    return_finish()
    store = pltpu.make_async_copy(filter_grad, filter_grad_hbm, store_sem.at[1])
    store.start()

    wait_all_seq(scatter_send, side_send_sem.at[0])
    for way, ref in sizes.items():
        wait_bytes(ref, side_send_sem.at[way])
    wait_all_seq(return_send, side_send_sem.at[19])
    sent = send_in.at[0, :, pl.ds(0, seq - 1)]
    for way in range(4):
        wait_bytes(sent, send_sem.at[way])
    pltpu.make_async_copy(out, out_hbm, store_sem.at[0]).wait()
    store.wait()


def local(history, cotangent, filter_weight, gain_first, bias_first, w_in, w_out, gain_second):
    user_count, row_count, features = history.shape
    seq = lax.axis_size("seq")
    feats = features // seq
    rows = F1 // seq
    bf16, f32 = jnp.bfloat16, jnp.float32
    tables = [jnp.asarray(t) for t in host_tables()]

    batch = lax.axis_size("batch")
    dma = pltpu.SemaphoreType.DMA
    operands = (
        history.reshape(row_count, features),
        cotangent.reshape(row_count, features),
        filter_weight,
        gain_first.reshape(1, features),
        bias_first.reshape(1, features),
        w_in,
        w_out,
        gain_second.reshape(1, features),
        *tables,
    )
    out, filter_grad = pl.pallas_call(
        functools.partial(kernel, seq, batch),
        out_shape=(
            jax.ShapeDtypeStruct((row_count, features), bf16),
            jax.ShapeDtypeStruct(filter_weight.shape, f32),
        ),
        in_specs=[pl.BlockSpec(memory_space=pltpu.HBM)] * len(operands),
        out_specs=(pl.BlockSpec(memory_space=pltpu.HBM),) * 2,
        scratch_shapes=[
            *[pltpu.VMEM(x.shape, x.dtype) for x in operands],
            pltpu.VMEM((row_count, features), bf16),
            pltpu.VMEM(filter_weight.shape, f32),
            pltpu.VMEM((2, rows, seq, feats, F2), bf16),
            pltpu.VMEM((2, seq, rows, feats, F2), bf16),
            pltpu.VMEM((2, seq, rows, feats, F2), bf16),
            pltpu.VMEM((2, rows, seq, feats, F2), bf16),
            pltpu.VMEM((feats * LINES, 2 * F2), bf16),
            pltpu.VMEM((feats, 2 * F2), bf16),
            pltpu.VMEM((feats * LINES, 2 * F2), bf16),
            pltpu.VMEM((feats, 2 * F2), bf16),
            pltpu.VMEM((feats * LINES, 2 * F2), bf16),
            pltpu.VMEM((feats, 2 * F2), bf16),
            pltpu.VMEM((F1 * feats, F2), f32),
            pltpu.VMEM((2 * LINES * feats, F2), f32),
            pltpu.VMEM((row_count, features), f32),
            pltpu.VMEM((8, 16, 128), f32),
            pltpu.VMEM((seq, 8, 128), f32),
            pltpu.VMEM((seq, 8, 128), f32),
            pltpu.VMEM((ZS, XS, CORES, 5, 16, 128), bf16),
            pltpu.VMEM((ZS, XS, CORES, 5, 16, 128), bf16),
            pltpu.VMEM((ZS, XS, 5, 16, 128), bf16),
            pltpu.VMEM((XS, ZS, 5, 16, 128), bf16),
            pltpu.VMEM((2, 2, 5, 16, 128), bf16),
            pltpu.VMEM((2, ZS, 5, 16, 128), bf16),
            pltpu.VMEM((ZS, 5, 16, 128), bf16),
            pltpu.VMEM((ZS - 1, 5, 16, 128), bf16),
            pltpu.VMEM((seq, 8, 128), f32),
            pltpu.VMEM((seq, 8, 128), f32),
            dma((len(operands),)),
            dma((2,)),
            dma((4,)),
            dma((4, rows // CHUNK)),
            dma((20,)),
            dma((20,)),
        ],
        compiler_params=pltpu.CompilerParams(
            collective_id=0, has_side_effects=True, vmem_limit_bytes=60 * 2**20
        ),
    )(*operands)
    return (out.reshape(user_count, row_count, features), filter_grad)


def solution(mesh):
    placed = (
        P("batch", "seq", None),
        P("batch", "seq", None),
        P(None, "seq", "batch", None),
        P(),
        P(),
        P(),
        P(),
        P(),
    )
    return jax.shard_map(
        local,
        mesh=mesh,
        in_specs=placed,
        out_specs=(P("batch", "seq", None), P(None, "seq", "batch", None)),
        check_vma=False,
    )
```

```python
import functools
import math

import jax
import jax.numpy as jnp
import ml_dtypes
import numpy as np
from jax import lax
from jax.experimental import pallas as pl
from jax.experimental.pallas import tpu as pltpu
from jax.sharding import PartitionSpec as P

F1 = 128
F2 = 128
LINES = 64
CHUNK = 2
ZS, XS, CORES = 4, 4, 2

epsilon = 1e-05
inv_root_two = 1.0 / math.sqrt(2.0)
inv_root_tau = 1.0 / math.sqrt(2.0 * math.pi)
inv_length = 1.0 / (F1 * F2)


def columns(table):
    blocks = np.split(table, table.shape[1] // 128, axis=1)
    return np.stack(blocks).astype(ml_dtypes.bfloat16)


def whole(table):
    return jnp.concatenate([table[k] for k in range(table.shape[0])], axis=1)


def host_tables():
    index = np.arange(F1)
    angle = 2.0 * np.pi * (index[:, None] * index[None, :] % F1) / F1
    cos, sin = np.cos(angle), np.sin(angle)
    outer_fwd = np.concatenate([cos[:LINES], -sin[:LINES]], axis=0)
    outer_inv = np.concatenate([cos[:LINES], -sin[:LINES]], axis=0).T
    inner_fwd = np.block([[cos, -sin], [sin, cos]])
    inner_inv = np.block([[cos, sin], [-sin, cos]])
    lines = np.arange(LINES + 1)
    phase = 2.0 * np.pi * (lines[:, None] * index[None, :]) / (F1 * F2)
    narrow = [columns(t) for t in (outer_fwd, outer_inv, inner_fwd, inner_inv)]
    twiddles = np.stack([np.cos(phase), np.sin(phase)]).astype(np.float32)
    return (*narrow, twiddles[:, :LINES], twiddles[:, LINES:], *permutations())


def permutations():
    spread = np.zeros((2, 2 * F2, 4 * F2), np.float32)
    collect = np.zeros((2 * F2, 2 * F2), np.float32)
    for part in range(2):
        for q in range(F2):
            for h in range(2):
                spread[h, part * F2 + q, (q // 4) * 16 + h * 8 + part * 4 + q % 4] = 1.0
            collect[(q // 4) * 8 + part * 4 + q % 4, part * F2 + q] = 1.0
    return columns(spread.reshape(4 * F2, 4 * F2)), columns(collect)


def dot(a, b):
    return jnp.dot(a, b, preferred_element_type=jnp.float32)


def dot_nt(a, b):
    return lax.dot_general(a, b, (((1,), (1,)), ((), ())), preferred_element_type=jnp.float32)


def mirror_rows(x):
    axis = x.ndim - 2
    size = x.shape[axis]
    row = lax.broadcasted_iota(jnp.int32, x.shape, axis)
    for step in (1, 2):
        up, down = pltpu.roll(x, step, axis), pltpu.roll(x, size - step, axis)
        x = jnp.where((row & step) != 0, up, down)
    return jnp.where((row & 4) != 0, -x, x)


def block_transpose(tiles):
    lane = lax.broadcasted_iota(jnp.int32, tiles[0].shape, 1) // 16
    result = []
    for to in range(8):
        total = tiles[to]
        for block in range(8):
            if block != to:
                moved = pltpu.roll(tiles[block], 16 * ((block - to) % 8), 1)
                total = jnp.where(lane == block, moved, total)
        result.append(total)
    return result


def mean(x):
    return jnp.mean(x, axis=-1, keepdims=True)


def local_rows(mixed, history, cot, gain_first, bias_first, w_in, w_out, gain_second):
    summed = mixed + history.astype(jnp.float32)
    center_one = summed - mean(summed)
    inv_one = lax.rsqrt(mean(center_one * center_one) + epsilon)
    norm_one = center_one * inv_one
    hidden = (norm_one * gain_first + bias_first).astype(jnp.bfloat16)
    preact = dot(hidden, w_in)
    cumul = 0.5 * (1.0 + lax.erf(preact * inv_root_two))
    activation = (preact * cumul).astype(jnp.bfloat16)
    output_sum = dot(activation, w_out) + hidden.astype(jnp.float32)
    center_two = output_sum - mean(output_sum)
    inv_two = lax.rsqrt(mean(center_two * center_two) + epsilon)
    norm_two = center_two * inv_two
    grad_norm = cot.astype(jnp.float32) * gain_second
    grad_sum = inv_two * (grad_norm - mean(grad_norm) - norm_two * mean(grad_norm * norm_two))
    grad_act = dot_nt(grad_sum.astype(jnp.bfloat16), w_out)
    density = jnp.exp(-0.5 * preact * preact) * inv_root_tau
    grad_pre = (grad_act * (cumul + preact * density)).astype(jnp.bfloat16)
    grad_hidden = dot_nt(grad_pre, w_in) + grad_sum
    grad_scaled = grad_hidden * gain_first
    return inv_one * (grad_scaled - mean(grad_scaled) - norm_one * mean(grad_scaled * norm_one))


def kernel(
    seq,
    batch,
    history_hbm,
    cotangent_hbm,
    filter_weight_hbm,
    gain_first_hbm,
    bias_first_hbm,
    w_in_hbm,
    w_out_hbm,
    gain_second_hbm,
    outer_fwd_hbm,
    outer_inv_hbm,
    inner_fwd_hbm,
    inner_inv_hbm,
    twiddle_hbm,
    twiddle_mid_hbm,
    spread_hbm,
    collect_hbm,
    out_hbm,
    filter_grad_hbm,
    history,
    cotangent,
    filter_weight,
    gain_first,
    bias_first,
    w_in,
    w_out,
    gain_second,
    outer_fwd,
    outer_inv,
    inner_fwd,
    inner_inv,
    twiddle,
    twiddle_mid,
    spread,
    collect,
    out,
    filter_grad,
    send_in,
    send_out,
    recv_in,
    recv_out,
    spec,
    spec_mid,
    back_spec,
    back_mid,
    filt,
    filt_mid,
    field,
    grad_field,
    grad_rows,
    stage,
    scatter_send,
    scatter_recv,
    gathered,
    core_send,
    core_recv,
    x_send,
    x_recv,
    z_send,
    z_recv,
    return_send,
    return_recv,
    load_sem,
    store_sem,
    send_sem,
    recv_sem,
    side_send_sem,
    side_recv_sem,
):
    me = lax.axis_index("seq")
    mine = lax.axis_index("batch")
    rows = F1 // seq
    feats = history.shape[1] // seq
    chunks = rows // CHUNK
    core = lax.rem(mine, CORES)
    along_x = lax.rem(mine // CORES, XS)
    along_z = mine // (CORES * XS)
    opposite = batch - 1 - mine
    low = me < seq // 2

    def batch_index(z, x, c):
        return (z * XS + x) * CORES + c

    x_peers = [lax.rem(along_x + k, XS) for k in range(1, XS)]
    z_peers = [lax.rem(along_z + k, ZS) for k in range(1, ZS)]
    to_x = [{"batch": batch_index(along_z, x, core)} for x in x_peers]
    to_z = [{"batch": batch_index(z, along_x, core)} for z in z_peers]
    to_core = {"batch": batch_index(along_z, along_x, 1 - core)}

    loads = {}
    for name, source, target in (
        ("filter", filter_weight_hbm, filter_weight),
        ("history", history_hbm, history),
        ("outer_fwd", outer_fwd_hbm, outer_fwd),
        ("twiddle", twiddle_hbm, twiddle),
        ("twiddle_mid", twiddle_mid_hbm, twiddle_mid),
        ("inner_fwd", inner_fwd_hbm, inner_fwd),
        ("spread", spread_hbm, spread),
        ("inner_inv", inner_inv_hbm, inner_inv),
        ("outer_inv", outer_inv_hbm, outer_inv),
        ("gain_first", gain_first_hbm, gain_first),
        ("bias_first", bias_first_hbm, bias_first),
        ("w_in", w_in_hbm, w_in),
        ("w_out", w_out_hbm, w_out),
        ("gain_second", gain_second_hbm, gain_second),
        ("cotangent", cotangent_hbm, cotangent),
        ("collect", collect_hbm, collect),
    ):
        loads[name] = pltpu.make_async_copy(source, target, load_sem.at[len(loads)])
        loads[name].start()

    barrier = pltpu.get_barrier_semaphore()

    def greet(peer):
        pl.semaphore_signal(
            barrier, inc=1, device_id=peer, device_id_type=pl.DeviceIdType.MESH
        )

    def greet_seq(k, _):
        greet({"seq": lax.rem(me + k, seq)})
        return 0

    def greet_opposite(k, _):
        greet({"seq": k, "batch": opposite})
        return 0

    lax.fori_loop(0, seq, greet_opposite, 0)
    for peer in (*to_z, *to_x, to_core):
        greet(peer)
    lax.fori_loop(1, seq, greet_seq, 0)

    def side_copy(src, dst, way, peer):
        pltpu.make_async_remote_copy(
            src_ref=src,
            dst_ref=dst,
            send_sem=side_send_sem.at[way],
            recv_sem=side_recv_sem.at[way],
            device_id=peer,
            device_id_type=pl.DeviceIdType.MESH,
        ).start()

    def wait_bytes(ref, sem):
        pltpu.make_async_copy(ref, ref, sem).wait()

    def wait_all_seq(ref, sem):
        @pl.when(low)
        def _():
            wait_bytes(ref.at[pl.ds(0, seq - 1)], sem)

        @pl.when(jnp.logical_not(low))
        def _():
            wait_bytes(ref, sem)

    sizes = {
        1: gathered.at[0, 0, 0],
        2: gathered.at[0, 0, 0],
        3: gathered.at[0, 0, 0],
        4: gathered.at[:, pl.ds(0, XS - 1), 0],
        9: gathered.at[:, :, 0],
        10: core_recv,
        11: x_recv.at[0],
        12: x_recv.at[0],
        13: x_recv.at[0],
        14: x_recv.at[0],
        15: z_recv,
    }

    def arrived(*ways):
        for way in ways:
            wait_bytes(sizes[way], side_recv_sem.at[way])

    def scatter_prepare():
        for part in range(2):
            for tile in range(2):
                for line in range(8):
                    stage[line, 8 * tile + 4 * part : 8 * tile + 4 * part + 4, :] = filter_weight[
                        part, line, :, 128 * tile : 128 * (tile + 1)
                    ].astype(jnp.float32)
        tiles = []
        for line in range(8):
            tile = stage[jnp.where(low, line, 7 - line)]
            tiles.append(jnp.where(low, tile, mirror_rows(tile)))
        for to, tile in enumerate(block_transpose(tiles)):
            scatter_send[to] = tile[:8]
            scatter_send[8 + to] = tile[8:]

    def scatter_start():
        target = jnp.where(low, mine, opposite)

        def one(k, _):
            peer = lax.rem(me + k, seq)
            side_copy(
                scatter_send.at[peer], scatter_recv.at[me], 0, {"seq": peer, "batch": target}
            )
            return 0

        @pl.when(low)
        def _():
            scatter_recv[me] = scatter_send[me]

        lax.fori_loop(jnp.where(low, 1, 0), seq, one, 0)

    def gather_start():
        wait_all_seq(scatter_recv, side_recv_sem.at[0])
        lane = lax.broadcasted_iota(jnp.int32, (8, 128), 1)
        zeros = jnp.zeros((8, 128), jnp.float32)
        moved = [pltpu.roll(scatter_recv[seq - 1 - t], 16, 1) for t in range(8)]
        tiles = []
        for t in range(9):
            before = moved[t - 1] if t > 0 else zeros
            after = moved[t] if t < 8 else zeros
            tile = jnp.where(lane < 16, before, after)
            tiles.append(tile + scatter_recv[t] if t < 8 else tile)
        for t in range(5):
            upper = tiles[t] if t < 4 else tiles[8]
            lower = tiles[4 + t] if t < 4 else zeros
            gathered[along_z, along_x, core, t] = jnp.concatenate([upper, lower], axis=0).astype(
                jnp.bfloat16
            )
        own = gathered.at[along_z, along_x, core]
        for k, peer in enumerate(to_z):
            side_copy(own, own, 1 + k, peer)
        gather_forward(along_z)

    def gather_forward(z):
        for peer in to_x:
            block = gathered.at[z, along_x, core]
            side_copy(block, block, 4, peer)

    def gather_z(k):
        arrived(1 + k)
        gather_forward(lax.rem(along_z + ZS - 1 - k, ZS))

    def gather_core():
        arrived(4)
        block = gathered.at[:, :, core]
        side_copy(block, block, 9, to_core)

    def gather_finish():
        arrived(9)
        loads["spread"].wait()
        parts = [gathered[:, :, :, t].reshape(batch * 16, 128) for t in range(5)]
        block = jnp.concatenate(parts[:4], axis=1)
        for h in range(2):
            table = jnp.concatenate(
                [spread[k, 2 * F2 * h : 2 * F2 * (h + 1)] for k in range(4)], axis=1
            )
            result = dot(table, block).astype(jnp.bfloat16).T.astype(jnp.float32)
            filt[512 * h : 512 * (h + 1), :] = result[:, :F2]
            filt[1024 + 512 * h : 1024 + 512 * (h + 1), :] = result[:, F2:]
        table = jnp.concatenate([spread[k, : 2 * F2] for k in range(4)], axis=1)
        filt_mid[...] = dot(table, parts[4]).astype(jnp.bfloat16).T[:feats]

    def filter_lines(base):
        blocks = []
        for i in range(4):
            real = filt[pl.ds(base + i, LINES, stride=feats), :]
            imag = filt[pl.ds(1024 + base + i, LINES, stride=feats), :]
            blocks.append(jnp.concatenate([real, imag], axis=1))
        return jnp.concatenate(blocks, axis=0)

    def reduce_start():
        for d in range(feats):
            where = pl.ds(d * LINES, LINES)
            term = times_conj(back_spec[where, :], spec[where, :]) * inv_length
            grad_field[pl.ds(d, LINES, stride=feats), :] = term[:, :F2]
            grad_field[pl.ds(1024 + d, LINES, stride=feats), :] = term[:, F2:]
        loads["collect"].wait()
        parts = []
        for h in range(2):
            real = grad_field[512 * h : 512 * (h + 1), :]
            imag = grad_field[1024 + 512 * h : 1024 + 512 * (h + 1), :]
            both = jnp.concatenate([real, imag], axis=1).astype(jnp.bfloat16)
            parts.append(dot_nt(whole(collect), both).reshape(batch, 8, 512))
        mid = jnp.concatenate(
            [
                times_conj(back_mid[...], spec_mid[...]) * inv_length,
                jnp.zeros((128 - feats, 2 * F2), jnp.float32),
            ],
            axis=0,
        ).astype(jnp.bfloat16)
        last = dot_nt(whole(collect), mid).reshape(batch, 8, 128)
        both = jnp.concatenate(parts, axis=1).astype(jnp.bfloat16)
        both = both.reshape(ZS, XS, CORES, 16, 512)
        for t in range(4):
            core_send[:, :, :, t] = both[..., 128 * t : 128 * (t + 1)]
        last = jnp.concatenate([last, jnp.zeros_like(last)], axis=1).astype(jnp.bfloat16)
        core_send[:, :, :, 4] = last.reshape(ZS, XS, CORES, 16, 128)
        side_copy(core_send.at[:, :, 1 - core], core_recv, 10, to_core)

    def add(a, b):
        return (a.astype(jnp.float32) + b.astype(jnp.float32)).astype(jnp.bfloat16)

    z_order = [lax.rem(along_z + k, ZS) for k in (2, 1, 3, 0)]

    def reduce_x():
        arrived(10)
        for place, z in enumerate(z_order):
            for x in range(XS):
                x_send[z, x] = add(core_send[z, x, core], core_recv[z, x])
            for k, peer in enumerate(to_x):
                side_copy(x_send.at[z, x_peers[k]], x_recv.at[z, k], 11 + place, peer)

    def reduce_z():
        for place, z in enumerate(z_order):
            arrived(11 + place)
            total = x_send[z, along_x].astype(jnp.float32)
            for k in range(XS - 1):
                total = total + x_recv[z, k].astype(jnp.float32)
            z_send[z] = total.astype(jnp.bfloat16)
            if place < ZS - 1:
                side_copy(
                    z_send.at[z],
                    z_recv.at[place],
                    15,
                    {"batch": batch_index(z, along_x, core)},
                )

    def return_grad():
        arrived(15)
        total = z_send[along_z].astype(jnp.float32)
        for k in range(ZS - 1):
            total = total + z_recv[k].astype(jnp.float32)
        tiles = [total[t, :8] for t in range(4)] + [total[t, 8:] for t in range(4)]
        tiles.append(total[4, :8])
        lane = lax.broadcasted_iota(jnp.int32, (8, 128), 1)
        moved = [pltpu.roll(t, 112, 1) for t in tiles]
        for t in range(8):
            return_send[t] = tiles[t]
            return_send[seq - 1 - t] = jnp.where(lane < 112, moved[t], moved[t + 1])

        def send(peer, target):
            side_copy(
                return_send.at[peer], return_recv.at[me], 19, {"seq": peer, "batch": target}
            )

        half = seq // 2

        def far(k, _):
            send(half + lax.rem(me + k, half), opposite)
            return 0

        def near(k, _):
            send(lax.rem(me + k, half), mine)
            return 0

        lax.fori_loop(0, half, far, 0)

        @pl.when(low)
        def _():
            return_recv[me] = return_send[me]

        lax.fori_loop(jnp.where(low, 1, 0), half, near, 0)

    def return_finish():
        wait_all_seq(return_recv, side_recv_sem.at[19])
        tiles = [
            jnp.concatenate([return_recv[t], return_recv[8 + t]], axis=0) for t in range(8)
        ]
        for line, tile in enumerate(block_transpose(tiles)):
            stage[jnp.where(low, line, 7 - line)] = jnp.where(low, tile, mirror_rows(tile))
        for part in range(2):
            for tile in range(2):
                for line in range(8):
                    filter_grad[part, line, :, 128 * tile : 128 * (tile + 1)] = stage[
                        line, 8 * tile + 4 * part : 8 * tile + 4 * part + 4, :
                    ]

    def exchange(src, dst, way, chunk):
        def one(k, _):
            peer = lax.rem(me + k, seq)
            pltpu.make_async_remote_copy(
                src_ref=src(peer),
                dst_ref=dst,
                send_sem=send_sem.at[way],
                recv_sem=recv_sem.at[way, chunk],
                device_id={"seq": peer},
                device_id_type=pl.DeviceIdType.MESH,
            ).start()
            return 0

        lax.fori_loop(1, seq, one, 0)

    def turn(x, way, chunk):
        for j in range(chunk * CHUNK, (chunk + 1) * CHUNK):
            send_in[way, j] = x(j).T.reshape(seq, feats, F2)

    def send_positions(way, chunk):
        part = pl.ds(chunk * CHUNK, CHUNK)
        recv_in[way, me, part] = send_in[way, part, me]
        exchange(
            lambda peer: send_in.at[way, part, peer], recv_in.at[way, me, part], 2 * way, chunk
        )

    def send_features(way, chunk):
        part = pl.ds(chunk * CHUNK, CHUNK)
        recv_out[way, part, me] = send_out[way, me, part]
        exchange(
            lambda peer: send_out.at[way, peer, part], recv_out.at[way, part, me], 2 * way + 1, chunk
        )

    def wait_chunk(way, chunk):
        wait_bytes(
            send_in.at[0, pl.ds(0, CHUNK), pl.ds(0, seq - 1)], recv_sem.at[way, chunk]
        )

    def absorb(way, chunk):
        mid = 0.0
        for source in range(seq):
            block = recv_in[way, source, chunk * CHUNK : (chunk + 1) * CHUNK].astype(jnp.float32)
            first = (source * rows + chunk * CHUNK) * feats
            field[first : first + CHUNK * feats, :] = block.reshape(CHUNK * feats, F2)
            for j in range(CHUNK):
                mid = mid + block[j] if j % 2 == 0 else mid - block[j]
        return mid

    def forward(mid, spectrum, spectrum_mid):
        cos, sin = twiddle[0], twiddle[1]

        def step(group, _):
            base = group * 4
            halves = []
            for sub in range(2):
                pair = [
                    field[pl.ds(base + 2 * sub + i, F1, stride=feats), :] for i in range(2)
                ]
                two = jnp.concatenate(pair, axis=1).astype(jnp.bfloat16)
                both = dot(whole(outer_fwd), two)
                for i in range(2):
                    real = both[:LINES, i * F2 : (i + 1) * F2]
                    imag = both[LINES:, i * F2 : (i + 1) * F2]
                    halves.append(
                        jnp.concatenate(
                            [real * cos + imag * sin, imag * cos - real * sin], axis=1
                        ).astype(jnp.bfloat16)
                    )
            where = pl.ds(pl.multiple_of(base * LINES, 4 * LINES), 4 * LINES)
            spectrum[where, :] = dot(jnp.concatenate(halves, axis=0), whole(inner_fwd)).astype(
                jnp.bfloat16
            )
            return 0

        lax.fori_loop(0, feats // 4, step, 0, unroll=True)
        cos_mid, sin_mid = twiddle_mid[0], twiddle_mid[1]
        half = jnp.concatenate([mid * cos_mid, -mid * sin_mid], axis=1).astype(jnp.bfloat16)
        spectrum_mid[...] = dot(half, whole(inner_fwd)).astype(jnp.bfloat16)

    def backward(way, product, product_mid):
        cos, sin = twiddle[0], twiddle[1]

        def step(group, _):
            base = group * 4
            where = pl.ds(pl.multiple_of(base * LINES, 4 * LINES), 4 * LINES)
            half = dot(product(where, filter_lines(base)), whole(inner_inv))
            for sub in range(2):
                columns = []
                for i in range(2):
                    part = half[(2 * sub + i) * LINES : (2 * sub + i + 1) * LINES]
                    real, imag = part[:, :F2], part[:, F2:]
                    columns.append(
                        jnp.concatenate(
                            [real * cos - imag * sin, imag * cos + real * sin], axis=0
                        ).astype(jnp.bfloat16)
                    )
                result = dot(whole(outer_inv), jnp.concatenate(columns, axis=1)) * inv_length
                for i in range(2):
                    field[pl.ds(base + 2 * sub + i, F1, stride=feats), :] = result[
                        :, i * F2 : (i + 1) * F2
                    ]
            return 0

        lax.fori_loop(0, feats // 4, step, 0, unroll=True)
        half = dot(product_mid(), whole(inner_inv))
        last = (half[:, :F2] * twiddle_mid[0] - half[:, F2:] * twiddle_mid[1]).astype(jnp.bfloat16)
        last = last.astype(jnp.float32) * inv_length
        both = field[...].reshape(F1 // 2, 2, feats, F2)
        sign = jnp.where(lax.broadcasted_iota(jnp.int32, both.shape, 1) == 0, 1.0, -1.0)
        both = both + sign * last[None, None]
        send_out[way] = both.astype(jnp.bfloat16).reshape(seq, rows, feats, F2)

    def split(z):
        return z[:, :F2].astype(jnp.float32), z[:, F2:].astype(jnp.float32)

    def times(z, f):
        zr, zi = split(z)
        fr, fi = split(f)
        return jnp.concatenate([zr * fr - zi * fi, zr * fi + zi * fr], axis=1).astype(jnp.bfloat16)

    def times_conj(z, f):
        zr, zi = split(z)
        fr, fi = split(f)
        return jnp.concatenate([fr * zr + fi * zi, fr * zi - fi * zr], axis=1)

    loads["filter"].wait()
    scatter_prepare()
    loads["history"].wait()
    for chunk in range(chunks):
        turn(lambda j: history[pl.ds(j * F2, F2), :], 0, chunk)
    pl.semaphore_wait(barrier, 2 * seq - 1 + ZS - 1 + XS - 1 + 1)
    scatter_start()
    for chunk in range(chunks // 2):
        send_positions(0, chunk)
    gather_start()
    gather_z(0)
    gather_z(2)
    for chunk in range(chunks // 2, chunks):
        send_positions(0, chunk)
    gather_z(1)
    for name in ("outer_fwd", "twiddle", "twiddle_mid", "inner_fwd", "inner_inv", "outer_inv"):
        loads[name].wait()
    mid = 0.0
    for chunk in range(chunks):
        wait_chunk(0, chunk)
        mid = mid + absorb(0, chunk)
    forward(mid, spec, spec_mid)
    gather_core()
    gather_finish()
    backward(
        0,
        lambda where, lines: times(spec[where, :], lines),
        lambda: times(spec_mid[...], filt_mid[...]),
    )
    for chunk in range(chunks):
        send_features(0, chunk)

    for name in ("gain_first", "bias_first", "w_in", "w_out", "gain_second", "cotangent"):
        loads[name].wait()
    for chunk in range(chunks):
        wait_chunk(1, chunk)
        for j in range(chunk * CHUNK, (chunk + 1) * CHUNK):
            mixed = recv_out[0, j].reshape(seq * feats, F2).T.astype(jnp.float32)
            part = pl.ds(j * F2, F2)
            grad_rows[part, :] = local_rows(
                mixed,
                history[part, :],
                cotangent[part, :],
                gain_first[...],
                bias_first[...],
                w_in[...],
                w_out[...],
                gain_second[...],
            )
        turn(lambda j: grad_rows[pl.ds(j * F2, F2), :].astype(jnp.bfloat16), 1, chunk)
        send_positions(1, chunk)

    mid = 0.0
    for chunk in range(chunks):
        wait_chunk(2, chunk)
        mid = mid + absorb(1, chunk)
    forward(mid, back_spec, back_mid)
    reduce_start()
    reduce_x()
    backward(
        1,
        lambda where, lines: times_conj(back_spec[where, :], lines).astype(jnp.bfloat16),
        lambda: times_conj(back_mid[...], filt_mid[...]).astype(jnp.bfloat16),
    )
    for chunk in range(chunks // 2):
        send_features(1, chunk)
    reduce_z()
    return_grad()
    for chunk in range(chunks // 2, chunks):
        send_features(1, chunk)
    for chunk in range(chunks):
        wait_chunk(3, chunk)
        for j in range(chunk * CHUNK, (chunk + 1) * CHUNK):
            back = recv_out[1, j].reshape(seq * feats, F2).T.astype(jnp.float32)
            part = pl.ds(j * F2, F2)
            out[part, :] = (grad_rows[part, :] + back).astype(jnp.bfloat16)
        part = pl.ds(chunk * CHUNK * F2, CHUNK * F2)
        pltpu.make_async_copy(out.at[part], out_hbm.at[part], store_sem.at[0]).start()
    return_finish()
    store = pltpu.make_async_copy(filter_grad, filter_grad_hbm, store_sem.at[1])
    store.start()

    wait_all_seq(scatter_send, side_send_sem.at[0])
    for way, ref in sizes.items():
        wait_bytes(ref, side_send_sem.at[way])
    wait_all_seq(return_send, side_send_sem.at[19])
    sent = send_in.at[0, :, pl.ds(0, seq - 1)]
    for way in range(4):
        wait_bytes(sent, send_sem.at[way])
    pltpu.make_async_copy(out, out_hbm, store_sem.at[0]).wait()
    store.wait()


def local(history, cotangent, filter_weight, gain_first, bias_first, w_in, w_out, gain_second):
    user_count, row_count, features = history.shape
    seq = lax.axis_size("seq")
    feats = features // seq
    rows = F1 // seq
    bf16, f32 = jnp.bfloat16, jnp.float32
    tables = [jnp.asarray(t) for t in host_tables()]

    batch = lax.axis_size("batch")
    dma = pltpu.SemaphoreType.DMA
    operands = (
        history.reshape(row_count, features),
        cotangent.reshape(row_count, features),
        filter_weight,
        gain_first.reshape(1, features),
        bias_first.reshape(1, features),
        w_in,
        w_out,
        gain_second.reshape(1, features),
        *tables,
    )
    out, filter_grad = pl.pallas_call(
        functools.partial(kernel, seq, batch),
        out_shape=(
            jax.ShapeDtypeStruct((row_count, features), bf16),
            jax.ShapeDtypeStruct(filter_weight.shape, f32),
        ),
        in_specs=[pl.BlockSpec(memory_space=pltpu.HBM)] * len(operands),
        out_specs=(pl.BlockSpec(memory_space=pltpu.HBM),) * 2,
        scratch_shapes=[
            *[pltpu.VMEM(x.shape, x.dtype) for x in operands],
            pltpu.VMEM((row_count, features), bf16),
            pltpu.VMEM(filter_weight.shape, f32),
            pltpu.VMEM((2, rows, seq, feats, F2), bf16),
            pltpu.VMEM((2, seq, rows, feats, F2), bf16),
            pltpu.VMEM((2, seq, rows, feats, F2), bf16),
            pltpu.VMEM((2, rows, seq, feats, F2), bf16),
            pltpu.VMEM((feats * LINES, 2 * F2), bf16),
            pltpu.VMEM((feats, 2 * F2), bf16),
            pltpu.VMEM((feats * LINES, 2 * F2), bf16),
            pltpu.VMEM((feats, 2 * F2), bf16),
            pltpu.VMEM((2 * LINES * feats, F2), f32),
            pltpu.VMEM((feats, 2 * F2), bf16),
            pltpu.VMEM((F1 * feats, F2), f32),
            pltpu.VMEM((2 * LINES * feats, F2), f32),
            pltpu.VMEM((row_count, features), f32),
            pltpu.VMEM((8, 16, 128), f32),
            pltpu.VMEM((seq, 8, 128), f32),
            pltpu.VMEM((seq, 8, 128), f32),
            pltpu.VMEM((ZS, XS, CORES, 5, 16, 128), bf16),
            pltpu.VMEM((ZS, XS, CORES, 5, 16, 128), bf16),
            pltpu.VMEM((ZS, XS, 5, 16, 128), bf16),
            pltpu.VMEM((ZS, XS, 5, 16, 128), bf16),
            pltpu.VMEM((ZS, XS - 1, 5, 16, 128), bf16),
            pltpu.VMEM((ZS, 5, 16, 128), bf16),
            pltpu.VMEM((ZS - 1, 5, 16, 128), bf16),
            pltpu.VMEM((seq, 8, 128), f32),
            pltpu.VMEM((seq, 8, 128), f32),
            dma((len(operands),)),
            dma((2,)),
            dma((4,)),
            dma((4, rows // CHUNK)),
            dma((20,)),
            dma((20,)),
        ],
        compiler_params=pltpu.CompilerParams(
            collective_id=0, has_side_effects=True, vmem_limit_bytes=60 * 2**20
        ),
    )(*operands)
    return (out.reshape(user_count, row_count, features), filter_grad)


def solution(mesh):
    placed = (
        P("batch", "seq", None),
        P("batch", "seq", None),
        P(None, "seq", "batch", None),
        P(),
        P(),
        P(),
        P(),
        P(),
    )
    return jax.shard_map(
        local,
        mesh=mesh,
        in_specs=placed,
        out_specs=(P("batch", "seq", None), P(None, "seq", "batch", None)),
        check_vma=False,
    )
```

```python
import functools
import math

import jax
import jax.numpy as jnp
import ml_dtypes
import numpy as np
from jax import lax
from jax.experimental import pallas as pl
from jax.experimental.pallas import tpu as pltpu
from jax.sharding import PartitionSpec as P

F1 = 128
F2 = 128
LINES = 64
CHUNK = 2
ZS, XS, CORES = 4, 4, 2

epsilon = 1e-05
inv_root_two = 1.0 / math.sqrt(2.0)
inv_root_tau = 1.0 / math.sqrt(2.0 * math.pi)
inv_length = 1.0 / (F1 * F2)


def columns(table):
    blocks = np.split(table, table.shape[1] // 128, axis=1)
    return np.stack(blocks).astype(ml_dtypes.bfloat16)


def whole(table):
    return jnp.concatenate([table[k] for k in range(table.shape[0])], axis=1)


def host_tables():
    index = np.arange(F1)
    angle = 2.0 * np.pi * (index[:, None] * index[None, :] % F1) / F1
    cos, sin = np.cos(angle), np.sin(angle)
    outer_fwd = np.concatenate([cos[:LINES], -sin[:LINES]], axis=0)
    outer_inv = np.concatenate([cos[:LINES], -sin[:LINES]], axis=0).T
    inner_fwd = np.block([[cos, -sin], [sin, cos]])
    inner_inv = np.block([[cos, sin], [-sin, cos]])
    lines = np.arange(LINES + 1)
    phase = 2.0 * np.pi * (lines[:, None] * index[None, :]) / (F1 * F2)
    narrow = [columns(t) for t in (outer_fwd, outer_inv, inner_fwd, inner_inv)]
    twiddles = np.stack([np.cos(phase), np.sin(phase)]).astype(np.float32)
    return (*narrow, twiddles[:, :LINES], twiddles[:, LINES:], *permutations())


def permutations():
    spread = np.zeros((2, 2 * F2, 4 * F2), np.float32)
    collect = np.zeros((2 * F2, 2 * F2), np.float32)
    for part in range(2):
        for q in range(F2):
            for h in range(2):
                spread[h, part * F2 + q, (q // 4) * 16 + h * 8 + part * 4 + q % 4] = 1.0
            block = q // 4
            place = (block % CORES) * (F2 // 4 // CORES) + block // CORES
            collect[place * 8 + part * 4 + q % 4, part * F2 + q] = 1.0
    return columns(spread.reshape(4 * F2, 4 * F2)), columns(collect)


def dot(a, b):
    return jnp.dot(a, b, preferred_element_type=jnp.float32)


def dot_nt(a, b):
    return lax.dot_general(a, b, (((1,), (1,)), ((), ())), preferred_element_type=jnp.float32)


def mirror_rows(x):
    axis = x.ndim - 2
    size = x.shape[axis]
    row = lax.broadcasted_iota(jnp.int32, x.shape, axis)
    for step in (1, 2):
        up, down = pltpu.roll(x, step, axis), pltpu.roll(x, size - step, axis)
        x = jnp.where((row & step) != 0, up, down)
    return jnp.where((row & 4) != 0, -x, x)


def block_transpose(tiles):
    lane = lax.broadcasted_iota(jnp.int32, tiles[0].shape, 1) // 16
    result = []
    for to in range(8):
        total = tiles[to]
        for block in range(8):
            if block != to:
                moved = pltpu.roll(tiles[block], 16 * ((block - to) % 8), 1)
                total = jnp.where(lane == block, moved, total)
        result.append(total)
    return result


def mean(x):
    return jnp.mean(x, axis=-1, keepdims=True)


def local_rows(mixed, history, cot, gain_first, bias_first, w_in, w_out, gain_second):
    summed = mixed + history.astype(jnp.float32)
    center_one = summed - mean(summed)
    inv_one = lax.rsqrt(mean(center_one * center_one) + epsilon)
    norm_one = center_one * inv_one
    hidden = (norm_one * gain_first + bias_first).astype(jnp.bfloat16)
    preact = dot(hidden, w_in)
    cumul = 0.5 * (1.0 + lax.erf(preact * inv_root_two))
    activation = (preact * cumul).astype(jnp.bfloat16)
    output_sum = dot(activation, w_out) + hidden.astype(jnp.float32)
    center_two = output_sum - mean(output_sum)
    inv_two = lax.rsqrt(mean(center_two * center_two) + epsilon)
    norm_two = center_two * inv_two
    grad_norm = cot.astype(jnp.float32) * gain_second
    grad_sum = inv_two * (grad_norm - mean(grad_norm) - norm_two * mean(grad_norm * norm_two))
    grad_act = dot_nt(grad_sum.astype(jnp.bfloat16), w_out)
    density = jnp.exp(-0.5 * preact * preact) * inv_root_tau
    grad_pre = (grad_act * (cumul + preact * density)).astype(jnp.bfloat16)
    grad_hidden = dot_nt(grad_pre, w_in) + grad_sum
    grad_scaled = grad_hidden * gain_first
    return inv_one * (grad_scaled - mean(grad_scaled) - norm_one * mean(grad_scaled * norm_one))


def kernel(
    seq,
    batch,
    history_hbm,
    cotangent_hbm,
    filter_weight_hbm,
    gain_first_hbm,
    bias_first_hbm,
    w_in_hbm,
    w_out_hbm,
    gain_second_hbm,
    outer_fwd_hbm,
    outer_inv_hbm,
    inner_fwd_hbm,
    inner_inv_hbm,
    twiddle_hbm,
    twiddle_mid_hbm,
    spread_hbm,
    collect_hbm,
    out_hbm,
    filter_grad_hbm,
    history,
    cotangent,
    filter_weight,
    gain_first,
    bias_first,
    w_in,
    w_out,
    gain_second,
    outer_fwd,
    outer_inv,
    inner_fwd,
    inner_inv,
    twiddle,
    twiddle_mid,
    spread,
    collect,
    out,
    filter_grad,
    send_in,
    send_out,
    recv_in,
    recv_out,
    spec,
    spec_mid,
    back_spec,
    back_mid,
    filt,
    filt_mid,
    field,
    grad_field,
    grad_rows,
    stage,
    scatter_send,
    scatter_recv,
    gathered,
    core_send,
    core_recv,
    x_send,
    x_recv,
    z_send,
    z_recv,
    return_send,
    return_recv,
    load_sem,
    store_sem,
    send_sem,
    recv_sem,
    side_send_sem,
    side_recv_sem,
):
    me = lax.axis_index("seq")
    mine = lax.axis_index("batch")
    rows = F1 // seq
    feats = history.shape[1] // seq
    chunks = rows // CHUNK
    core = lax.rem(mine, CORES)
    along_x = lax.rem(mine // CORES, XS)
    along_z = mine // (CORES * XS)
    opposite = batch - 1 - mine
    low = me < seq // 2

    def batch_index(z, x, c):
        return (z * XS + x) * CORES + c

    x_peers = [lax.rem(along_x + k, XS) for k in range(1, XS)]
    z_peers = [lax.rem(along_z + k, ZS) for k in range(1, ZS)]
    to_x = [{"batch": batch_index(along_z, x, core)} for x in x_peers]
    to_z = [{"batch": batch_index(z, along_x, core)} for z in z_peers]
    to_core = {"batch": batch_index(along_z, along_x, 1 - core)}

    loads = {}
    for name, source, target in (
        ("filter", filter_weight_hbm, filter_weight),
        ("history", history_hbm, history),
        ("outer_fwd", outer_fwd_hbm, outer_fwd),
        ("twiddle", twiddle_hbm, twiddle),
        ("twiddle_mid", twiddle_mid_hbm, twiddle_mid),
        ("inner_fwd", inner_fwd_hbm, inner_fwd),
        ("spread", spread_hbm, spread),
        ("inner_inv", inner_inv_hbm, inner_inv),
        ("outer_inv", outer_inv_hbm, outer_inv),
        ("gain_first", gain_first_hbm, gain_first),
        ("bias_first", bias_first_hbm, bias_first),
        ("w_in", w_in_hbm, w_in),
        ("w_out", w_out_hbm, w_out),
        ("gain_second", gain_second_hbm, gain_second),
        ("cotangent", cotangent_hbm, cotangent),
        ("collect", collect_hbm, collect),
    ):
        loads[name] = pltpu.make_async_copy(source, target, load_sem.at[len(loads)])
        loads[name].start()

    barrier = pltpu.get_barrier_semaphore()

    def greet(peer):
        pl.semaphore_signal(
            barrier, inc=1, device_id=peer, device_id_type=pl.DeviceIdType.MESH
        )

    def greet_seq(k, _):
        greet({"seq": lax.rem(me + k, seq)})
        return 0

    def greet_opposite(k, _):
        greet({"seq": k, "batch": opposite})
        return 0

    lax.fori_loop(0, seq, greet_opposite, 0)
    for peer in (*to_z, *to_x, to_core):
        greet(peer)
    lax.fori_loop(1, seq, greet_seq, 0)

    def side_copy(src, dst, way, peer):
        pltpu.make_async_remote_copy(
            src_ref=src,
            dst_ref=dst,
            send_sem=side_send_sem.at[way],
            recv_sem=side_recv_sem.at[way],
            device_id=peer,
            device_id_type=pl.DeviceIdType.MESH,
        ).start()

    def wait_bytes(ref, sem):
        pltpu.make_async_copy(ref, ref, sem).wait()

    def wait_all_seq(ref, sem):
        @pl.when(low)
        def _():
            wait_bytes(ref.at[pl.ds(0, seq - 1)], sem)

        @pl.when(jnp.logical_not(low))
        def _():
            wait_bytes(ref, sem)

    sizes = {
        1: gathered.at[0, 0, 0],
        2: gathered.at[0, 0, 0],
        3: gathered.at[0, 0, 0],
        4: gathered.at[:, pl.ds(0, XS - 1), 0],
        9: gathered.at[:, :, 0],
        10: core_recv,
        11: x_recv.at[0],
        12: x_recv.at[0],
        13: x_recv.at[0],
        14: x_recv.at[0],
        15: z_recv,
    }

    def arrived(*ways):
        for way in ways:
            wait_bytes(sizes[way], side_recv_sem.at[way])

    def scatter_prepare():
        for part in range(2):
            for tile in range(2):
                for line in range(8):
                    stage[line, 8 * tile + 4 * part : 8 * tile + 4 * part + 4, :] = filter_weight[
                        part, line, :, 128 * tile : 128 * (tile + 1)
                    ].astype(jnp.float32)
        tiles = []
        for line in range(8):
            tile = stage[jnp.where(low, line, 7 - line)]
            tiles.append(jnp.where(low, tile, mirror_rows(tile)))
        for to, tile in enumerate(block_transpose(tiles)):
            scatter_send[to] = tile[:8]
            scatter_send[8 + to] = tile[8:]

    def scatter_start():
        target = jnp.where(low, mine, opposite)

        def one(k, _):
            peer = lax.rem(me + k, seq)
            side_copy(
                scatter_send.at[peer], scatter_recv.at[me], 0, {"seq": peer, "batch": target}
            )
            return 0

        @pl.when(low)
        def _():
            scatter_recv[me] = scatter_send[me]

        lax.fori_loop(jnp.where(low, 1, 0), seq, one, 0)

    def gather_start():
        wait_all_seq(scatter_recv, side_recv_sem.at[0])
        lane = lax.broadcasted_iota(jnp.int32, (8, 128), 1)
        zeros = jnp.zeros((8, 128), jnp.float32)
        moved = [pltpu.roll(scatter_recv[seq - 1 - t], 16, 1) for t in range(8)]
        tiles = []
        for t in range(9):
            before = moved[t - 1] if t > 0 else zeros
            after = moved[t] if t < 8 else zeros
            tile = jnp.where(lane < 16, before, after)
            tiles.append(tile + scatter_recv[t] if t < 8 else tile)
        for t in range(5):
            upper = tiles[t] if t < 4 else tiles[8]
            lower = tiles[4 + t] if t < 4 else zeros
            gathered[along_z, along_x, core, t] = jnp.concatenate([upper, lower], axis=0).astype(
                jnp.bfloat16
            )
        own = gathered.at[along_z, along_x, core]
        for k, peer in enumerate(to_z):
            side_copy(own, own, 1 + k, peer)
        gather_forward(along_z)

    def gather_forward(z):
        for peer in to_x:
            block = gathered.at[z, along_x, core]
            side_copy(block, block, 4, peer)

    def gather_z(k):
        arrived(1 + k)
        gather_forward(lax.rem(along_z + ZS - 1 - k, ZS))

    def gather_core():
        arrived(4)
        block = gathered.at[:, :, core]
        side_copy(block, block, 9, to_core)

    def gather_finish():
        arrived(9)
        loads["spread"].wait()
        parts = [gathered[:, :, :, t].reshape(batch * 16, 128) for t in range(5)]
        block = jnp.concatenate(parts[:4], axis=1)
        for h in range(2):
            table = jnp.concatenate(
                [spread[k, 2 * F2 * h : 2 * F2 * (h + 1)] for k in range(4)], axis=1
            )
            result = dot(table, block).astype(jnp.bfloat16).T.astype(jnp.float32)
            filt[512 * h : 512 * (h + 1), :] = result[:, :F2]
            filt[1024 + 512 * h : 1024 + 512 * (h + 1), :] = result[:, F2:]
        table = jnp.concatenate([spread[k, : 2 * F2] for k in range(4)], axis=1)
        filt_mid[...] = dot(table, parts[4]).astype(jnp.bfloat16).T[:feats]

    def filter_lines(base):
        blocks = []
        for i in range(4):
            real = filt[pl.ds(base + i, LINES, stride=feats), :]
            imag = filt[pl.ds(1024 + base + i, LINES, stride=feats), :]
            blocks.append(jnp.concatenate([real, imag], axis=1))
        return jnp.concatenate(blocks, axis=0)

    def reduce_start():
        for d in range(feats):
            where = pl.ds(d * LINES, LINES)
            term = times_conj(back_spec[where, :], spec[where, :]) * inv_length
            grad_field[pl.ds(d, LINES, stride=feats), :] = term[:, :F2]
            grad_field[pl.ds(1024 + d, LINES, stride=feats), :] = term[:, F2:]
        loads["collect"].wait()
        operands = []
        for h in range(2):
            real = grad_field[512 * h : 512 * (h + 1), :]
            imag = grad_field[1024 + 512 * h : 1024 + 512 * (h + 1), :]
            operands.append(jnp.concatenate([real, imag], axis=1).astype(jnp.bfloat16))
        mid = jnp.concatenate(
            [
                times_conj(back_mid[...], spec_mid[...]) * inv_length,
                jnp.zeros((128 - feats, 2 * F2), jnp.float32),
            ],
            axis=0,
        ).astype(jnp.bfloat16)
        for c in (1 - core, core):
            where = pl.ds(pl.multiple_of(c * F2, F2), F2)
            table = jnp.concatenate([collect[0, where], collect[1, where]], axis=1)
            parts = [dot_nt(table, x).reshape(batch // CORES, 8, 512) for x in operands]
            last = dot_nt(table, mid).reshape(batch // CORES, 8, 128)
            both = jnp.concatenate(parts, axis=1).astype(jnp.bfloat16)
            both = both.reshape(ZS, XS, 16, 512)
            for t in range(4):
                core_send[c, :, :, t] = both[..., 128 * t : 128 * (t + 1)]
            last = jnp.concatenate([last, jnp.zeros_like(last)], axis=1).astype(jnp.bfloat16)
            core_send[c, :, :, 4] = last.reshape(ZS, XS, 16, 128)
            if c is not core:
                side_copy(core_send.at[c], core_recv, 10, to_core)

    def add(a, b):
        return (a.astype(jnp.float32) + b.astype(jnp.float32)).astype(jnp.bfloat16)

    z_order = [lax.rem(along_z + k, ZS) for k in (2, 1, 3, 0)]

    def reduce_x():
        arrived(10)
        for place, z in enumerate(z_order):
            for x in range(XS):
                x_send[z, x] = add(core_send[core, z, x], core_recv[z, x])
            for k, peer in enumerate(to_x):
                side_copy(x_send.at[z, x_peers[k]], x_recv.at[z, k], 11 + place, peer)

    def reduce_z():
        for place, z in enumerate(z_order):
            arrived(11 + place)
            total = x_send[z, along_x].astype(jnp.float32)
            for k in range(XS - 1):
                total = total + x_recv[z, k].astype(jnp.float32)
            z_send[z] = total.astype(jnp.bfloat16)
            if place < ZS - 1:
                side_copy(
                    z_send.at[z],
                    z_recv.at[place],
                    15,
                    {"batch": batch_index(z, along_x, core)},
                )

    def return_grad():
        arrived(15)
        total = z_send[along_z].astype(jnp.float32)
        for k in range(ZS - 1):
            total = total + z_recv[k].astype(jnp.float32)
        tiles = [total[t, :8] for t in range(4)] + [total[t, 8:] for t in range(4)]
        tiles.append(total[4, :8])
        lane = lax.broadcasted_iota(jnp.int32, (8, 128), 1)
        moved = [pltpu.roll(t, 112, 1) for t in tiles]
        for t in range(8):
            return_send[t] = tiles[t]
            return_send[seq - 1 - t] = jnp.where(lane < 112, moved[t], moved[t + 1])

        def send(peer, target):
            side_copy(
                return_send.at[peer], return_recv.at[me], 19, {"seq": peer, "batch": target}
            )

        half = seq // 2

        def far(k, _):
            send(half + lax.rem(me + k, half), opposite)
            return 0

        def near(k, _):
            send(lax.rem(me + k, half), mine)
            return 0

        lax.fori_loop(0, half, far, 0)

        @pl.when(low)
        def _():
            return_recv[me] = return_send[me]

        lax.fori_loop(jnp.where(low, 1, 0), half, near, 0)

    def return_finish():
        wait_all_seq(return_recv, side_recv_sem.at[19])
        tiles = [
            jnp.concatenate([return_recv[t], return_recv[8 + t]], axis=0) for t in range(8)
        ]
        for line, tile in enumerate(block_transpose(tiles)):
            stage[jnp.where(low, line, 7 - line)] = jnp.where(low, tile, mirror_rows(tile))
        for part in range(2):
            for tile in range(2):
                for line in range(8):
                    filter_grad[part, line, :, 128 * tile : 128 * (tile + 1)] = stage[
                        line, 8 * tile + 4 * part : 8 * tile + 4 * part + 4, :
                    ]

    def exchange(src, dst, way, chunk):
        def one(k, _):
            peer = lax.rem(me + k, seq)
            pltpu.make_async_remote_copy(
                src_ref=src(peer),
                dst_ref=dst,
                send_sem=send_sem.at[way],
                recv_sem=recv_sem.at[way, chunk],
                device_id={"seq": peer},
                device_id_type=pl.DeviceIdType.MESH,
            ).start()
            return 0

        lax.fori_loop(1, seq, one, 0)

    def turn(x, way, chunk):
        for j in range(chunk * CHUNK, (chunk + 1) * CHUNK):
            send_in[way, j] = x(j).T.reshape(seq, feats, F2)

    def send_positions(way, chunk):
        part = pl.ds(chunk * CHUNK, CHUNK)
        recv_in[way, me, part] = send_in[way, part, me]
        exchange(
            lambda peer: send_in.at[way, part, peer], recv_in.at[way, me, part], 2 * way, chunk
        )

    def send_features(way, chunk):
        part = pl.ds(chunk * CHUNK, CHUNK)
        recv_out[way, part, me] = send_out[way, me, part]
        exchange(
            lambda peer: send_out.at[way, peer, part], recv_out.at[way, part, me], 2 * way + 1, chunk
        )

    def wait_chunk(way, chunk):
        wait_bytes(
            send_in.at[0, pl.ds(0, CHUNK), pl.ds(0, seq - 1)], recv_sem.at[way, chunk]
        )

    def absorb(way, chunk):
        mid = 0.0
        for source in range(seq):
            block = recv_in[way, source, chunk * CHUNK : (chunk + 1) * CHUNK].astype(jnp.float32)
            first = (source * rows + chunk * CHUNK) * feats
            field[first : first + CHUNK * feats, :] = block.reshape(CHUNK * feats, F2)
            for j in range(CHUNK):
                mid = mid + block[j] if j % 2 == 0 else mid - block[j]
        return mid

    def forward(mid, spectrum, spectrum_mid):
        cos, sin = twiddle[0], twiddle[1]

        def step(group, _):
            base = group * 4
            halves = []
            for sub in range(2):
                pair = [
                    field[pl.ds(base + 2 * sub + i, F1, stride=feats), :] for i in range(2)
                ]
                two = jnp.concatenate(pair, axis=1).astype(jnp.bfloat16)
                both = dot(whole(outer_fwd), two)
                for i in range(2):
                    real = both[:LINES, i * F2 : (i + 1) * F2]
                    imag = both[LINES:, i * F2 : (i + 1) * F2]
                    halves.append(
                        jnp.concatenate(
                            [real * cos + imag * sin, imag * cos - real * sin], axis=1
                        ).astype(jnp.bfloat16)
                    )
            where = pl.ds(pl.multiple_of(base * LINES, 4 * LINES), 4 * LINES)
            spectrum[where, :] = dot(jnp.concatenate(halves, axis=0), whole(inner_fwd)).astype(
                jnp.bfloat16
            )
            return 0

        lax.fori_loop(0, feats // 4, step, 0, unroll=True)
        cos_mid, sin_mid = twiddle_mid[0], twiddle_mid[1]
        half = jnp.concatenate([mid * cos_mid, -mid * sin_mid], axis=1).astype(jnp.bfloat16)
        spectrum_mid[...] = dot(half, whole(inner_fwd)).astype(jnp.bfloat16)

    def backward(way, product, product_mid):
        cos, sin = twiddle[0], twiddle[1]

        def step(group, _):
            base = group * 4
            where = pl.ds(pl.multiple_of(base * LINES, 4 * LINES), 4 * LINES)
            half = dot(product(where, filter_lines(base)), whole(inner_inv))
            for sub in range(2):
                columns = []
                for i in range(2):
                    part = half[(2 * sub + i) * LINES : (2 * sub + i + 1) * LINES]
                    real, imag = part[:, :F2], part[:, F2:]
                    columns.append(
                        jnp.concatenate(
                            [real * cos - imag * sin, imag * cos + real * sin], axis=0
                        ).astype(jnp.bfloat16)
                    )
                result = dot(whole(outer_inv), jnp.concatenate(columns, axis=1)) * inv_length
                for i in range(2):
                    field[pl.ds(base + 2 * sub + i, F1, stride=feats), :] = result[
                        :, i * F2 : (i + 1) * F2
                    ]
            return 0

        lax.fori_loop(0, feats // 4, step, 0, unroll=True)
        half = dot(product_mid(), whole(inner_inv))
        last = (half[:, :F2] * twiddle_mid[0] - half[:, F2:] * twiddle_mid[1]).astype(jnp.bfloat16)
        last = last.astype(jnp.float32) * inv_length
        both = field[...].reshape(F1 // 2, 2, feats, F2)
        sign = jnp.where(lax.broadcasted_iota(jnp.int32, both.shape, 1) == 0, 1.0, -1.0)
        both = both + sign * last[None, None]
        send_out[way] = both.astype(jnp.bfloat16).reshape(seq, rows, feats, F2)

    def split(z):
        return z[:, :F2].astype(jnp.float32), z[:, F2:].astype(jnp.float32)

    def times(z, f):
        zr, zi = split(z)
        fr, fi = split(f)
        return jnp.concatenate([zr * fr - zi * fi, zr * fi + zi * fr], axis=1).astype(jnp.bfloat16)

    def times_conj(z, f):
        zr, zi = split(z)
        fr, fi = split(f)
        return jnp.concatenate([fr * zr + fi * zi, fr * zi - fi * zr], axis=1)

    loads["filter"].wait()
    scatter_prepare()
    loads["history"].wait()
    for chunk in range(chunks):
        turn(lambda j: history[pl.ds(j * F2, F2), :], 0, chunk)
    pl.semaphore_wait(barrier, 2 * seq - 1 + ZS - 1 + XS - 1 + 1)
    scatter_start()
    for chunk in range(chunks // 2):
        send_positions(0, chunk)
    gather_start()
    gather_z(0)
    gather_z(2)
    for chunk in range(chunks // 2, chunks):
        send_positions(0, chunk)
    gather_z(1)
    for name in ("outer_fwd", "twiddle", "twiddle_mid", "inner_fwd", "inner_inv", "outer_inv"):
        loads[name].wait()
    mid = 0.0
    for chunk in range(chunks):
        wait_chunk(0, chunk)
        mid = mid + absorb(0, chunk)
    forward(mid, spec, spec_mid)
    gather_core()
    gather_finish()
    backward(
        0,
        lambda where, lines: times(spec[where, :], lines),
        lambda: times(spec_mid[...], filt_mid[...]),
    )
    for chunk in range(chunks):
        send_features(0, chunk)

    for name in ("gain_first", "bias_first", "w_in", "w_out", "gain_second", "cotangent"):
        loads[name].wait()
    for chunk in range(chunks):
        wait_chunk(1, chunk)
        for j in range(chunk * CHUNK, (chunk + 1) * CHUNK):
            mixed = recv_out[0, j].reshape(seq * feats, F2).T.astype(jnp.float32)
            part = pl.ds(j * F2, F2)
            grad_rows[part, :] = local_rows(
                mixed,
                history[part, :],
                cotangent[part, :],
                gain_first[...],
                bias_first[...],
                w_in[...],
                w_out[...],
                gain_second[...],
            )
        turn(lambda j: grad_rows[pl.ds(j * F2, F2), :].astype(jnp.bfloat16), 1, chunk)
        send_positions(1, chunk)

    mid = 0.0
    for chunk in range(chunks):
        wait_chunk(2, chunk)
        mid = mid + absorb(1, chunk)
    forward(mid, back_spec, back_mid)
    reduce_start()
    reduce_x()
    backward(
        1,
        lambda where, lines: times_conj(back_spec[where, :], lines).astype(jnp.bfloat16),
        lambda: times_conj(back_mid[...], filt_mid[...]).astype(jnp.bfloat16),
    )
    send_features(1, 0)
    reduce_z()
    send_features(1, 1)
    return_grad()
    for chunk in range(2, chunks):
        send_features(1, chunk)
    for chunk in range(chunks):
        wait_chunk(3, chunk)
        for j in range(chunk * CHUNK, (chunk + 1) * CHUNK):
            back = recv_out[1, j].reshape(seq * feats, F2).T.astype(jnp.float32)
            part = pl.ds(j * F2, F2)
            out[part, :] = (grad_rows[part, :] + back).astype(jnp.bfloat16)
        part = pl.ds(chunk * CHUNK * F2, CHUNK * F2)
        pltpu.make_async_copy(out.at[part], out_hbm.at[part], store_sem.at[0]).start()
    return_finish()
    store = pltpu.make_async_copy(filter_grad, filter_grad_hbm, store_sem.at[1])
    store.start()

    wait_all_seq(scatter_send, side_send_sem.at[0])
    for way, ref in sizes.items():
        wait_bytes(ref, side_send_sem.at[way])
    wait_all_seq(return_send, side_send_sem.at[19])
    sent = send_in.at[0, :, pl.ds(0, seq - 1)]
    for way in range(4):
        wait_bytes(sent, send_sem.at[way])
    pltpu.make_async_copy(out, out_hbm, store_sem.at[0]).wait()
    store.wait()


def local(history, cotangent, filter_weight, gain_first, bias_first, w_in, w_out, gain_second):
    user_count, row_count, features = history.shape
    seq = lax.axis_size("seq")
    feats = features // seq
    rows = F1 // seq
    bf16, f32 = jnp.bfloat16, jnp.float32
    tables = [jnp.asarray(t) for t in host_tables()]

    batch = lax.axis_size("batch")
    dma = pltpu.SemaphoreType.DMA
    operands = (
        history.reshape(row_count, features),
        cotangent.reshape(row_count, features),
        filter_weight,
        gain_first.reshape(1, features),
        bias_first.reshape(1, features),
        w_in,
        w_out,
        gain_second.reshape(1, features),
        *tables,
    )
    out, filter_grad = pl.pallas_call(
        functools.partial(kernel, seq, batch),
        out_shape=(
            jax.ShapeDtypeStruct((row_count, features), bf16),
            jax.ShapeDtypeStruct(filter_weight.shape, f32),
        ),
        in_specs=[pl.BlockSpec(memory_space=pltpu.HBM)] * len(operands),
        out_specs=(pl.BlockSpec(memory_space=pltpu.HBM),) * 2,
        scratch_shapes=[
            *[pltpu.VMEM(x.shape, x.dtype) for x in operands],
            pltpu.VMEM((row_count, features), bf16),
            pltpu.VMEM(filter_weight.shape, f32),
            pltpu.VMEM((2, rows, seq, feats, F2), bf16),
            pltpu.VMEM((2, seq, rows, feats, F2), bf16),
            pltpu.VMEM((2, seq, rows, feats, F2), bf16),
            pltpu.VMEM((2, rows, seq, feats, F2), bf16),
            pltpu.VMEM((feats * LINES, 2 * F2), bf16),
            pltpu.VMEM((feats, 2 * F2), bf16),
            pltpu.VMEM((feats * LINES, 2 * F2), bf16),
            pltpu.VMEM((feats, 2 * F2), bf16),
            pltpu.VMEM((2 * LINES * feats, F2), f32),
            pltpu.VMEM((feats, 2 * F2), bf16),
            pltpu.VMEM((F1 * feats, F2), f32),
            pltpu.VMEM((2 * LINES * feats, F2), f32),
            pltpu.VMEM((row_count, features), f32),
            pltpu.VMEM((8, 16, 128), f32),
            pltpu.VMEM((seq, 8, 128), f32),
            pltpu.VMEM((seq, 8, 128), f32),
            pltpu.VMEM((ZS, XS, CORES, 5, 16, 128), bf16),
            pltpu.VMEM((CORES, ZS, XS, 5, 16, 128), bf16),
            pltpu.VMEM((ZS, XS, 5, 16, 128), bf16),
            pltpu.VMEM((ZS, XS, 5, 16, 128), bf16),
            pltpu.VMEM((ZS, XS - 1, 5, 16, 128), bf16),
            pltpu.VMEM((ZS, 5, 16, 128), bf16),
            pltpu.VMEM((ZS - 1, 5, 16, 128), bf16),
            pltpu.VMEM((seq, 8, 128), f32),
            pltpu.VMEM((seq, 8, 128), f32),
            dma((len(operands),)),
            dma((2,)),
            dma((4,)),
            dma((4, rows // CHUNK)),
            dma((20,)),
            dma((20,)),
        ],
        compiler_params=pltpu.CompilerParams(
            collective_id=0, has_side_effects=True, vmem_limit_bytes=60 * 2**20
        ),
    )(*operands)
    return (out.reshape(user_count, row_count, features), filter_grad)


def solution(mesh):
    placed = (
        P("batch", "seq", None),
        P("batch", "seq", None),
        P(None, "seq", "batch", None),
        P(),
        P(),
        P(),
        P(),
        P(),
    )
    return jax.shard_map(
        local,
        mesh=mesh,
        in_specs=placed,
        out_specs=(P("batch", "seq", None), P(None, "seq", "batch", None)),
        check_vma=False,
    )
```

```python
import functools
import math

import jax
import jax.numpy as jnp
import ml_dtypes
import numpy as np
from jax import lax
from jax.experimental import pallas as pl
from jax.experimental.pallas import tpu as pltpu
from jax.sharding import PartitionSpec as P

F1 = 128
F2 = 128
LINES = 64
CHUNK = 2
ZS, XS, CORES = 4, 4, 2

epsilon = 1e-05
inv_root_two = 1.0 / math.sqrt(2.0)
inv_root_tau = 1.0 / math.sqrt(2.0 * math.pi)
inv_length = 1.0 / (F1 * F2)


def columns(table):
    blocks = np.split(table, table.shape[1] // 128, axis=1)
    return np.stack(blocks).astype(ml_dtypes.bfloat16)


def whole(table):
    return jnp.concatenate([table[k] for k in range(table.shape[0])], axis=1)


def host_tables():
    index = np.arange(F1)
    angle = 2.0 * np.pi * (index[:, None] * index[None, :] % F1) / F1
    cos, sin = np.cos(angle), np.sin(angle)
    outer_fwd = np.concatenate([cos[:LINES], -sin[:LINES]], axis=0)
    outer_inv = np.concatenate([cos[:LINES], -sin[:LINES]], axis=0).T
    inner_fwd = np.block([[cos, -sin], [sin, cos]])
    inner_inv = np.block([[cos, sin], [-sin, cos]])
    lines = np.arange(LINES + 1)
    phase = 2.0 * np.pi * (lines[:, None] * index[None, :]) / (F1 * F2)
    narrow = [columns(t) for t in (outer_fwd, outer_inv, inner_fwd, inner_inv)]
    twiddles = np.stack([np.cos(phase), np.sin(phase)]).astype(np.float32)
    return (*narrow, twiddles[:, :LINES], twiddles[:, LINES:], *permutations())


def permutations():
    spread = np.zeros((2, 2 * F2, 4 * F2), np.float32)
    collect = np.zeros((2 * F2, 2 * F2), np.float32)
    for part in range(2):
        for q in range(F2):
            for h in range(2):
                spread[h, part * F2 + q, (q // 4) * 16 + h * 8 + part * 4 + q % 4] = 1.0
            block = q // 4
            place = (block % CORES) * (F2 // 4 // CORES) + block // CORES
            collect[place * 8 + part * 4 + q % 4, part * F2 + q] = 1.0
    return columns(spread.reshape(4 * F2, 4 * F2)), columns(collect)


def dot(a, b):
    return jnp.dot(a, b, preferred_element_type=jnp.float32)


def dot_nt(a, b):
    return lax.dot_general(a, b, (((1,), (1,)), ((), ())), preferred_element_type=jnp.float32)


def mirror_rows(x):
    axis = x.ndim - 2
    size = x.shape[axis]
    row = lax.broadcasted_iota(jnp.int32, x.shape, axis)
    for step in (1, 2):
        up, down = pltpu.roll(x, step, axis), pltpu.roll(x, size - step, axis)
        x = jnp.where((row & step) != 0, up, down)
    return jnp.where((row & 4) != 0, -x, x)


def block_transpose(tiles):
    lane = lax.broadcasted_iota(jnp.int32, tiles[0].shape, 1) // 16
    result = []
    for to in range(8):
        total = tiles[to]
        for block in range(8):
            if block != to:
                moved = pltpu.roll(tiles[block], 16 * ((block - to) % 8), 1)
                total = jnp.where(lane == block, moved, total)
        result.append(total)
    return result


def mean(x):
    return jnp.mean(x, axis=-1, keepdims=True)


def local_rows(mixed, history, cot, gain_first, bias_first, w_in, w_out, gain_second):
    summed = mixed + history.astype(jnp.float32)
    center_one = summed - mean(summed)
    inv_one = lax.rsqrt(mean(center_one * center_one) + epsilon)
    norm_one = center_one * inv_one
    hidden = (norm_one * gain_first + bias_first).astype(jnp.bfloat16)
    preact = dot(hidden, w_in)
    cumul = 0.5 * (1.0 + lax.erf(preact * inv_root_two))
    activation = (preact * cumul).astype(jnp.bfloat16)
    output_sum = dot(activation, w_out) + hidden.astype(jnp.float32)
    center_two = output_sum - mean(output_sum)
    inv_two = lax.rsqrt(mean(center_two * center_two) + epsilon)
    norm_two = center_two * inv_two
    grad_norm = cot.astype(jnp.float32) * gain_second
    grad_sum = inv_two * (grad_norm - mean(grad_norm) - norm_two * mean(grad_norm * norm_two))
    grad_act = dot_nt(grad_sum.astype(jnp.bfloat16), w_out)
    density = jnp.exp(-0.5 * preact * preact) * inv_root_tau
    grad_pre = (grad_act * (cumul + preact * density)).astype(jnp.bfloat16)
    grad_hidden = dot_nt(grad_pre, w_in) + grad_sum
    grad_scaled = grad_hidden * gain_first
    return inv_one * (grad_scaled - mean(grad_scaled) - norm_one * mean(grad_scaled * norm_one))


def kernel(
    seq,
    batch,
    history_hbm,
    cotangent_hbm,
    filter_weight_hbm,
    gain_first_hbm,
    bias_first_hbm,
    w_in_hbm,
    w_out_hbm,
    gain_second_hbm,
    outer_fwd_hbm,
    outer_inv_hbm,
    inner_fwd_hbm,
    inner_inv_hbm,
    twiddle_hbm,
    twiddle_mid_hbm,
    spread_hbm,
    collect_hbm,
    out_hbm,
    filter_grad_hbm,
    history,
    cotangent,
    filter_weight,
    gain_first,
    bias_first,
    w_in,
    w_out,
    gain_second,
    outer_fwd,
    outer_inv,
    inner_fwd,
    inner_inv,
    twiddle,
    twiddle_mid,
    spread,
    collect,
    out,
    filter_grad,
    send_in,
    send_out,
    recv_in,
    recv_out,
    spec,
    spec_mid,
    back_spec,
    back_mid,
    filt,
    filt_mid,
    field,
    grad_field,
    grad_rows,
    stage,
    scatter_send,
    scatter_recv,
    gathered,
    core_send,
    core_recv,
    x_send,
    x_recv,
    z_send,
    z_recv,
    return_send,
    return_recv,
    load_sem,
    store_sem,
    send_sem,
    recv_sem,
    side_send_sem,
    side_recv_sem,
):
    me = lax.axis_index("seq")
    mine = lax.axis_index("batch")
    rows = F1 // seq
    feats = history.shape[1] // seq
    chunks = rows // CHUNK
    core = lax.rem(mine, CORES)
    along_x = lax.rem(mine // CORES, XS)
    along_z = mine // (CORES * XS)
    opposite = batch - 1 - mine
    low = me < seq // 2

    def batch_index(z, x, c):
        return (z * XS + x) * CORES + c

    x_peers = [lax.rem(along_x + k, XS) for k in range(1, XS)]
    z_peers = [lax.rem(along_z + k, ZS) for k in range(1, ZS)]
    to_x = [{"batch": batch_index(along_z, x, core)} for x in x_peers]
    to_z = [{"batch": batch_index(z, along_x, core)} for z in z_peers]
    to_core = {"batch": batch_index(along_z, along_x, 1 - core)}

    loads = {}
    for name, source, target in (
        ("filter", filter_weight_hbm, filter_weight),
        ("history", history_hbm, history),
        ("outer_fwd", outer_fwd_hbm, outer_fwd),
        ("twiddle", twiddle_hbm, twiddle),
        ("twiddle_mid", twiddle_mid_hbm, twiddle_mid),
        ("inner_fwd", inner_fwd_hbm, inner_fwd),
        ("spread", spread_hbm, spread),
        ("inner_inv", inner_inv_hbm, inner_inv),
        ("outer_inv", outer_inv_hbm, outer_inv),
        ("gain_first", gain_first_hbm, gain_first),
        ("bias_first", bias_first_hbm, bias_first),
        ("w_in", w_in_hbm, w_in),
        ("w_out", w_out_hbm, w_out),
        ("gain_second", gain_second_hbm, gain_second),
        ("cotangent", cotangent_hbm, cotangent),
        ("collect", collect_hbm, collect),
    ):
        loads[name] = pltpu.make_async_copy(source, target, load_sem.at[len(loads)])
        loads[name].start()

    barrier = pltpu.get_barrier_semaphore()

    def greet(peer):
        pl.semaphore_signal(
            barrier, inc=1, device_id=peer, device_id_type=pl.DeviceIdType.MESH
        )

    def greet_seq(k, _):
        greet({"seq": lax.rem(me + k, seq)})
        return 0

    def greet_opposite(k, _):
        greet({"seq": k, "batch": opposite})
        return 0

    lax.fori_loop(0, seq, greet_opposite, 0)
    for peer in (*to_z, *to_x, to_core):
        greet(peer)
    lax.fori_loop(1, seq, greet_seq, 0)

    def side_copy(src, dst, way, peer):
        pltpu.make_async_remote_copy(
            src_ref=src,
            dst_ref=dst,
            send_sem=side_send_sem.at[way],
            recv_sem=side_recv_sem.at[way],
            device_id=peer,
            device_id_type=pl.DeviceIdType.MESH,
        ).start()

    def wait_bytes(ref, sem):
        pltpu.make_async_copy(ref, ref, sem).wait()

    def wait_all_seq(ref, sem):
        @pl.when(low)
        def _():
            wait_bytes(ref.at[pl.ds(0, seq - 1)], sem)

        @pl.when(jnp.logical_not(low))
        def _():
            wait_bytes(ref, sem)

    sizes = {
        1: gathered.at[0, 0, 0],
        2: gathered.at[0, 0, 0],
        3: gathered.at[0, 0, 0],
        4: gathered.at[:, pl.ds(0, XS - 1), 0],
        9: gathered.at[:, :, 0],
        10: core_recv,
        11: x_recv.at[0],
        12: x_recv.at[0],
        13: x_recv.at[0],
        14: x_recv.at[0],
        15: z_recv,
    }

    def arrived(*ways):
        for way in ways:
            wait_bytes(sizes[way], side_recv_sem.at[way])

    def scatter_prepare():
        for part in range(2):
            for tile in range(2):
                for line in range(8):
                    stage[line, 8 * tile + 4 * part : 8 * tile + 4 * part + 4, :] = filter_weight[
                        part, line, :, 128 * tile : 128 * (tile + 1)
                    ].astype(jnp.float32)
        tiles = []
        for line in range(8):
            tile = stage[jnp.where(low, line, 7 - line)]
            tiles.append(jnp.where(low, tile, mirror_rows(tile)))
        for to, tile in enumerate(block_transpose(tiles)):
            scatter_send[to] = tile[:8]
            scatter_send[8 + to] = tile[8:]

    def scatter_start():
        target = jnp.where(low, mine, opposite)

        def one(k, _):
            peer = lax.rem(me + k, seq)
            side_copy(
                scatter_send.at[peer], scatter_recv.at[me], 0, {"seq": peer, "batch": target}
            )
            return 0

        @pl.when(low)
        def _():
            scatter_recv[me] = scatter_send[me]

        lax.fori_loop(jnp.where(low, 1, 0), seq, one, 0)

    def gather_start():
        wait_all_seq(scatter_recv, side_recv_sem.at[0])
        lane = lax.broadcasted_iota(jnp.int32, (8, 128), 1)
        zeros = jnp.zeros((8, 128), jnp.float32)
        moved = [pltpu.roll(scatter_recv[seq - 1 - t], 16, 1) for t in range(8)]
        tiles = []
        for t in range(9):
            before = moved[t - 1] if t > 0 else zeros
            after = moved[t] if t < 8 else zeros
            tile = jnp.where(lane < 16, before, after)
            tiles.append(tile + scatter_recv[t] if t < 8 else tile)
        for t in range(5):
            upper = tiles[t] if t < 4 else tiles[8]
            lower = tiles[4 + t] if t < 4 else zeros
            gathered[along_z, along_x, core, t] = jnp.concatenate([upper, lower], axis=0).astype(
                jnp.bfloat16
            )
        own = gathered.at[along_z, along_x, core]
        for k, peer in enumerate(to_z):
            side_copy(own, own, 1 + k, peer)
        gather_forward(along_z)

    def gather_forward(z):
        for peer in to_x:
            block = gathered.at[z, along_x, core]
            side_copy(block, block, 4, peer)

    def gather_z(k):
        arrived(1 + k)
        gather_forward(lax.rem(along_z + ZS - 1 - k, ZS))

    def gather_core():
        arrived(4)
        block = gathered.at[:, :, core]
        side_copy(block, block, 9, to_core)

    def gather_finish():
        arrived(9)
        loads["spread"].wait()
        parts = [gathered[:, :, :, t].reshape(batch * 16, 128) for t in range(5)]
        block = jnp.concatenate(parts[:4], axis=1)
        for h in range(2):
            table = jnp.concatenate(
                [spread[k, 2 * F2 * h : 2 * F2 * (h + 1)] for k in range(4)], axis=1
            )
            result = dot(table, block).astype(jnp.bfloat16).T.astype(jnp.float32)
            filt[512 * h : 512 * (h + 1), :] = result[:, :F2]
            filt[1024 + 512 * h : 1024 + 512 * (h + 1), :] = result[:, F2:]
        table = jnp.concatenate([spread[k, : 2 * F2] for k in range(4)], axis=1)
        filt_mid[...] = dot(table, parts[4]).astype(jnp.bfloat16).T[:feats]

    def filter_lines(base):
        blocks = []
        for i in range(4):
            real = filt[pl.ds(base + i, LINES, stride=feats), :]
            imag = filt[pl.ds(1024 + base + i, LINES, stride=feats), :]
            blocks.append(jnp.concatenate([real, imag], axis=1))
        return jnp.concatenate(blocks, axis=0)

    def reduce_start():
        for d in range(feats):
            where = pl.ds(d * LINES, LINES)
            term = times_conj(back_spec[where, :], spec[where, :]) * inv_length
            grad_field[pl.ds(d, LINES, stride=feats), :] = term[:, :F2]
            grad_field[pl.ds(1024 + d, LINES, stride=feats), :] = term[:, F2:]
        loads["collect"].wait()
        operands = []
        for h in range(2):
            real = grad_field[512 * h : 512 * (h + 1), :]
            imag = grad_field[1024 + 512 * h : 1024 + 512 * (h + 1), :]
            operands.append(jnp.concatenate([real, imag], axis=1).astype(jnp.bfloat16))
        mid = jnp.concatenate(
            [
                times_conj(back_mid[...], spec_mid[...]) * inv_length,
                jnp.zeros((128 - feats, 2 * F2), jnp.float32),
            ],
            axis=0,
        ).astype(jnp.bfloat16)
        for c in (1 - core, core):
            where = pl.ds(pl.multiple_of(c * F2, F2), F2)
            table = jnp.concatenate([collect[0, where], collect[1, where]], axis=1)
            parts = [dot_nt(table, x).reshape(batch // CORES, 8, 512) for x in operands]
            last = dot_nt(table, mid).reshape(batch // CORES, 8, 128)
            both = jnp.concatenate(parts, axis=1).astype(jnp.bfloat16)
            both = both.reshape(ZS, XS, 16, 512)
            for t in range(4):
                core_send[c, :, :, t] = both[..., 128 * t : 128 * (t + 1)]
            last = jnp.concatenate([last, jnp.zeros_like(last)], axis=1).astype(jnp.bfloat16)
            core_send[c, :, :, 4] = last.reshape(ZS, XS, 16, 128)
            if c is not core:
                side_copy(core_send.at[c], core_recv, 10, to_core)

    def add(a, b):
        return (a.astype(jnp.float32) + b.astype(jnp.float32)).astype(jnp.bfloat16)

    z_order = [lax.rem(along_z + k, ZS) for k in (2, 1, 3, 0)]

    def reduce_x():
        arrived(10)
        for place, z in enumerate(z_order):
            for x in range(XS):
                x_send[z, x] = add(core_send[core, z, x], core_recv[z, x])
            for k, peer in enumerate(to_x):
                side_copy(x_send.at[z, x_peers[k]], x_recv.at[z, k], 11 + place, peer)

    def reduce_z():
        for place, z in enumerate(z_order):
            arrived(11 + place)
            total = x_send[z, along_x].astype(jnp.float32)
            for k in range(XS - 1):
                total = total + x_recv[z, k].astype(jnp.float32)
            z_send[z] = total.astype(jnp.bfloat16)
            if place < ZS - 1:
                side_copy(
                    z_send.at[z],
                    z_recv.at[place],
                    15,
                    {"batch": batch_index(z, along_x, core)},
                )

    def return_grad():
        arrived(15)
        total = z_send[along_z].astype(jnp.float32)
        for k in range(ZS - 1):
            total = total + z_recv[k].astype(jnp.float32)
        tiles = [total[t, :8] for t in range(4)] + [total[t, 8:] for t in range(4)]
        tiles.append(total[4, :8])
        lane = lax.broadcasted_iota(jnp.int32, (8, 128), 1)
        moved = [pltpu.roll(t, 112, 1) for t in tiles]
        for t in range(8):
            return_send[t] = tiles[t]
            return_send[seq - 1 - t] = jnp.where(lane < 112, moved[t], moved[t + 1])

        def send(peer, target):
            side_copy(
                return_send.at[peer], return_recv.at[me], 19, {"seq": peer, "batch": target}
            )

        half = seq // 2

        def far(k, _):
            send(half + lax.rem(me + k, half), opposite)
            return 0

        def near(k, _):
            send(lax.rem(me + k, half), mine)
            return 0

        lax.fori_loop(0, half, far, 0)

        @pl.when(low)
        def _():
            return_recv[me] = return_send[me]

        lax.fori_loop(jnp.where(low, 1, 0), half, near, 0)

    def return_finish():
        wait_all_seq(return_recv, side_recv_sem.at[19])
        tiles = [
            jnp.concatenate([return_recv[t], return_recv[8 + t]], axis=0) for t in range(8)
        ]
        for line, tile in enumerate(block_transpose(tiles)):
            stage[jnp.where(low, line, 7 - line)] = jnp.where(low, tile, mirror_rows(tile))
        for part in range(2):
            for tile in range(2):
                for line in range(8):
                    filter_grad[part, line, :, 128 * tile : 128 * (tile + 1)] = stage[
                        line, 8 * tile + 4 * part : 8 * tile + 4 * part + 4, :
                    ]

    def exchange(src, dst, way, chunk):
        def one(k, _):
            peer = lax.rem(me + k, seq)
            pltpu.make_async_remote_copy(
                src_ref=src(peer),
                dst_ref=dst,
                send_sem=send_sem.at[way],
                recv_sem=recv_sem.at[way, chunk],
                device_id={"seq": peer},
                device_id_type=pl.DeviceIdType.MESH,
            ).start()
            return 0

        lax.fori_loop(1, seq, one, 0)

    def turn(x, way, chunk):
        for j in range(chunk * CHUNK, (chunk + 1) * CHUNK):
            send_in[way, j] = x(j).T.reshape(seq, feats, F2)

    def send_positions(way, chunk):
        part = pl.ds(chunk * CHUNK, CHUNK)
        recv_in[way, me, part] = send_in[way, part, me]
        exchange(
            lambda peer: send_in.at[way, part, peer], recv_in.at[way, me, part], 2 * way, chunk
        )

    def send_features(way, chunk):
        part = pl.ds(chunk * CHUNK, CHUNK)
        recv_out[way, part, me] = send_out[way, me, part]
        exchange(
            lambda peer: send_out.at[way, peer, part], recv_out.at[way, part, me], 2 * way + 1, chunk
        )

    def wait_chunk(way, chunk):
        wait_bytes(
            send_in.at[0, pl.ds(0, CHUNK), pl.ds(0, seq - 1)], recv_sem.at[way, chunk]
        )

    def absorb(way, chunk):
        mid = 0.0
        for source in range(seq):
            block = recv_in[way, source, chunk * CHUNK : (chunk + 1) * CHUNK].astype(jnp.float32)
            first = (source * rows + chunk * CHUNK) * feats
            field[first : first + CHUNK * feats, :] = block.reshape(CHUNK * feats, F2)
            for j in range(CHUNK):
                mid = mid + block[j] if j % 2 == 0 else mid - block[j]
        return mid

    def forward(mid, spectrum, spectrum_mid):
        cos, sin = twiddle[0], twiddle[1]

        def step(group, _):
            base = group * 4
            halves = []
            for sub in range(2):
                pair = [
                    field[pl.ds(base + 2 * sub + i, F1, stride=feats), :] for i in range(2)
                ]
                two = jnp.concatenate(pair, axis=1).astype(jnp.bfloat16)
                both = dot(whole(outer_fwd), two)
                for i in range(2):
                    real = both[:LINES, i * F2 : (i + 1) * F2]
                    imag = both[LINES:, i * F2 : (i + 1) * F2]
                    halves.append(
                        jnp.concatenate(
                            [real * cos + imag * sin, imag * cos - real * sin], axis=1
                        ).astype(jnp.bfloat16)
                    )
            where = pl.ds(pl.multiple_of(base * LINES, 4 * LINES), 4 * LINES)
            spectrum[where, :] = dot(jnp.concatenate(halves, axis=0), whole(inner_fwd)).astype(
                jnp.bfloat16
            )
            return 0

        lax.fori_loop(0, feats // 4, step, 0, unroll=True)
        cos_mid, sin_mid = twiddle_mid[0], twiddle_mid[1]
        half = jnp.concatenate([mid * cos_mid, -mid * sin_mid], axis=1).astype(jnp.bfloat16)
        spectrum_mid[...] = dot(half, whole(inner_fwd)).astype(jnp.bfloat16)

    def backward(way, product, product_mid):
        cos, sin = twiddle[0], twiddle[1]

        def step(group, _):
            base = group * 4
            where = pl.ds(pl.multiple_of(base * LINES, 4 * LINES), 4 * LINES)
            half = dot(product(where, filter_lines(base)), whole(inner_inv))
            for sub in range(2):
                columns = []
                for i in range(2):
                    part = half[(2 * sub + i) * LINES : (2 * sub + i + 1) * LINES]
                    real, imag = part[:, :F2], part[:, F2:]
                    columns.append(
                        jnp.concatenate(
                            [real * cos - imag * sin, imag * cos + real * sin], axis=0
                        ).astype(jnp.bfloat16)
                    )
                result = dot(whole(outer_inv), jnp.concatenate(columns, axis=1)) * inv_length
                for i in range(2):
                    field[pl.ds(base + 2 * sub + i, F1, stride=feats), :] = result[
                        :, i * F2 : (i + 1) * F2
                    ]
            return 0

        lax.fori_loop(0, feats // 4, step, 0, unroll=True)
        half = dot(product_mid(), whole(inner_inv))
        last = (half[:, :F2] * twiddle_mid[0] - half[:, F2:] * twiddle_mid[1]).astype(jnp.bfloat16)
        last = last.astype(jnp.float32) * inv_length
        both = field[: F1 * feats, :].reshape(F1 // 2, 2, feats, F2)
        sign = jnp.where(lax.broadcasted_iota(jnp.int32, both.shape, 1) == 0, 1.0, -1.0)
        both = both + sign * last[None, None]
        send_out[way] = both.astype(jnp.bfloat16).reshape(seq, rows, feats, F2)

    def split(z):
        return z[:, :F2].astype(jnp.float32), z[:, F2:].astype(jnp.float32)

    def times(z, f):
        zr, zi = split(z)
        fr, fi = split(f)
        return jnp.concatenate([zr * fr - zi * fi, zr * fi + zi * fr], axis=1).astype(jnp.bfloat16)

    def times_conj(z, f):
        zr, zi = split(z)
        fr, fi = split(f)
        return jnp.concatenate([fr * zr + fi * zi, fr * zi - fi * zr], axis=1)

    loads["filter"].wait()
    scatter_prepare()
    loads["history"].wait()
    for chunk in range(chunks):
        turn(lambda j: history[pl.ds(j * F2, F2), :], 0, chunk)
    pl.semaphore_wait(barrier, 2 * seq - 1 + ZS - 1 + XS - 1 + 1)
    scatter_start()
    for chunk in range(chunks // 2):
        send_positions(0, chunk)
    gather_start()
    gather_z(0)
    gather_z(2)
    for chunk in range(chunks // 2, chunks):
        send_positions(0, chunk)
    gather_z(1)
    for name in ("outer_fwd", "twiddle", "twiddle_mid", "inner_fwd", "inner_inv", "outer_inv"):
        loads[name].wait()
    mid = 0.0
    for chunk in range(chunks):
        wait_chunk(0, chunk)
        mid = mid + absorb(0, chunk)
    forward(mid, spec, spec_mid)
    gather_core()
    gather_finish()
    backward(
        0,
        lambda where, lines: times(spec[where, :], lines),
        lambda: times(spec_mid[...], filt_mid[...]),
    )
    for chunk in range(chunks):
        send_features(0, chunk)

    for name in ("gain_first", "bias_first", "w_in", "w_out", "gain_second", "cotangent"):
        loads[name].wait()
    for chunk in range(chunks):
        wait_chunk(1, chunk)
        for j in range(chunk * CHUNK, (chunk + 1) * CHUNK):
            mixed = recv_out[0, j].reshape(seq * feats, F2).T.astype(jnp.float32)
            part = pl.ds(j * F2, F2)
            grad_rows[part, :] = local_rows(
                mixed,
                history[part, :],
                cotangent[part, :],
                gain_first[...],
                bias_first[...],
                w_in[...],
                w_out[...],
                gain_second[...],
            )
        turn(lambda j: grad_rows[pl.ds(j * F2, F2), :].astype(jnp.bfloat16), 1, chunk)
        send_positions(1, chunk)

    mid = 0.0
    for chunk in range(chunks):
        wait_chunk(2, chunk)
        mid = mid + absorb(1, chunk)
    forward(mid, back_spec, back_mid)
    reduce_start()
    reduce_x()
    backward(
        1,
        lambda where, lines: times_conj(back_spec[where, :], lines).astype(jnp.bfloat16),
        lambda: times_conj(back_mid[...], filt_mid[...]).astype(jnp.bfloat16),
    )
    send_features(1, 0)
    reduce_z()
    send_features(1, 1)
    return_grad()
    for chunk in range(2, chunks):
        send_features(1, chunk)
    for chunk in range(chunks):
        wait_chunk(3, chunk)
        for j in range(chunk * CHUNK, (chunk + 1) * CHUNK):
            back = recv_out[1, j].reshape(seq * feats, F2).T.astype(jnp.float32)
            part = pl.ds(j * F2, F2)
            out[part, :] = (grad_rows[part, :] + back).astype(jnp.bfloat16)
        part = pl.ds(chunk * CHUNK * F2, CHUNK * F2)
        pltpu.make_async_copy(out.at[part], out_hbm.at[part], store_sem.at[0]).start()
    return_finish()
    store = pltpu.make_async_copy(filter_grad, filter_grad_hbm, store_sem.at[1])
    store.start()

    wait_all_seq(scatter_send, side_send_sem.at[0])
    for way, ref in sizes.items():
        wait_bytes(ref, side_send_sem.at[way])
    wait_all_seq(return_send, side_send_sem.at[19])
    sent = send_in.at[0, :, pl.ds(0, seq - 1)]
    for way in range(4):
        wait_bytes(sent, send_sem.at[way])
    pltpu.make_async_copy(out, out_hbm, store_sem.at[0]).wait()
    store.wait()


def local(history, cotangent, filter_weight, gain_first, bias_first, w_in, w_out, gain_second):
    user_count, row_count, features = history.shape
    seq = lax.axis_size("seq")
    feats = features // seq
    rows = F1 // seq
    bf16, f32 = jnp.bfloat16, jnp.float32
    tables = [jnp.asarray(t) for t in host_tables()]

    batch = lax.axis_size("batch")
    dma = pltpu.SemaphoreType.DMA
    operands = (
        history.reshape(row_count, features),
        cotangent.reshape(row_count, features),
        filter_weight,
        gain_first.reshape(1, features),
        bias_first.reshape(1, features),
        w_in,
        w_out,
        gain_second.reshape(1, features),
        *tables,
    )
    out, filter_grad = pl.pallas_call(
        functools.partial(kernel, seq, batch),
        out_shape=(
            jax.ShapeDtypeStruct((row_count, features), bf16),
            jax.ShapeDtypeStruct(filter_weight.shape, f32),
        ),
        in_specs=[pl.BlockSpec(memory_space=pltpu.HBM)] * len(operands),
        out_specs=(pl.BlockSpec(memory_space=pltpu.HBM),) * 2,
        scratch_shapes=[
            *[pltpu.VMEM(x.shape, x.dtype) for x in operands],
            pltpu.VMEM((row_count, features), bf16),
            pltpu.VMEM(filter_weight.shape, f32),
            pltpu.VMEM((2, rows, seq, feats, F2), bf16),
            pltpu.VMEM((2, seq, rows, feats, F2), bf16),
            pltpu.VMEM((2, seq, rows, feats, F2), bf16),
            pltpu.VMEM((2, rows, seq, feats, F2), bf16),
            pltpu.VMEM((feats * LINES, 2 * F2), bf16),
            pltpu.VMEM((feats, 2 * F2), bf16),
            pltpu.VMEM((feats * LINES, 2 * F2), bf16),
            pltpu.VMEM((feats, 2 * F2), bf16),
            pltpu.VMEM((2 * LINES * feats + feats, F2), f32),
            pltpu.VMEM((feats, 2 * F2), bf16),
            pltpu.VMEM((F1 * feats + feats, F2), f32),
            pltpu.VMEM((2 * LINES * feats + feats, F2), f32),
            pltpu.VMEM((row_count, features), f32),
            pltpu.VMEM((8, 16, 128), f32),
            pltpu.VMEM((seq, 8, 128), f32),
            pltpu.VMEM((seq, 8, 128), f32),
            pltpu.VMEM((ZS, XS, CORES, 5, 16, 128), bf16),
            pltpu.VMEM((CORES, ZS, XS, 5, 16, 128), bf16),
            pltpu.VMEM((ZS, XS, 5, 16, 128), bf16),
            pltpu.VMEM((ZS, XS, 5, 16, 128), bf16),
            pltpu.VMEM((ZS, XS - 1, 5, 16, 128), bf16),
            pltpu.VMEM((ZS, 5, 16, 128), bf16),
            pltpu.VMEM((ZS - 1, 5, 16, 128), bf16),
            pltpu.VMEM((seq, 8, 128), f32),
            pltpu.VMEM((seq, 8, 128), f32),
            dma((len(operands),)),
            dma((2,)),
            dma((4,)),
            dma((4, rows // CHUNK)),
            dma((20,)),
            dma((20,)),
        ],
        compiler_params=pltpu.CompilerParams(
            collective_id=0, has_side_effects=True, vmem_limit_bytes=60 * 2**20
        ),
    )(*operands)
    return (out.reshape(user_count, row_count, features), filter_grad)


def solution(mesh):
    placed = (
        P("batch", "seq", None),
        P("batch", "seq", None),
        P(None, "seq", "batch", None),
        P(),
        P(),
        P(),
        P(),
        P(),
    )
    return jax.shard_map(
        local,
        mesh=mesh,
        in_specs=placed,
        out_specs=(P("batch", "seq", None), P(None, "seq", "batch", None)),
        check_vma=False,
    )
```
